256 devices in a mesh: group: 16 (over y, x), index: 8 (over z), tensor: 2 (over core).
Axes of the slice: x: 4, y: 4, z: 8, core: 2. Of those that a mesh axis runs over, the one named last changes fastest.
Arguments:
- queries: bfloat16 [16384, 4096], P(('group', 'index'), 'tensor'), may hold values from -4 to 4
- passages: bfloat16 [65536, 4096], P(('group', 'index'), 'tensor'), may hold values from -4 to 4
- positive_slot: int32 [16384], P(('group', 'index')), may hold values from 0 to 511
- hard_offset: int32 [16384, 7], P(('group', 'index')), may hold values from 0 to 6, as said below
- hard_slot: int32 [16384, 7], P(('group', 'index')), may hold values from 0 to 511
Outputs:
- loss: float32 [], replicated
- query_grad: bfloat16 [16384, 4096], P(('group', 'index'), 'tensor')
- passage_grad: bfloat16 [65536, 4096], P(('group', 'index'), 'tensor')
The draws below stay inside these ranges and needn't reach their ends.
Inputs may be any that keep to these rules, and one draw needn't show every extreme that they name: `hard_offset`: within one block's rows, one offset is named exactly 192 times and the other offsets share the remaining 128 * 7 - 192 entries evenly, their counts differing by at most one; which offset is the busy one varies by block.
All inputs are finite; a program needn't handle non-finite values.
Results may differ from the reference program's by a relative error of at most 0.008.
Values may be sent and summed in bfloat16 or wider, within the bound.
A program may use at most 128 MiB of HBM per device.

```python
import math
import jax
import jax.numpy as jnp
from jax import lax

D = 4096
NEG = 7
Q_DEV = 128
GROUP_SIZE = 16
OWNERS = 8
P_DEV = 512
CAP = 192
QUERIES = 16384
PASSAGES = 65536


topic_count = 32


def route_table(key):
    base_key = jax.random.fold_in(key, 101)
    blocks = QUERIES // Q_DEV
    entries = Q_DEV * NEG
    others = OWNERS - 2
    busy = jax.random.randint(jax.random.fold_in(base_key, 1), (blocks, 1), 0, OWNERS - 1)
    rotate = jax.random.randint(jax.random.fold_in(base_key, 2), (blocks, 1), 0, others)
    shuffle_keys = jax.random.split(jax.random.fold_in(base_key, 3), blocks)
    orders = jax.vmap(lambda one_key: jax.random.permutation(one_key, entries))(shuffle_keys)
    places = jnp.arange(entries, dtype=jnp.int32)[None, :]
    spread = (busy + 1 + (places - CAP + rotate) % others) % (OWNERS - 1)
    values = jnp.where(places < CAP, busy, spread).astype(jnp.int32)
    table = jnp.zeros((blocks, entries), jnp.int32).at[jnp.arange(blocks)[:, None], orders].set(values)
    return table.reshape(QUERIES, NEG).astype(jnp.int32)


def slot_table(key):
    return jax.random.randint(jax.random.fold_in(key, 202), (QUERIES, NEG), 0, P_DEV).astype(jnp.int32)


def positive_table(key):
    return jax.random.randint(jax.random.fold_in(key, 303), (QUERIES,), 0, P_DEV).astype(jnp.int32)


def topic_tables(key):
    topics = jax.random.randint(jax.random.fold_in(key, 404), (PASSAGES,), 0, topic_count)
    centres = jax.random.normal(jax.random.fold_in(key, 405), (topic_count, D), jnp.float32)
    return (topics, centres)


def raw_rows(key, topics, centres, row_ids):
    noise_key = jax.random.fold_in(key, 406)
    noise = jax.vmap(lambda row_id: jax.random.normal(jax.random.fold_in(noise_key, row_id), (D,), jnp.float32))(row_ids)
    return noise + centres[topics[row_ids]]


def draw_positive_slot(key, part):
    return positive_table(key)


def draw_hard_offset(key, part):
    return route_table(key)


def draw_hard_slot(key, part):
    return slot_table(key)


def draw_passages(key, part):
    topics, centres = topic_tables(key)
    blocks = PASSAGES // P_DEV
    row_ids = jnp.arange(PASSAGES, dtype=jnp.int32).reshape(blocks, P_DEV)
    made = lax.map(lambda ids: raw_rows(key, topics, centres, ids), row_ids).reshape(PASSAGES, D)
    factor = 0.7 / math.sqrt(D)
    return jnp.clip(made * factor, -4.0, 4.0).astype(jnp.bfloat16)


def draw_queries(key, part):
    topics, centres = topic_tables(key)
    offsets = route_table(key)
    slots = slot_table(key)
    positives = positive_table(key)
    own_key = jax.random.fold_in(key, 9)
    blocks = QUERIES // Q_DEV
    block_ids = jnp.arange(QUERIES, dtype=jnp.int32) // Q_DEV
    group_pos = block_ids // OWNERS
    index_pos = block_ids % OWNERS
    owner_ids = (index_pos[:, None] + 1 + offsets) % OWNERS
    hard_ids = ((group_pos[:, None] * OWNERS + owner_ids) * P_DEV + slots).astype(jnp.int32)
    positive_ids = (block_ids * P_DEV + positives).astype(jnp.int32)
    pull = jax.random.uniform(jax.random.fold_in(own_key, 1), (QUERIES, 1), jnp.float32, 0.1, 0.18)
    hard_pull = jax.random.uniform(jax.random.fold_in(own_key, 2), (QUERIES, NEG), jnp.float32, 0.0, 0.18)
    noise_key = jax.random.fold_in(own_key, 3)

    def one_block(inputs):
        block_now, positive_now, hard_now, pull_now, hard_pull_now = inputs
        positive_raw = raw_rows(key, topics, centres, positive_now)
        hard_raw = raw_rows(key, topics, centres, hard_now.reshape(Q_DEV * NEG)).reshape(Q_DEV, NEG, D)
        noise = jax.random.normal(jax.random.fold_in(noise_key, block_now), (Q_DEV, D), jnp.float32)
        return noise + pull_now * positive_raw + jnp.sum(hard_pull_now[:, :, None] * hard_raw, axis=1)
    made = lax.map(one_block, (jnp.arange(blocks, dtype=jnp.int32), positive_ids.reshape(blocks, Q_DEV), hard_ids.reshape(blocks, Q_DEV, NEG), pull.reshape(blocks, Q_DEV, 1), hard_pull.reshape(blocks, Q_DEV, NEG))).reshape(QUERIES, D)
    factor = 0.9 / math.sqrt(D)
    return jnp.clip(made * factor, -4.0, 4.0).astype(jnp.bfloat16)


def setup_inputs(seed: int = 0) -> dict:
    seeds = jax.random.split(jax.random.key(seed), 6)
    queries = draw_queries(jax.random.fold_in(seeds[5], 71), 0)
    passages = draw_passages(jax.random.fold_in(seeds[5], 71), 0)
    positive_slot = draw_positive_slot(jax.random.fold_in(seeds[5], 71), 0)
    hard_offset = draw_hard_offset(jax.random.fold_in(seeds[5], 71), 0)
    hard_slot = draw_hard_slot(jax.random.fold_in(seeds[5], 71), 0)
    return dict(queries=queries, passages=passages, positive_slot=positive_slot, hard_offset=hard_offset, hard_slot=hard_slot)


epsilon = 1e-06
inverse_temp = 50.0

def normalize(values):
    widened = values.astype(jnp.float32)
    norms = jnp.sqrt(lax.optimization_barrier(jnp.sum(widened * widened, axis=1, keepdims=True)) + epsilon)
    return (widened / norms, norms)

def project_out(gradient, unit_rows, norms):
    along = lax.optimization_barrier(jnp.sum(unit_rows * gradient, axis=1, keepdims=True))
    return ((gradient - unit_rows * along) / norms).astype(jnp.bfloat16)

def reference(queries, passages, positive_slot, hard_offset, hard_slot):
    unit_query, query_norm = normalize(queries)
    query_hat = unit_query.astype(jnp.bfloat16)
    unit_passage, passage_norm = normalize(passages)
    passage_hat = unit_passage.astype(jnp.bfloat16)
    unit_passage = None
    span = GROUP_SIZE * Q_DEV
    query_blocks = query_hat.reshape(GROUP_SIZE, OWNERS, Q_DEV, D)
    positive_blocks = positive_slot.reshape(GROUP_SIZE, OWNERS, Q_DEV)
    offset_blocks = hard_offset.reshape(GROUP_SIZE, OWNERS, Q_DEV, NEG)
    slot_blocks = hard_slot.reshape(GROUP_SIZE, OWNERS, Q_DEV, NEG)
    group_ids = jnp.arange(GROUP_SIZE, dtype=jnp.int32)

    def per_index(passage_sums, index_now):
        own_queries = query_blocks[:, index_now].reshape(span, D)
        positive_rows = ((group_ids[:, None] * OWNERS + index_now) * P_DEV + positive_blocks[:, index_now]).reshape(span).astype(jnp.int32)
        owner_ids = (index_now + 1 + offset_blocks[:, index_now]) % OWNERS
        hard_ids = ((group_ids[:, None, None] * OWNERS + owner_ids) * P_DEV + slot_blocks[:, index_now]).reshape(span * NEG).astype(jnp.int32)
        batch_block = passage_hat[positive_rows]
        hard_rows = passage_hat[hard_ids].reshape(span, NEG, D)
        in_scores = inverse_temp * jnp.dot(own_queries, batch_block.T, preferred_element_type=jnp.float32)
        hard_scores = inverse_temp * jnp.einsum('qd,qjd->qj', own_queries.astype(jnp.float32), hard_rows.astype(jnp.float32))
        log_total = jnp.log(lax.optimization_barrier(jnp.sum(jnp.exp(in_scores), axis=1)) + lax.optimization_barrier(jnp.sum(jnp.exp(hard_scores), axis=1)))
        target = jnp.eye(span, dtype=jnp.float32)
        loss_sum = jnp.sum(log_total - lax.optimization_barrier(jnp.sum(in_scores * target, axis=1)))
        in_weight = (inverse_temp * (jnp.exp(in_scores - log_total[:, None]) - target)).astype(jnp.bfloat16)
        hard_weight = (inverse_temp * jnp.exp(hard_scores - log_total[:, None])).astype(jnp.bfloat16)
        query_sum = jnp.dot(in_weight, batch_block, preferred_element_type=jnp.float32)
        query_sum = query_sum + jnp.einsum('qj,qjd->qd', hard_weight.astype(jnp.float32), hard_rows.astype(jnp.float32))
        positive_grad = jnp.dot(in_weight.T, own_queries, preferred_element_type=jnp.float32)
        hard_grad = (hard_weight.astype(jnp.float32)[:, :, None] * own_queries.astype(jnp.float32)[:, None, :]).astype(jnp.bfloat16)
        passage_sums = passage_sums.at[positive_rows].add(positive_grad)
        passage_sums = passage_sums.at[hard_ids].add(hard_grad.reshape(span * NEG, D).astype(jnp.float32))
        return (passage_sums, (query_sum, loss_sum))
    passage_sums, (query_sums, loss_parts) = lax.scan(per_index, jnp.zeros((PASSAGES, D), jnp.float32), jnp.arange(OWNERS, dtype=jnp.int32))
    query_sums = query_sums.reshape(OWNERS, GROUP_SIZE, Q_DEV, D).transpose(1, 0, 2, 3).reshape(QUERIES, D)
    loss = jnp.sum(loss_parts) / QUERIES
    query_grad = project_out(query_sums, unit_query, query_norm)
    passage_grad = project_out(passage_sums, passages.astype(jnp.float32) / passage_norm, passage_norm)
    return (loss, query_grad, passage_grad)
```

```python
import jax
import jax.numpy as jnp
from jax import lax
from jax.experimental import pallas as pl
from jax.experimental.pallas import tpu as pltpu
from jax.sharding import PartitionSpec as P

epsilon = 1e-06
inverse_temp = 50.0
side = 4
lanes = 128
f32 = jnp.float32
bf16 = jnp.bfloat16


def dot_nt(a, b):
    return lax.dot_general(a, b, (((1,), (1,)), ((), ())), preferred_element_type=f32)


def dot_nn(a, b):
    return jnp.dot(a, b, preferred_element_type=f32)


def tile_lanes(values, count):
    return jnp.concatenate([values] * count, axis=1)


def fold_lanes(values):
    total = values[:, :lanes]
    for k in range(1, values.shape[1] // lanes):
        total = total + values[:, k * lanes : (k + 1) * lanes]
    return total


def to_column(row):
    return jnp.transpose(jnp.broadcast_to(row, (lanes, lanes)))


def kernel(
    slot_ref,
    offset_ref,
    hard_slot_ref,
    q_hbm,
    p_hbm,
    loss_ref,
    dq_ref,
    dp_ref,
    p_ref,
    zq,
    sh_mine,
    sh_peer,
    eh_t,
    eh,
    zs_send,
    zs_recv,
    pq,
    xq,
    yp,
    si_mine,
    si_peer,
    ein_t,
    ein_s,
    ein,
    pin,
    xs_send,
    xs_recv,
    ys_send,
    ys_recv,
    dq_acc,
    dp_acc,
    wt,
    pick,
    norm_mine,
    norm_peer,
    pcol,
    qcol,
    aux_own,
    aux_z,
    aux_x,
    pos_own,
    aux_y,
    sum_out,
    sum_z,
    sum_x,
    fac_own,
    fac_z,
    fac_x,
    own_out,
    own_y,
    loss_z,
    loss_x,
    loss_y,
    along_p_mine,
    along_p_peer,
    own_col,
    rest_col,
    ratio_col,
    along_col,
    send_sems,
    recv_sems,
    load_sems,
):
    rows, width = q_hbm.shape
    p_rows = p_ref.shape[0]
    half = rows // 2
    tiles = p_rows // rows
    group = lax.axis_index("group")
    z = lax.axis_index("index")
    t = lax.axis_index("tensor")
    y = lax.div(group, side)
    x = lax.rem(group, side)
    owners = lax.axis_size("index")

    def at_z(k):
        return (group, lax.rem(z + k + owners, owners), t)

    def at_x(k):
        return (y * side + lax.rem(x + k + side, side), z, t)

    def at_y(k):
        return (lax.rem(y + k + side, side) * side + x, z, t)

    other = (group, z, 1 - t)

    sent = []
    done = [0]

    def drain(count):
        for copy in sent[done[0] : count]:
            copy.wait_send()
        done[0] = max(done[0], count)

    def send(src, dst, target):
        k = len(sent)
        copy = pltpu.make_async_remote_copy(
            src_ref=src,
            dst_ref=dst,
            send_sem=send_sems.at[k],
            recv_sem=recv_sems.at[k],
            device_id=target,
            device_id_type=pl.DeviceIdType.MESH,
        )
        copy.start()
        sent.append(copy)
        return copy

    def rows_of(slot, part=None):
        if part is None:
            return pl.ds(slot * rows, rows)
        return pl.ds(slot * rows + part * half, half)

    far = 6

    def place(k, before, start):
        if k == 4:
            return far * rows + start
        return (2 * (k - 1) + int((start < half) != before)) * rows + start

    first_lanes = lax.broadcasted_iota(jnp.int32, (1, lanes), 1) < half

    def of_tile(tile, pair):
        if tile == far:
            return pair(far)
        block = tile - tile % 2
        low, high = (block, block + 1) if tile == block else (block + 1, block)
        return jnp.where(first_lanes, pair(low), pair(high))

    z_targets = [at_z(1), at_z(-1), at_z(2), at_z(-2), at_z(3), at_z(-3), at_z(4)]
    z_homes = [at_z(-1), at_z(1), at_z(-2), at_z(2), at_z(-3), at_z(3), at_z(4)]
    x_targets = [at_x(1), at_x(-1), at_x(2)]
    x_homes = [at_x(-1), at_x(1), at_x(2)]
    y_targets = [at_y(1), at_y(-1), at_y(2)]
    y_homes = [at_y(-1), at_y(1), at_y(2)]

    load_q = pltpu.make_async_copy(q_hbm, xq.at[rows_of(0)], load_sems.at[0])
    load_p = pltpu.make_async_copy(p_hbm, p_ref, load_sems.at[1])
    load_q.start()
    load_p.start()

    barrier = pltpu.get_barrier_semaphore()
    peers = z_targets + x_targets + y_targets + [other]
    for peer in peers:
        pl.semaphore_signal(barrier, inc=1, device_id=peer, device_id_type=pl.DeviceIdType.MESH)
    pl.semaphore_wait(barrier, len(peers))

    def z_rows(k, before, c):
        return pl.ds(place(k, before, c * half), half)

    z_right = {}
    z_left = {}
    for c in range(2):
        right_own = q_hbm.at[pl.ds(c * half, half)]
        left_own = q_hbm.at[pl.ds((1 - c) * half, half)]
        z_right[1, c] = send(right_own, zq.at[z_rows(1, True, c)], at_z(1))
        z_left[1, 1 - c] = send(left_own, zq.at[z_rows(1, False, 1 - c)], at_z(-1))
    x_right = send(q_hbm, xq.at[rows_of(1)], at_x(1))
    x_left = send(q_hbm, xq.at[rows_of(2)], at_x(-1))
    load_q.wait()
    load_p.wait()
    q_ref = xq

    slots = slot_ref[0:1, :]
    for i in range(tiles):
        ids = lax.broadcasted_iota(jnp.int32, (rows, lanes), 0) + i * rows
        chosen = jnp.where(ids == slots, 1.0, 0.0).astype(f32)
        pick[:, i * rows : (i + 1) * rows] = jnp.transpose(chosen).astype(bf16)
        wt[i * rows : (i + 1) * rows, 7 * rows : 8 * rows] = chosen.astype(bf16)
        wt[i * rows : (i + 1) * rows, 8 * rows : 9 * rows] = chosen.astype(bf16)

    wide = 512

    def pick_columns(i, _):
        columns = pl.ds(pl.multiple_of(i * wide, wide), wide)
        yp[0:rows, columns] = dot_nn(pick[...], p_ref[:, columns]).astype(bf16)
        return 0

    lax.fori_loop(0, width // wide, pick_columns, 0)
    y_right = send(yp.at[rows_of(0)], yp.at[rows_of(1)], at_y(1))
    y_left = send(yp.at[rows_of(0)], yp.at[rows_of(2)], at_y(-1))

    strip = 32

    def square_strip(source, base):
        def body(i, _):
            part = pl.ds(pl.multiple_of(i * strip, strip), strip)
            values = source[part, :].astype(f32)
            norm_mine[pl.ds(pl.multiple_of(base + i * strip, strip), strip), :] = fold_lanes(
                values * values
            )
            return 0

        return body

    lax.fori_loop(0, p_rows // strip, square_strip(p_ref, 0), 0)
    lax.fori_loop(0, rows // strip, square_strip(q_ref, p_rows), 0)
    norm_copy = send(norm_mine, norm_peer, other)
    norm_copy.wait_recv()

    def scale_of(start):
        squares = norm_mine[start : start + rows, :] + norm_peer[start : start + rows, :]
        total = jnp.sum(squares, axis=1, keepdims=True)
        return jnp.broadcast_to(1.0 / jnp.sqrt(total + epsilon), (rows, lanes))

    position_row = jnp.zeros((1, lanes), f32)
    for i in range(tiles):
        scale = scale_of(i * rows)
        pcol[i * rows : (i + 1) * rows, :] = scale
        ids = lax.broadcasted_iota(jnp.int32, (rows, lanes), 0) + i * rows
        position_row = position_row + jnp.sum(
            jnp.where(ids == slots, scale, 0.0), axis=0, keepdims=True
        )
    q_scale = scale_of(p_rows)
    qcol[...] = q_scale
    q_row = jnp.transpose(q_scale)[0:1, :]
    owner_ids = lax.rem(offset_ref[...] + (z + 1), owners)
    aux_own[0:7, :] = (owner_ids * p_rows + hard_slot_ref[...]).astype(f32)
    aux_own[7:8, :] = q_row
    pos_own[...] = jnp.broadcast_to(position_row, (8, lanes))
    aux_z_copies = [send(aux_own, aux_z.at[m], z_targets[m]) for m in range(7)]
    aux_x_copies = [send(aux_own, aux_x.at[m], x_targets[m]) for m in range(3)]
    aux_y_copies = [send(pos_own, aux_y.at[m], y_targets[m]) for m in range(3)]

    def forward_z(k, c):
        z_right[k, c].wait_recv()
        here = zq.at[z_rows(k, True, c)]
        if k < 3 or c == 0:
            z_right[k + 1, c] = send(here, zq.at[z_rows(k + 1, True, c)], at_z(1))
        z_left[k, 1 - c].wait_recv()
        here = zq.at[z_rows(k, False, 1 - c)]
        if k < 3 or c == 0:
            z_left[k + 1, 1 - c] = send(here, zq.at[z_rows(k + 1, False, 1 - c)], at_z(-1))

    line = lax.broadcasted_iota(jnp.int32, (8, lanes), 0)
    hard_copies = {}

    def hard_part(tile, count):
        def body(i, _):
            part = pl.ds(pl.multiple_of(i * 256, 256), 256)
            scores = dot_nt(p_ref[part, :], zq[tile * rows : (tile + count) * rows, :])
            for n in range(count):
                sh_mine[tile + n, part, :] = scores[:, n * lanes : (n + 1) * lanes]
            return 0

        lax.fori_loop(0, p_rows // 256, body, 0)
        here = pl.ds(tile, count)
        copy = send(sh_mine.at[here], sh_peer.at[here], other)
        for n in range(count):
            hard_copies[tile + n] = copy if n == 0 else None

    first_slot = (z * p_rows).astype(f32)
    hard_sums = {}

    def hard_exp(tile):
        if hard_copies[tile] is not None:
            hard_copies[tile].wait_recv()
        if tile == far or tile % 2 == 0:
            for block in (far,) if tile == far else (tile, tile + 1):
                aux_z_copies[block].wait_recv()
        packet = of_tile(tile, lambda block: aux_z[block])
        row_scale = inverse_temp * packet[7:8, :]
        columns = slice(tile * rows, (tile + 1) * rows)

        def body(i, carry):
            sums, moments = carry
            part = pl.ds(pl.multiple_of(i * rows, rows), rows)
            ids = (
                lax.broadcasted_iota(jnp.int32, (rows, lanes), 0) + i * rows
            ).astype(f32) + first_slot
            times = jnp.zeros((rows, lanes), f32)
            for j in range(7):
                times = times + jnp.where(ids == packet[j : j + 1, :], 1.0, 0.0)
            scale = pcol[part, :]
            score = (sh_mine[tile, part, :] + sh_peer[tile, part, :]) * (scale * row_scale)
            weight = jnp.where(times > 0.0, times * jnp.exp(score), 0.0)
            eh_t[part, columns] = weight
            eh[columns, part] = jnp.transpose(weight * scale).astype(bf16)
            return (
                sums + jnp.sum(weight, axis=0, keepdims=True),
                moments + jnp.sum(weight * score, axis=0, keepdims=True),
            )

        zero = jnp.zeros((1, lanes), f32)
        sums, moments = lax.fori_loop(0, tiles, body, (zero, zero))
        hard_sums[tile] = jnp.where(line == 0, sums, moments)

    sum_z_copies = {}

    def send_hard_sum(slot):
        sum_out[slot] = of_tile(slot, lambda tile: hard_sums[tile])
        sum_z_copies[slot] = send(sum_out.at[slot], sum_z.at[slot], z_homes[slot])

    def in_product(start, stop, other_rows):
        def body(i, _):
            columns = pl.ds(pl.multiple_of(i * wide, wide), wide)
            pin[start:stop, columns] = dot_nn(ein[start:stop, :], other_rows[:, columns])
            return 0

        lax.fori_loop(0, width // wide, body, 0)

    grain = 16

    def stage(dst, dst_row, src, src_row, count, add=None, add_row=0):
        def body(i, _):
            values = src[pl.ds(pl.multiple_of(src_row + i * grain, grain), grain), :]
            if add is not None:
                values = values + add[
                    pl.ds(pl.multiple_of(add_row + i * grain, grain), grain), :
                ].astype(f32)
            dst[pl.ds(pl.multiple_of(dst_row + i * grain, grain), grain), :] = values.astype(
                dst.dtype
            )
            return 0

        lax.fori_loop(0, count // grain, body, 0)

    def square_first(send_buffer, recv_buffer, at):
        stage(send_buffer, 2 * rows, pin, 3 * rows, rows)
        return (
            send(send_buffer.at[rows_of(2, 0)], recv_buffer.at[rows_of(2, 0)], at(1)),
            send(send_buffer.at[rows_of(2, 1)], recv_buffer.at[rows_of(2, 1)], at(-1)),
        )

    def square_free(send_buffer, recv_buffer, at):
        stage(send_buffer, 0, pin, rows, half)
        before = send(send_buffer.at[rows_of(0, 0)], recv_buffer.at[rows_of(0, 0)], at(-1))
        stage(send_buffer, rows + half, pin, 2 * rows + half, half)
        after = send(send_buffer.at[rows_of(1, 1)], recv_buffer.at[rows_of(1, 1)], at(1))
        return [before, after]

    def square_last(first, send_buffer, recv_buffer, at):
        first[0].wait_recv()
        stage(send_buffer, rows, pin, 2 * rows, half, recv_buffer, 2 * rows)
        after = send(send_buffer.at[rows_of(1, 0)], recv_buffer.at[rows_of(1, 0)], at(1))
        first[1].wait_recv()
        stage(send_buffer, half, pin, rows + half, half, recv_buffer, 2 * rows + half)
        before = send(send_buffer.at[rows_of(0, 1)], recv_buffer.at[rows_of(0, 1)], at(-1))
        return [before, after]

    in_sums = [jnp.zeros((1, lanes), f32) for _ in range(side)]
    in_moments = [jnp.zeros((1, lanes), f32) for _ in range(side)]
    diagonal = lax.broadcasted_iota(jnp.int32, (rows, lanes), 0) == lax.broadcasted_iota(
        jnp.int32, (rows, lanes), 1
    )

    def in_part(c_start, c_stop, n_start, n_stop):
        def body(i, _):
            part = pl.ds(pl.multiple_of(c_start * rows + i * rows, rows), rows)
            scores = dot_nt(yp[part, :], xq[n_start * rows : n_stop * rows, :])
            for n in range(n_start, n_stop):
                k = (n - n_start) * lanes
                si_mine[n, part, :] = scores[:, k : k + lanes]
            return 0

        lax.fori_loop(0, c_stop - c_start, body, 0)
        block = (pl.ds(n_start, n_stop - n_start), pl.ds(c_start * rows, (c_stop - c_start) * rows))
        return send(si_mine.at[block], si_peer.at[block], other)

    def in_exp(c, n):
        c_row = position_row if c == 0 else aux_y[c - 1][0:1, :]
        scale = to_column(c_row)
        part = slice(c * rows, (c + 1) * rows)
        row_scale = inverse_temp * (q_row if n == 0 else aux_x[n - 1][7:8, :])
        columns = slice(n * rows, (n + 1) * rows)
        score = (si_mine[n, part, :] + si_peer[n, part, :]) * (scale * row_scale)
        weight = jnp.exp(score)
        own = None
        if c == 0 and n == 0:
            own = jnp.sum(jnp.where(diagonal, score, 0.0), axis=0, keepdims=True)
            weight = jnp.where(diagonal, 0.0, weight)
        ein_t[part, columns] = weight
        ein_s[part, columns] = weight * score
        ein[columns, part] = jnp.transpose(weight * scale).astype(bf16)
        in_sums[n] = in_sums[n] + jnp.sum(weight, axis=0, keepdims=True)
        in_moments[n] = in_moments[n] + jnp.sum(weight * score, axis=0, keepdims=True)
        return own

    forward_z(1, 0)
    hard_part(0, 1)
    hard_exp(0)
    forward_z(1, 1)
    x_right.wait_recv()
    x_far_right = send(xq.at[rows_of(1, 0)], xq.at[rows_of(3, 0)], at_x(1))
    x_left.wait_recv()
    x_far_left = send(xq.at[rows_of(2, 1)], xq.at[rows_of(3, 1)], at_x(-1))
    y_right.wait_recv()
    y_far_right = send(yp.at[rows_of(1, 0)], yp.at[rows_of(3, 0)], at_y(1))
    y_left.wait_recv()
    y_far_left = send(yp.at[rows_of(2, 1)], yp.at[rows_of(3, 1)], at_y(-1))
    hard_part(1, 1)
    near_copy = in_part(0, 3, 0, 3)
    hard_exp(1)
    for copy in aux_x_copies + aux_y_copies:
        copy.wait_recv()
    near_copy.wait_recv()
    own_score = in_exp(0, 0)
    for c in range(3):
        for n in range(3):
            if c or n:
                in_exp(c, n)
    forward_z(2, 0)
    hard_part(2, 1)
    x_far_right.wait_recv()
    x_far_left.wait_recv()
    far_x_copy = in_part(0, 3, 3, 4)
    y_far_right.wait_recv()
    y_far_left.wait_recv()
    far_y_copy = in_part(3, 4, 0, 4)
    hard_exp(2)
    far_x_copy.wait_recv()
    for c in range(3):
        in_exp(c, 3)
    far_y_copy.wait_recv()
    for n in range(side):
        in_exp(3, n)
    sum_x_copies = []
    for n in range(1, side):
        sum_out[6 + n] = jnp.where(line == 0, in_sums[n], in_moments[n])
        sum_x_copies.append(send(sum_out.at[6 + n], sum_x.at[n - 1], x_homes[n - 1]))
    in_product(3 * rows, 4 * rows, yp)
    x_first = square_first(xs_send, xs_recv, at_x)
    forward_z(2, 1)
    hard_part(3, 1)
    in_product(0, 3 * rows, yp)
    x_second = square_free(xs_send, xs_recv, at_x)
    hard_exp(3)
    forward_z(3, 0)
    hard_part(4, 1)
    x_second += square_last(x_first, xs_send, xs_recv, at_x)
    hard_exp(4)

    def hard_query(slot, count, base):
        def body(i, _):
            columns = pl.ds(pl.multiple_of(i * wide, wide), wide)
            pq[base : base + count * rows, columns] = dot_nn(
                eh[slot * rows : (slot + count) * rows, :], p_ref[:, columns]
            )
            return 0

        lax.fori_loop(0, width // wide, body, 0)

    back_right = {}
    back_left = {}

    pq_base = {3: 0, 2: 2 * rows, 1: 0, 4: 4 * rows}

    def stage_back(k, start, count, right, came=None, wait=True):
        first = place(k, not right, start)
        base = first - 2 * (k - 1) * rows + pq_base[k]
        if came is None:
            stage(zs_send, first, pq, base, count)
        else:
            if wait:
                (back_right if right else back_left)[came].wait_recv()
            stage(zs_send, first, pq, base, count, zs_recv, place(k + 1, not right, start))

    def start_back(k, start, count, right):
        here = pl.ds(place(k, not right, start), count)
        (back_right if right else back_left)[k, start] = send(
            zs_send.at[here], zs_recv.at[here], at_z(1 if right else -1)
        )

    def send_back(k, start, count, right, came=None, wait=True):
        stage_back(k, start, count, right, came, wait)
        start_back(k, start, count, right)

    hard_query(4, 1, 0)
    stage_back(3, half, half, True)
    stage_back(3, 0, half, False)
    forward_z(3, 1)
    hard_part(5, 1)
    start_back(3, half, half, True)
    start_back(3, 0, half, False)
    hard_exp(5)
    for slot in range(6):
        send_hard_sum(slot)
    z_right[4, 0].wait_recv()
    z_left[4, 1].wait_recv()
    hard_part(far, 1)
    hard_query(5, 1, rows)
    hard_exp(far)
    send_hard_sum(far)
    hard_query(far, 1, 4 * rows)
    send_back(4, 0, half, True)
    send_back(4, half, half, False)
    older = len(sent) - 8

    rest = in_sums[0]
    moment = in_moments[0]
    for m in range(3):
        sum_x_copies[m].wait_recv()
        rest = rest + sum_x[m][0:1, :]
        moment = moment + sum_x[m][1:2, :]
    for m in range(7):
        sum_z_copies[m].wait_recv()
        rest = rest + sum_z[m][0:1, :]
        moment = moment + sum_z[m][1:2, :]
    total = rest + jnp.exp(own_score)
    ratio = inverse_temp / total
    factor = ratio * q_row
    inverse = 1.0 / total
    fac_own[...] = jnp.where(line == 0, factor, inverse)
    fac_x_copies = [send(fac_own, fac_x.at[m], x_targets[m]) for m in range(3)]
    fac_z_copies = [send(fac_own, fac_z.at[m], z_targets[m]) for m in range(7)]
    loss_z[z] = jnp.broadcast_to(jnp.log(total) - own_score, (8, lanes))
    loss_z_copies = [send(loss_z.at[z], loss_z.at[z], at_z(k)) for k in range(1, 8)]

    hard_query(2, 2, 2 * rows)

    along = (moment - rest * own_score) / total
    own_col[...] = to_column(factor * rest)
    ratio_col[...] = to_column(factor)
    rest_col[...] = to_column(factor * rest * position_row)
    along_col[...] = to_column(along * q_row * q_row)
    repeat = width // lanes

    for copy in fac_x_copies:
        copy.wait_recv()
    for n in range(side):
        fac_row = factor if n == 0 else fac_x[n - 1][0:1, :]
        columns = slice(n * rows, (n + 1) * rows)
        for c in range(side):
            part = slice(c * rows, (c + 1) * rows)
            ein[part, columns] = (ein_t[part, columns] * fac_row).astype(bf16)

    in_product(3 * rows, 4 * rows, xq)
    y_first = square_first(ys_send, ys_recv, at_y)
    send_back(2, half, half, True, came=(3, half))
    send_back(2, 0, half, False, came=(3, 0))
    in_product(rows, 3 * rows, xq)
    y_second = square_free(ys_send, ys_recv, at_y)

    for copy in x_second:
        copy.wait_recv()

    def gather_x(i, _):
        part = pl.ds(pl.multiple_of(i * grain, grain), grain)
        after = pl.ds(pl.multiple_of(rows + i * grain, grain), grain)
        values = pin[part, :] + (
            xs_recv[part, :].astype(f32) + xs_recv[after, :].astype(f32)
        )
        dq_acc[part, :] = (
            values * tile_lanes(ratio_col[part, :], repeat)
            - yp[part, :].astype(f32) * tile_lanes(rest_col[part, :], repeat)
            - q_ref[part, :].astype(f32) * tile_lanes(along_col[part, :], repeat)
        )
        return 0

    lax.fori_loop(0, rows // grain, gather_x, 0)

    in_product(0, rows, xq)

    own_along = None
    own_copies = []
    for c in range(side):
        part = slice(c * rows, (c + 1) * rows)
        shares = jnp.zeros((rows, lanes), f32)
        for n in range(side):
            inverse_row = inverse if n == 0 else fac_x[n - 1][1:2, :]
            shares = shares + ein_s[part, n * rows : (n + 1) * rows] * inverse_row
        row = jnp.sum(jnp.transpose(shares), axis=0, keepdims=True)
        if c == 0:
            own_along = row - rest * own_score * inverse
        else:
            own_out[c - 1] = jnp.broadcast_to(row, (8, lanes))
            own_copies.append(send(own_out.at[c - 1], own_y.at[c - 1], y_homes[c - 1]))
    send_back(3, 0, half, True, came=(4, 0))
    send_back(3, half, half, False, came=(4, half))
    hard_query(0, 2, 0)

    for m in range(7):
        fac_z_copies[m].wait_recv()
    for m in range(7):
        columns = slice(m * rows, (m + 1) * rows)
        fac_row = of_tile(m, lambda block: fac_z[block][0:1, :])
        for c in range(tiles):
            part = slice(c * rows, (c + 1) * rows)
            wt[part, columns] = (eh_t[part, columns] * fac_row).astype(bf16)

    y_second += square_last(y_first, ys_send, ys_recv, at_y)
    send_back(1, half, half, True, came=(2, half))
    send_back(1, 0, half, False, came=(2, 0))

    def passage_hard(i, _):
        columns = pl.ds(pl.multiple_of(i * 256, 256), 256)
        dp_acc[:, columns] = dot_nn(wt[:, 0 : 7 * rows], zq[0 : 7 * rows, columns])
        return 0

    lax.fori_loop(0, width // 256, passage_hard, 0)
    drain(older)

    def passage_along(i, _):
        part = pl.ds(pl.multiple_of(i * grain, grain), grain)
        along_p_mine[part, :] = fold_lanes(dp_acc[part, :] * p_ref[part, :].astype(f32))
        return 0

    lax.fori_loop(0, p_rows // grain, passage_along, 0)
    along_p_copy = send(along_p_mine, along_p_peer, other)
    quarter = half // 2
    for start in (0, quarter):
        send_back(2, start, quarter, True, came=(3, 0), wait=start == 0)
        send_back(2, half + start, quarter, False, came=(3, half), wait=start == 0)

    for copy in loss_z_copies:
        copy.wait_recv()
    value = loss_z[0]
    for k in range(1, 8):
        value = value + loss_z[k]
    loss_x[x] = value
    loss_x_copies = [send(loss_x.at[x], loss_x.at[x], at_x(k)) for k in range(1, side)]
    older = len(sent) - 8
    for copy in loss_x_copies:
        copy.wait_recv()
    value = loss_x[0]
    for k in range(1, side):
        value = value + loss_x[k]
    loss_y[y] = value
    loss_y_copies = [send(loss_y.at[y], loss_y.at[y], at_y(k)) for k in range(1, side)]

    for m in range(3):
        own_copies[m].wait_recv()
        own_along = own_along + own_y[m][0:1, :]
    along_p_copy.wait_recv()
    for copy in y_second:
        copy.wait_recv()

    def positive_rows(i, _):
        part = pl.ds(pl.multiple_of(i * grain, grain), grain)
        after = pl.ds(pl.multiple_of(rows + i * grain, grain), grain)
        values = pin[part, :] + (ys_recv[part, :].astype(f32) + ys_recv[after, :].astype(f32))
        values = values - tile_lanes(own_col[part, :], repeat) * q_ref[part, :].astype(f32)
        high = values.astype(bf16)
        zq[pl.ds(pl.multiple_of(7 * rows + i * grain, grain), grain), :] = high
        zq[pl.ds(pl.multiple_of(8 * rows + i * grain, grain), grain), :] = (
            values - high.astype(f32)
        ).astype(bf16)
        return 0

    lax.fori_loop(0, rows // grain, positive_rows, 0)

    def passage_out(i, _):
        part = pl.ds(pl.multiple_of(i * rows, rows), rows)
        scale = pcol[part, :]
        shares = (along_p_mine[part, :] + along_p_peer[part, :]) * scale
        shares = shares + wt[part, 7 * rows : 8 * rows].astype(f32) * own_along
        along = jnp.sum(shares, axis=1, keepdims=True)
        along = jnp.broadcast_to(along, (rows, lanes)) * scale
        for c in range(width // wide):
            columns = slice(c * wide, (c + 1) * wide)
            values = dp_acc[part, columns] + dot_nn(
                wt[part, 7 * rows : 9 * rows], zq[7 * rows : 9 * rows, columns]
            )
            dp_ref[part, columns] = (
                (values - p_ref[part, columns].astype(f32) * tile_lanes(along, wide // lanes))
                * tile_lanes(scale, wide // lanes)
            ).astype(bf16)
        return 0

    lax.fori_loop(0, tiles // 2, passage_out, 0)
    send_back(1, 0, quarter, True, came=(2, 0))
    send_back(1, half, quarter, False, came=(2, half))
    lax.fori_loop(tiles // 2, tiles, passage_out, 0)
    send_back(1, quarter, quarter, True, came=(2, quarter))
    send_back(1, half + quarter, quarter, False, came=(2, half + quarter))
    for copy in loss_y_copies:
        copy.wait_recv()
    value = loss_y[0]
    for k in range(1, side):
        value = value + loss_y[k]
    queries = rows * owners * side * side
    loss_ref[0, 0] = jnp.sum(value[0:1, :]) * (1.0 / queries)
    drain(older)

    def query_out(first):
        def body(i, _):
            part = pl.ds(pl.multiple_of(first + i * grain, grain), grain)
            before = pl.ds(pl.multiple_of(place(1, True, first) + i * grain, grain), grain)
            after = pl.ds(pl.multiple_of(place(1, False, first) + i * grain, grain), grain)
            back = zs_recv[before, :].astype(f32) + zs_recv[after, :].astype(f32)
            dq_ref[part, :] = (
                dq_acc[part, :] + back * tile_lanes(ratio_col[part, :], repeat)
            ).astype(bf16)
            return 0

        lax.fori_loop(0, quarter // grain, body, 0)

    back_right[1, half].wait_recv()
    back_left[1, 0].wait_recv()
    for start in (0, quarter):
        back_right[1, start].wait_recv()
        query_out(start)
        back_left[1, half + start].wait_recv()
        query_out(half + start)
    drain(len(sent))


def flush(dq_ref, dp_ref, dq_out, dp_out, sems):
    copies = [
        pltpu.make_async_copy(dp_ref, dp_out, sems.at[0]),
        pltpu.make_async_copy(dq_ref, dq_out, sems.at[1]),
    ]
    for copy in copies:
        copy.start()
    for copy in copies:
        copy.wait()


def on_device(queries, passages, positive_slot, hard_offset, hard_slot):
    rows, width = queries.shape
    p_rows = passages.shape[0]
    copies = 128
    vmem = pl.BlockSpec(memory_space=pltpu.VMEM)
    hbm = pl.BlockSpec(memory_space=pltpu.HBM)

    def f(*shape):
        return pltpu.VMEM(shape, f32)

    def b(*shape):
        return pltpu.VMEM(shape, bf16)

    loss, query_grad, passage_grad = pl.pallas_call(
        kernel,
        out_shape=(
            jax.ShapeDtypeStruct((1, 1), f32),
            pltpu.VMEM(queries.shape, bf16),
            pltpu.VMEM(passages.shape, bf16),
        ),
        in_specs=[vmem, vmem, vmem, hbm, hbm],
        out_specs=(pl.BlockSpec(memory_space=pltpu.SMEM), vmem, vmem),
        scratch_shapes=[
            b(p_rows, width),
            b(9 * rows, width),
            f(7, p_rows, rows),
            f(7, p_rows, rows),
            f(p_rows, 7 * rows),
            b(7 * rows, p_rows),
            b(7 * rows, width),
            b(7 * rows, width),
            f(5 * rows, width),
            b(4 * rows, width),
            b(4 * rows, width),
            f(4, 4 * rows, rows),
            f(4, 4 * rows, rows),
            f(4 * rows, 4 * rows),
            f(4 * rows, 4 * rows),
            b(4 * rows, 4 * rows),
            f(4 * rows, width),
            b(3 * rows, width),
            b(3 * rows, width),
            b(3 * rows, width),
            b(3 * rows, width),
            f(rows, width),
            f(p_rows, width),
            b(p_rows, 9 * rows),
            b(rows, p_rows),
            f(p_rows + rows, lanes),
            f(p_rows + rows, lanes),
            f(p_rows, lanes),
            f(rows, lanes),
            f(8, lanes),
            f(7, 8, lanes),
            f(3, 8, lanes),
            f(8, lanes),
            f(3, 8, lanes),
            f(10, 8, lanes),
            f(7, 8, lanes),
            f(3, 8, lanes),
            f(8, lanes),
            f(7, 8, lanes),
            f(3, 8, lanes),
            f(3, 8, lanes),
            f(3, 8, lanes),
            f(8, 8, lanes),
            f(4, 8, lanes),
            f(4, 8, lanes),
            f(p_rows, lanes),
            f(p_rows, lanes),
            f(rows, lanes),
            f(rows, lanes),
            f(rows, lanes),
            f(rows, lanes),
            pltpu.SemaphoreType.DMA((copies,)),
            pltpu.SemaphoreType.DMA((copies,)),
            pltpu.SemaphoreType.DMA((2,)),
        ],
        compiler_params=pltpu.CompilerParams(
            collective_id=0, has_side_effects=True, vmem_limit_bytes=58 * 1024 * 1024
        ),
        cost_estimate=pl.CostEstimate(
            flops=15_000_000_000, bytes_accessed=6_000_000, transcendentals=800_000
        ),
    )(positive_slot.reshape(1, rows), hard_offset.T, hard_slot.T, queries, passages)
    query_grad, passage_grad = pl.pallas_call(
        flush,
        out_shape=(
            jax.ShapeDtypeStruct(queries.shape, bf16),
            jax.ShapeDtypeStruct(passages.shape, bf16),
        ),
        in_specs=[vmem, vmem],
        out_specs=(hbm, hbm),
        scratch_shapes=[pltpu.SemaphoreType.DMA((2,))],
        compiler_params=pltpu.CompilerParams(vmem_limit_bytes=1024 * 1024),
    )(
        pltpu.with_memory_space_constraint(query_grad, pltpu.VMEM),
        pltpu.with_memory_space_constraint(passage_grad, pltpu.VMEM),
    )
    return loss[0, 0], query_grad, passage_grad


def solution(mesh):
    in_specs = (
        P(("group", "index"), "tensor"),
        P(("group", "index"), "tensor"),
        P(("group", "index")),
        P(("group", "index"), None),
        P(("group", "index"), None),
    )
    out_specs = (P(), P(("group", "index"), "tensor"), P(("group", "index"), "tensor"))
    return jax.shard_map(
        on_device, mesh=mesh, in_specs=in_specs, out_specs=out_specs, check_vma=False
    )
```

```python
import jax
import jax.numpy as jnp
from jax import lax
from jax.experimental import pallas as pl
from jax.experimental.pallas import tpu as pltpu
from jax.sharding import PartitionSpec as P

epsilon = 1e-06
inverse_temp = 50.0
side = 4
lanes = 128
f32 = jnp.float32
bf16 = jnp.bfloat16


def dot_nt(a, b):
    return lax.dot_general(a, b, (((1,), (1,)), ((), ())), preferred_element_type=f32)


def dot_nn(a, b):
    return jnp.dot(a, b, preferred_element_type=f32)


def tile_lanes(values, count):
    return jnp.concatenate([values] * count, axis=1)


def fold_lanes(values):
    total = values[:, :lanes]
    for k in range(1, values.shape[1] // lanes):
        total = total + values[:, k * lanes : (k + 1) * lanes]
    return total


def to_column(row):
    return jnp.transpose(jnp.broadcast_to(row, (lanes, lanes)))


def kernel(
    slot_ref,
    offset_ref,
    hard_slot_ref,
    q_hbm,
    p_hbm,
    loss_ref,
    dq_ref,
    dp_ref,
    p_ref,
    zq,
    sh_mine,
    sh_peer,
    eh_t,
    eh,
    zs_send,
    zs_recv,
    pq,
    xq,
    yp,
    si_mine,
    si_peer,
    ein_t,
    ein_s,
    ein,
    pin,
    xs_send,
    xs_recv,
    ys_send,
    ys_recv,
    dq_acc,
    dp_acc,
    wt,
    pick,
    norm_mine,
    norm_peer,
    pcol,
    qcol,
    ccol,
    aux_own,
    aux_z,
    aux_x,
    pos_own,
    aux_y,
    sum_out,
    sum_z,
    sum_x,
    fac_own,
    fac_z,
    fac_x,
    own_out,
    own_y,
    loss_z,
    loss_x,
    loss_y,
    along_p_mine,
    along_p_peer,
    own_col,
    rest_col,
    ratio_col,
    along_col,
    send_sems,
    recv_sems,
    load_sems,
):
    rows, width = q_hbm.shape
    p_rows = p_ref.shape[0]
    half = rows // 2
    tiles = p_rows // rows
    group = lax.axis_index("group")
    z = lax.axis_index("index")
    t = lax.axis_index("tensor")
    y = lax.div(group, side)
    x = lax.rem(group, side)
    owners = lax.axis_size("index")

    def at_z(k):
        return (group, lax.rem(z + k + owners, owners), t)

    def at_x(k):
        return (y * side + lax.rem(x + k + side, side), z, t)

    def at_y(k):
        return (lax.rem(y + k + side, side) * side + x, z, t)

    other = (group, z, 1 - t)

    sent = []
    done = [0]

    def drain(count):
        for copy in sent[done[0] : count]:
            copy.wait_send()
        done[0] = max(done[0], count)

    def send(src, dst, target):
        k = len(sent)
        copy = pltpu.make_async_remote_copy(
            src_ref=src,
            dst_ref=dst,
            send_sem=send_sems.at[k],
            recv_sem=recv_sems.at[k],
            device_id=target,
            device_id_type=pl.DeviceIdType.MESH,
        )
        copy.start()
        sent.append(copy)
        return copy

    def rows_of(slot, part=None):
        if part is None:
            return pl.ds(slot * rows, rows)
        return pl.ds(slot * rows + part * half, half)

    far = 6

    def place(k, before, start):
        if k == 4:
            return far * rows + start
        return (2 * (k - 1) + int((start < half) != before)) * rows + start

    first_lanes = lax.broadcasted_iota(jnp.int32, (1, lanes), 1) < half

    def of_tile(tile, pair):
        if tile == far:
            return pair(far)
        block = tile - tile % 2
        low, high = (block, block + 1) if tile == block else (block + 1, block)
        return jnp.where(first_lanes, pair(low), pair(high))

    z_targets = [at_z(1), at_z(-1), at_z(2), at_z(-2), at_z(3), at_z(-3), at_z(4)]
    z_homes = [at_z(-1), at_z(1), at_z(-2), at_z(2), at_z(-3), at_z(3), at_z(4)]
    x_targets = [at_x(1), at_x(-1), at_x(2)]
    x_homes = [at_x(-1), at_x(1), at_x(2)]
    y_targets = [at_y(1), at_y(-1), at_y(2)]
    y_homes = [at_y(-1), at_y(1), at_y(2)]

    load_q = pltpu.make_async_copy(q_hbm, xq.at[rows_of(0)], load_sems.at[0])
    load_p = pltpu.make_async_copy(p_hbm, p_ref, load_sems.at[1])
    load_q.start()
    load_p.start()

    barrier = pltpu.get_barrier_semaphore()
    peers = z_targets + x_targets + y_targets + [other]
    for peer in peers:
        pl.semaphore_signal(barrier, inc=1, device_id=peer, device_id_type=pl.DeviceIdType.MESH)
    pl.semaphore_wait(barrier, len(peers))

    def z_rows(k, before, c):
        return pl.ds(place(k, before, c * half), half)

    z_right = {}
    z_left = {}
    for c in range(2):
        right_own = q_hbm.at[pl.ds(c * half, half)]
        left_own = q_hbm.at[pl.ds((1 - c) * half, half)]
        z_right[1, c] = send(right_own, zq.at[z_rows(1, True, c)], at_z(1))
        z_left[1, 1 - c] = send(left_own, zq.at[z_rows(1, False, 1 - c)], at_z(-1))
    x_right = send(q_hbm, xq.at[rows_of(1)], at_x(1))
    x_left = send(q_hbm, xq.at[rows_of(2)], at_x(-1))
    load_q.wait()
    load_p.wait()
    q_ref = xq

    slots = slot_ref[0:1, :]
    for i in range(tiles):
        ids = lax.broadcasted_iota(jnp.int32, (rows, lanes), 0) + i * rows
        chosen = jnp.where(ids == slots, 1.0, 0.0).astype(f32)
        pick[:, i * rows : (i + 1) * rows] = jnp.transpose(chosen).astype(bf16)
        wt[i * rows : (i + 1) * rows, 7 * rows : 8 * rows] = chosen.astype(bf16)
        wt[i * rows : (i + 1) * rows, 8 * rows : 9 * rows] = chosen.astype(bf16)

    wide = 512

    def pick_columns(i, _):
        columns = pl.ds(pl.multiple_of(i * wide, wide), wide)
        yp[0:rows, columns] = dot_nn(pick[...], p_ref[:, columns]).astype(bf16)
        return 0

    lax.fori_loop(0, width // wide, pick_columns, 0)
    y_right = send(yp.at[rows_of(0)], yp.at[rows_of(1)], at_y(1))
    y_left = send(yp.at[rows_of(0)], yp.at[rows_of(2)], at_y(-1))

    strip = 32

    def square_strip(source, base):
        def body(i, _):
            part = pl.ds(pl.multiple_of(i * strip, strip), strip)
            values = source[part, :].astype(f32)
            norm_mine[pl.ds(pl.multiple_of(base + i * strip, strip), strip), :] = fold_lanes(
                values * values
            )
            return 0

        return body

    lax.fori_loop(0, p_rows // strip, square_strip(p_ref, 0), 0)
    lax.fori_loop(0, rows // strip, square_strip(q_ref, p_rows), 0)
    norm_copy = send(norm_mine, norm_peer, other)
    norm_copy.wait_recv()

    def scale_of(start):
        squares = norm_mine[start : start + rows, :] + norm_peer[start : start + rows, :]
        total = jnp.sum(squares, axis=1, keepdims=True)
        return jnp.broadcast_to(1.0 / jnp.sqrt(total + epsilon), (rows, lanes))

    position_row = jnp.zeros((1, lanes), f32)
    for i in range(tiles):
        scale = scale_of(i * rows)
        pcol[i * rows : (i + 1) * rows, :] = scale
        ids = lax.broadcasted_iota(jnp.int32, (rows, lanes), 0) + i * rows
        position_row = position_row + jnp.sum(
            jnp.where(ids == slots, scale, 0.0), axis=0, keepdims=True
        )
    q_scale = scale_of(p_rows)
    qcol[...] = q_scale
    q_row = jnp.transpose(q_scale)[0:1, :]
    owner_ids = lax.rem(offset_ref[...] + (z + 1), owners)
    aux_own[0:7, :] = (owner_ids * p_rows + hard_slot_ref[...]).astype(f32)
    aux_own[7:8, :] = q_row
    pos_own[...] = jnp.broadcast_to(position_row, (8, lanes))
    aux_z_copies = [send(aux_own, aux_z.at[m], z_targets[m]) for m in range(7)]
    aux_x_copies = [send(aux_own, aux_x.at[m], x_targets[m]) for m in range(3)]
    aux_y_copies = [send(pos_own, aux_y.at[m], y_targets[m]) for m in range(3)]

    def forward_z(k, c):
        z_right[k, c].wait_recv()
        here = zq.at[z_rows(k, True, c)]
        if k < 3 or c == 0:
            z_right[k + 1, c] = send(here, zq.at[z_rows(k + 1, True, c)], at_z(1))
        z_left[k, 1 - c].wait_recv()
        here = zq.at[z_rows(k, False, 1 - c)]
        if k < 3 or c == 0:
            z_left[k + 1, 1 - c] = send(here, zq.at[z_rows(k + 1, False, 1 - c)], at_z(-1))

    line = lax.broadcasted_iota(jnp.int32, (8, lanes), 0)
    hard_copies = {}

    def hard_part(tile, count):
        def body(i, _):
            part = pl.ds(pl.multiple_of(i * 256, 256), 256)
            scores = dot_nt(p_ref[part, :], zq[tile * rows : (tile + count) * rows, :])
            for n in range(count):
                sh_mine[tile + n, part, :] = scores[:, n * lanes : (n + 1) * lanes]
            return 0

        lax.fori_loop(0, p_rows // 256, body, 0)
        here = pl.ds(tile, count)
        copy = send(sh_mine.at[here], sh_peer.at[here], other)
        for n in range(count):
            hard_copies[tile + n] = copy if n == 0 else None

    first_slot = (z * p_rows).astype(f32)
    hard_sums = {}

    def hard_exp(tile):
        if hard_copies[tile] is not None:
            hard_copies[tile].wait_recv()
        if tile == far or tile % 2 == 0:
            for block in (far,) if tile == far else (tile, tile + 1):
                aux_z_copies[block].wait_recv()
        packet = of_tile(tile, lambda block: aux_z[block])
        row_scale = inverse_temp * packet[7:8, :]
        columns = slice(tile * rows, (tile + 1) * rows)

        def body(i, carry):
            sums, moments = carry
            part = pl.ds(pl.multiple_of(i * rows, rows), rows)
            ids = (
                lax.broadcasted_iota(jnp.int32, (rows, lanes), 0) + i * rows
            ).astype(f32) + first_slot
            times = jnp.zeros((rows, lanes), f32)
            for j in range(7):
                times = times + jnp.where(ids == packet[j : j + 1, :], 1.0, 0.0)
            scale = pcol[part, :]
            score = (sh_mine[tile, part, :] + sh_peer[tile, part, :]) * (scale * row_scale)
            weight = jnp.where(times > 0.0, times * jnp.exp(score), 0.0)
            eh_t[part, columns] = weight
            eh[columns, part] = jnp.transpose(weight * scale).astype(bf16)
            return (
                sums + jnp.sum(weight, axis=0, keepdims=True),
                moments + jnp.sum(weight * score, axis=0, keepdims=True),
            )

        zero = jnp.zeros((1, lanes), f32)
        sums, moments = lax.fori_loop(0, tiles, body, (zero, zero))
        hard_sums[tile] = jnp.where(line == 0, sums, moments)

    sum_z_copies = {}

    def send_hard_sum(slot):
        sum_out[slot] = of_tile(slot, lambda tile: hard_sums[tile])
        sum_z_copies[slot] = send(sum_out.at[slot], sum_z.at[slot], z_homes[slot])

    forward_z(1, 0)
    forward_z(1, 1)
    x_right.wait_recv()
    x_far_right = send(xq.at[rows_of(1, 0)], xq.at[rows_of(3, 0)], at_x(1))
    x_left.wait_recv()
    x_far_left = send(xq.at[rows_of(2, 1)], xq.at[rows_of(3, 1)], at_x(-1))
    y_right.wait_recv()
    y_far_right = send(yp.at[rows_of(1, 0)], yp.at[rows_of(3, 0)], at_y(1))
    y_left.wait_recv()
    y_far_left = send(yp.at[rows_of(2, 1)], yp.at[rows_of(3, 1)], at_y(-1))
    hard_part(0, 2)
    hard_exp(0)
    hard_exp(1)
    forward_z(2, 0)

    x_far_right.wait_recv()
    x_far_left.wait_recv()
    y_far_right.wait_recv()
    y_far_left.wait_recv()

    def in_part(i, _):
        part = pl.ds(pl.multiple_of(i * rows, rows), rows)
        si_mine[part, :] = dot_nt(yp[part, :], xq[...])
        return 0

    lax.fori_loop(0, side, in_part, 0)
    in_copy = send(si_mine, si_peer, other)
    hard_part(2, 1)
    for copy in aux_x_copies + aux_y_copies:
        copy.wait_recv()
    in_copy.wait_recv()
    in_sums = [jnp.zeros((1, lanes), f32) for _ in range(side)]
    in_moments = [jnp.zeros((1, lanes), f32) for _ in range(side)]
    own_score = None
    diagonal = lax.broadcasted_iota(jnp.int32, (rows, lanes), 0) == lax.broadcasted_iota(
        jnp.int32, (rows, lanes), 1
    )
    for c in range(side):
        c_row = position_row if c == 0 else aux_y[c - 1][0:1, :]
        scale = to_column(c_row)
        ccol[c * rows : (c + 1) * rows, :] = scale
        part = slice(c * rows, (c + 1) * rows)
        for n in range(side):
            row_scale = inverse_temp * (q_row if n == 0 else aux_x[n - 1][7:8, :])
            columns = slice(n * rows, (n + 1) * rows)
            score = (si_mine[part, columns] + si_peer[part, columns]) * (scale * row_scale)
            weight = jnp.exp(score)
            if c == 0 and n == 0:
                own_score = jnp.sum(jnp.where(diagonal, score, 0.0), axis=0, keepdims=True)
                weight = jnp.where(diagonal, 0.0, weight)
            ein_t[part, columns] = weight
            ein_s[part, columns] = weight * score
            ein[columns, part] = jnp.transpose(weight * scale).astype(bf16)
            in_sums[n] = in_sums[n] + jnp.sum(weight, axis=0, keepdims=True)
            in_moments[n] = in_moments[n] + jnp.sum(weight * score, axis=0, keepdims=True)
    sum_x_copies = []
    for n in range(1, side):
        sum_out[6 + n] = jnp.where(line == 0, in_sums[n], in_moments[n])
        sum_x_copies.append(send(sum_out.at[6 + n], sum_x.at[n - 1], x_homes[n - 1]))

    forward_z(2, 1)

    def in_product(start, stop, other_rows):
        def body(i, _):
            columns = pl.ds(pl.multiple_of(i * wide, wide), wide)
            pin[start:stop, columns] = dot_nn(ein[start:stop, :], other_rows[:, columns])
            return 0

        lax.fori_loop(0, width // wide, body, 0)

    in_product(3 * rows, 4 * rows, yp)

    grain = 16

    def stage(dst, dst_row, src, src_row, count, add=None, add_row=0):
        def body(i, _):
            values = src[pl.ds(pl.multiple_of(src_row + i * grain, grain), grain), :]
            if add is not None:
                values = values + add[
                    pl.ds(pl.multiple_of(add_row + i * grain, grain), grain), :
                ].astype(f32)
            dst[pl.ds(pl.multiple_of(dst_row + i * grain, grain), grain), :] = values.astype(
                dst.dtype
            )
            return 0

        lax.fori_loop(0, count // grain, body, 0)

    def square_first(send_buffer, recv_buffer, at):
        stage(send_buffer, 2 * rows, pin, 3 * rows, rows)
        return (
            send(send_buffer.at[rows_of(2, 0)], recv_buffer.at[rows_of(2, 0)], at(1)),
            send(send_buffer.at[rows_of(2, 1)], recv_buffer.at[rows_of(2, 1)], at(-1)),
        )

    def square_free(send_buffer, recv_buffer, at):
        stage(send_buffer, 0, pin, rows, half)
        before = send(send_buffer.at[rows_of(0, 0)], recv_buffer.at[rows_of(0, 0)], at(-1))
        stage(send_buffer, rows + half, pin, 2 * rows + half, half)
        after = send(send_buffer.at[rows_of(1, 1)], recv_buffer.at[rows_of(1, 1)], at(1))
        return [before, after]

    def square_last(first, send_buffer, recv_buffer, at):
        first[0].wait_recv()
        stage(send_buffer, rows, pin, 2 * rows, half, recv_buffer, 2 * rows)
        after = send(send_buffer.at[rows_of(1, 0)], recv_buffer.at[rows_of(1, 0)], at(1))
        first[1].wait_recv()
        stage(send_buffer, half, pin, rows + half, half, recv_buffer, 2 * rows + half)
        before = send(send_buffer.at[rows_of(0, 1)], recv_buffer.at[rows_of(0, 1)], at(-1))
        return [before, after]

    x_first = square_first(xs_send, xs_recv, at_x)
    hard_part(3, 1)
    in_product(0, 3 * rows, yp)
    x_second = square_free(xs_send, xs_recv, at_x)
    hard_exp(2)
    forward_z(3, 0)
    hard_part(4, 1)
    hard_exp(3)
    hard_exp(4)

    def hard_query(slot, count, base):
        def body(i, _):
            columns = pl.ds(pl.multiple_of(i * wide, wide), wide)
            pq[base : base + count * rows, columns] = dot_nn(
                eh[slot * rows : (slot + count) * rows, :], p_ref[:, columns]
            )
            return 0

        lax.fori_loop(0, width // wide, body, 0)

    back_right = {}
    back_left = {}

    pq_base = {3: 0, 2: 2 * rows, 1: 0, 4: 4 * rows}

    def stage_back(k, start, count, right, came=None, wait=True):
        first = place(k, not right, start)
        base = first - 2 * (k - 1) * rows + pq_base[k]
        if came is None:
            stage(zs_send, first, pq, base, count)
        else:
            if wait:
                (back_right if right else back_left)[came].wait_recv()
            stage(zs_send, first, pq, base, count, zs_recv, place(k + 1, not right, start))

    def start_back(k, start, count, right):
        here = pl.ds(place(k, not right, start), count)
        (back_right if right else back_left)[k, start] = send(
            zs_send.at[here], zs_recv.at[here], at_z(1 if right else -1)
        )

    def send_back(k, start, count, right, came=None, wait=True):
        stage_back(k, start, count, right, came, wait)
        start_back(k, start, count, right)

    hard_query(4, 1, 0)
    stage_back(3, half, half, True)
    stage_back(3, 0, half, False)
    x_second += square_last(x_first, xs_send, xs_recv, at_x)
    forward_z(3, 1)
    hard_part(5, 1)
    start_back(3, half, half, True)
    start_back(3, 0, half, False)
    hard_exp(5)
    for slot in range(6):
        send_hard_sum(slot)
    z_right[4, 0].wait_recv()
    z_left[4, 1].wait_recv()
    hard_part(far, 1)
    hard_query(5, 1, rows)
    hard_exp(far)
    send_hard_sum(far)
    hard_query(far, 1, 4 * rows)
    send_back(4, 0, half, True)
    send_back(4, half, half, False)
    older = len(sent) - 8

    rest = in_sums[0]
    moment = in_moments[0]
    for m in range(3):
        sum_x_copies[m].wait_recv()
        rest = rest + sum_x[m][0:1, :]
        moment = moment + sum_x[m][1:2, :]
    for m in range(7):
        sum_z_copies[m].wait_recv()
        rest = rest + sum_z[m][0:1, :]
        moment = moment + sum_z[m][1:2, :]
    total = rest + jnp.exp(own_score)
    ratio = inverse_temp / total
    factor = ratio * q_row
    inverse = 1.0 / total
    fac_own[...] = jnp.where(line == 0, factor, inverse)
    fac_x_copies = [send(fac_own, fac_x.at[m], x_targets[m]) for m in range(3)]
    fac_z_copies = [send(fac_own, fac_z.at[m], z_targets[m]) for m in range(7)]
    loss_z[z] = jnp.broadcast_to(jnp.log(total) - own_score, (8, lanes))
    loss_z_copies = [send(loss_z.at[z], loss_z.at[z], at_z(k)) for k in range(1, 8)]

    hard_query(2, 2, 2 * rows)

    along = (moment - rest * own_score) / total
    own_col[...] = to_column(factor * rest)
    ratio_col[...] = to_column(factor)
    rest_col[...] = to_column(factor * rest * position_row)
    along_col[...] = to_column(along * q_row * q_row)
    repeat = width // lanes

    for copy in fac_x_copies:
        copy.wait_recv()
    for n in range(side):
        fac_row = factor if n == 0 else fac_x[n - 1][0:1, :]
        columns = slice(n * rows, (n + 1) * rows)
        for c in range(side):
            part = slice(c * rows, (c + 1) * rows)
            ein[part, columns] = (ein_t[part, columns] * fac_row).astype(bf16)

    in_product(3 * rows, 4 * rows, xq)
    y_first = square_first(ys_send, ys_recv, at_y)
    send_back(2, half, half, True, came=(3, half))
    send_back(2, 0, half, False, came=(3, 0))
    in_product(rows, 3 * rows, xq)
    y_second = square_free(ys_send, ys_recv, at_y)

    for copy in x_second:
        copy.wait_recv()

    def gather_x(i, _):
        part = pl.ds(pl.multiple_of(i * grain, grain), grain)
        after = pl.ds(pl.multiple_of(rows + i * grain, grain), grain)
        values = pin[part, :] + (
            xs_recv[part, :].astype(f32) + xs_recv[after, :].astype(f32)
        )
        dq_acc[part, :] = (
            values * tile_lanes(ratio_col[part, :], repeat)
            - yp[part, :].astype(f32) * tile_lanes(rest_col[part, :], repeat)
            - q_ref[part, :].astype(f32) * tile_lanes(along_col[part, :], repeat)
        )
        return 0

    lax.fori_loop(0, rows // grain, gather_x, 0)

    in_product(0, rows, xq)

    own_along = None
    own_copies = []
    for c in range(side):
        part = slice(c * rows, (c + 1) * rows)
        shares = jnp.zeros((rows, lanes), f32)
        for n in range(side):
            inverse_row = inverse if n == 0 else fac_x[n - 1][1:2, :]
            shares = shares + ein_s[part, n * rows : (n + 1) * rows] * inverse_row
        row = jnp.sum(jnp.transpose(shares), axis=0, keepdims=True)
        if c == 0:
            own_along = row - rest * own_score * inverse
        else:
            own_out[c - 1] = jnp.broadcast_to(row, (8, lanes))
            own_copies.append(send(own_out.at[c - 1], own_y.at[c - 1], y_homes[c - 1]))
    send_back(3, 0, half, True, came=(4, 0))
    send_back(3, half, half, False, came=(4, half))
    hard_query(0, 2, 0)

    for m in range(7):
        fac_z_copies[m].wait_recv()
    for m in range(7):
        columns = slice(m * rows, (m + 1) * rows)
        fac_row = of_tile(m, lambda block: fac_z[block][0:1, :])
        for c in range(tiles):
            part = slice(c * rows, (c + 1) * rows)
            wt[part, columns] = (eh_t[part, columns] * fac_row).astype(bf16)

    y_second += square_last(y_first, ys_send, ys_recv, at_y)
    send_back(1, half, half, True, came=(2, half))
    send_back(1, 0, half, False, came=(2, 0))

    def passage_hard(i, _):
        columns = pl.ds(pl.multiple_of(i * 256, 256), 256)
        dp_acc[:, columns] = dot_nn(wt[:, 0 : 7 * rows], zq[0 : 7 * rows, columns])
        return 0

    lax.fori_loop(0, width // 256, passage_hard, 0)
    drain(older)

    def passage_along(i, _):
        part = pl.ds(pl.multiple_of(i * grain, grain), grain)
        along_p_mine[part, :] = fold_lanes(dp_acc[part, :] * p_ref[part, :].astype(f32))
        return 0

    lax.fori_loop(0, p_rows // grain, passage_along, 0)
    along_p_copy = send(along_p_mine, along_p_peer, other)
    quarter = half // 2
    for start in (0, quarter):
        send_back(2, start, quarter, True, came=(3, 0), wait=start == 0)
        send_back(2, half + start, quarter, False, came=(3, half), wait=start == 0)

    for copy in loss_z_copies:
        copy.wait_recv()
    value = loss_z[0]
    for k in range(1, 8):
        value = value + loss_z[k]
    loss_x[x] = value
    loss_x_copies = [send(loss_x.at[x], loss_x.at[x], at_x(k)) for k in range(1, side)]
    older = len(sent) - 8
    for copy in loss_x_copies:
        copy.wait_recv()
    value = loss_x[0]
    for k in range(1, side):
        value = value + loss_x[k]
    loss_y[y] = value
    loss_y_copies = [send(loss_y.at[y], loss_y.at[y], at_y(k)) for k in range(1, side)]

    for m in range(3):
        own_copies[m].wait_recv()
        own_along = own_along + own_y[m][0:1, :]
    along_p_copy.wait_recv()
    for copy in y_second:
        copy.wait_recv()

    def positive_rows(i, _):
        part = pl.ds(pl.multiple_of(i * grain, grain), grain)
        after = pl.ds(pl.multiple_of(rows + i * grain, grain), grain)
        values = pin[part, :] + (ys_recv[part, :].astype(f32) + ys_recv[after, :].astype(f32))
        values = values - tile_lanes(own_col[part, :], repeat) * q_ref[part, :].astype(f32)
        high = values.astype(bf16)
        zq[pl.ds(pl.multiple_of(7 * rows + i * grain, grain), grain), :] = high
        zq[pl.ds(pl.multiple_of(8 * rows + i * grain, grain), grain), :] = (
            values - high.astype(f32)
        ).astype(bf16)
        return 0

    lax.fori_loop(0, rows // grain, positive_rows, 0)

    def passage_out(i, _):
        part = pl.ds(pl.multiple_of(i * rows, rows), rows)
        scale = pcol[part, :]
        shares = (along_p_mine[part, :] + along_p_peer[part, :]) * scale
        shares = shares + wt[part, 7 * rows : 8 * rows].astype(f32) * own_along
        along = jnp.sum(shares, axis=1, keepdims=True)
        along = jnp.broadcast_to(along, (rows, lanes)) * scale
        for c in range(width // wide):
            columns = slice(c * wide, (c + 1) * wide)
            values = dp_acc[part, columns] + dot_nn(
                wt[part, 7 * rows : 9 * rows], zq[7 * rows : 9 * rows, columns]
            )
            dp_ref[part, columns] = (
                (values - p_ref[part, columns].astype(f32) * tile_lanes(along, wide // lanes))
                * tile_lanes(scale, wide // lanes)
            ).astype(bf16)
        return 0

    lax.fori_loop(0, tiles // 2, passage_out, 0)
    send_back(1, 0, quarter, True, came=(2, 0))
    send_back(1, half, quarter, False, came=(2, half))
    lax.fori_loop(tiles // 2, tiles, passage_out, 0)
    send_back(1, quarter, quarter, True, came=(2, quarter))
    send_back(1, half + quarter, quarter, False, came=(2, half + quarter))
    for copy in loss_y_copies:
        copy.wait_recv()
    value = loss_y[0]
    for k in range(1, side):
        value = value + loss_y[k]
    queries = rows * owners * side * side
    mean = jnp.sum(value[0:1, :], axis=1, keepdims=True) * (1.0 / queries)
    loss_ref[...] = jnp.broadcast_to(mean, (8, lanes))
    drain(older)

    def query_out(first):
        def body(i, _):
            part = pl.ds(pl.multiple_of(first + i * grain, grain), grain)
            before = pl.ds(pl.multiple_of(place(1, True, first) + i * grain, grain), grain)
            after = pl.ds(pl.multiple_of(place(1, False, first) + i * grain, grain), grain)
            back = zs_recv[before, :].astype(f32) + zs_recv[after, :].astype(f32)
            dq_ref[part, :] = (
                dq_acc[part, :] + back * tile_lanes(ratio_col[part, :], repeat)
            ).astype(bf16)
            return 0

        lax.fori_loop(0, quarter // grain, body, 0)

    back_right[1, half].wait_recv()
    back_left[1, 0].wait_recv()
    for start in (0, quarter):
        back_right[1, start].wait_recv()
        query_out(start)
        back_left[1, half + start].wait_recv()
        query_out(half + start)
    drain(len(sent))


def flush(loss_ref, dq_ref, dp_ref, loss_out, dq_out, dp_out, one, sems):
    copies = [
        pltpu.make_async_copy(dp_ref, dp_out, sems.at[0]),
        pltpu.make_async_copy(dq_ref, dq_out, sems.at[1]),
    ]
    for copy in copies:
        copy.start()
    one[...] = loss_ref[0:1, 0:1]
    copies.append(pltpu.make_async_copy(one, loss_out, sems.at[2]))
    copies[2].start()
    for copy in copies:
        copy.wait()


def on_device(queries, passages, positive_slot, hard_offset, hard_slot):
    rows, width = queries.shape
    p_rows = passages.shape[0]
    copies = 110
    vmem = pl.BlockSpec(memory_space=pltpu.VMEM)
    hbm = pl.BlockSpec(memory_space=pltpu.HBM)

    def f(*shape):
        return pltpu.VMEM(shape, f32)

    def b(*shape):
        return pltpu.VMEM(shape, bf16)

    loss, query_grad, passage_grad = pl.pallas_call(
        kernel,
        out_shape=(
            pltpu.VMEM((8, lanes), f32),
            pltpu.VMEM(queries.shape, bf16),
            pltpu.VMEM(passages.shape, bf16),
        ),
        in_specs=[vmem, vmem, vmem, hbm, hbm],
        out_specs=(vmem, vmem, vmem),
        scratch_shapes=[
            b(p_rows, width),
            b(9 * rows, width),
            f(7, p_rows, rows),
            f(7, p_rows, rows),
            f(p_rows, 7 * rows),
            b(7 * rows, p_rows),
            b(7 * rows, width),
            b(7 * rows, width),
            f(5 * rows, width),
            b(4 * rows, width),
            b(4 * rows, width),
            f(4 * rows, 4 * rows),
            f(4 * rows, 4 * rows),
            f(4 * rows, 4 * rows),
            f(4 * rows, 4 * rows),
            b(4 * rows, 4 * rows),
            f(4 * rows, width),
            b(3 * rows, width),
            b(3 * rows, width),
            b(3 * rows, width),
            b(3 * rows, width),
            f(rows, width),
            f(p_rows, width),
            b(p_rows, 9 * rows),
            b(rows, p_rows),
            f(p_rows + rows, lanes),
            f(p_rows + rows, lanes),
            f(p_rows, lanes),
            f(rows, lanes),
            f(4 * rows, lanes),
            f(8, lanes),
            f(7, 8, lanes),
            f(3, 8, lanes),
            f(8, lanes),
            f(3, 8, lanes),
            f(10, 8, lanes),
            f(7, 8, lanes),
            f(3, 8, lanes),
            f(8, lanes),
            f(7, 8, lanes),
            f(3, 8, lanes),
            f(3, 8, lanes),
            f(3, 8, lanes),
            f(8, 8, lanes),
            f(4, 8, lanes),
            f(4, 8, lanes),
            f(p_rows, lanes),
            f(p_rows, lanes),
            f(rows, lanes),
            f(rows, lanes),
            f(rows, lanes),
            f(rows, lanes),
            pltpu.SemaphoreType.DMA((copies,)),
            pltpu.SemaphoreType.DMA((copies,)),
            pltpu.SemaphoreType.DMA((2,)),
        ],
        compiler_params=pltpu.CompilerParams(
            collective_id=0, has_side_effects=True, vmem_limit_bytes=58 * 1024 * 1024
        ),
        cost_estimate=pl.CostEstimate(
            flops=15_000_000_000, bytes_accessed=6_000_000, transcendentals=800_000
        ),
    )(positive_slot.reshape(1, rows), hard_offset.T, hard_slot.T, queries, passages)
    loss, query_grad, passage_grad = pl.pallas_call(
        flush,
        out_shape=(
            jax.ShapeDtypeStruct((1, 1), f32),
            jax.ShapeDtypeStruct(queries.shape, bf16),
            jax.ShapeDtypeStruct(passages.shape, bf16),
        ),
        in_specs=[vmem, vmem, vmem],
        out_specs=(hbm, hbm, hbm),
        scratch_shapes=[f(1, 1), pltpu.SemaphoreType.DMA((3,))],
        compiler_params=pltpu.CompilerParams(vmem_limit_bytes=1024 * 1024),
    )(
        pltpu.with_memory_space_constraint(loss, pltpu.VMEM),
        pltpu.with_memory_space_constraint(query_grad, pltpu.VMEM),
        pltpu.with_memory_space_constraint(passage_grad, pltpu.VMEM),
    )
    return loss[0, 0], query_grad, passage_grad


def solution(mesh):
    in_specs = (
        P(("group", "index"), "tensor"),
        P(("group", "index"), "tensor"),
        P(("group", "index")),
        P(("group", "index"), None),
        P(("group", "index"), None),
    )
    out_specs = (P(), P(("group", "index"), "tensor"), P(("group", "index"), "tensor"))
    return jax.shard_map(
        on_device, mesh=mesh, in_specs=in_specs, out_specs=out_specs, check_vma=False
    )
```

```python
import jax
import jax.numpy as jnp
from jax import lax
from jax.experimental import pallas as pl
from jax.experimental.pallas import tpu as pltpu
from jax.sharding import PartitionSpec as P

epsilon = 1e-06
inverse_temp = 50.0
side = 4
lanes = 128
shared = ("aux_z", "aux_x", "aux_y", "sum_z", "sum_x", "fac_z", "fac_x", "own")
shared = shared + ("loss_z", "loss_x", "loss_y")
kinds = shared + ("z", "x", "y", "back_z", "back_x", "back_y", "norm", "hard", "in", "along")
alone = 61
f32 = jnp.float32
bf16 = jnp.bfloat16


def dot_nt(a, b):
    return lax.dot_general(a, b, (((1,), (1,)), ((), ())), preferred_element_type=f32)


def dot_nn(a, b):
    return jnp.dot(a, b, preferred_element_type=f32)


def tile_lanes(values, count):
    return jnp.concatenate([values] * count, axis=1)


def fold_lanes(values):
    total = values[:, :lanes]
    for k in range(1, values.shape[1] // lanes):
        total = total + values[:, k * lanes : (k + 1) * lanes]
    return total


def to_column(row):
    return jnp.transpose(jnp.broadcast_to(row, (lanes, lanes)))


def kernel(
    slot_ref,
    offset_ref,
    hard_slot_ref,
    q_hbm,
    p_hbm,
    loss_ref,
    dq_ref,
    dp_ref,
    p_ref,
    zq,
    sh_mine,
    sh_peer,
    eh_t,
    eh,
    zs_send,
    zs_recv,
    pq,
    xq,
    yp,
    si_mine,
    si_peer,
    ein_t,
    ein_s,
    ein,
    pin,
    xs_send,
    xs_recv,
    ys_send,
    ys_recv,
    dq_acc,
    dp_acc,
    wt,
    pick,
    norm_mine,
    norm_peer,
    pcol,
    qcol,
    ccol,
    aux_own,
    aux_z,
    aux_x,
    pos_own,
    aux_y,
    sum_out,
    sum_z,
    sum_x,
    fac_own,
    fac_z,
    fac_x,
    own_out,
    own_y,
    loss_z,
    loss_x,
    loss_y,
    along_p_mine,
    along_p_peer,
    own_col,
    rest_col,
    ratio_col,
    along_col,
    send_sems,
    recv_sems,
    load_sems,
):
    rows, width = q_hbm.shape
    p_rows = p_ref.shape[0]
    half = rows // 2
    tiles = p_rows // rows
    group = lax.axis_index("group")
    z = lax.axis_index("index")
    t = lax.axis_index("tensor")
    y = lax.div(group, side)
    x = lax.rem(group, side)
    owners = lax.axis_size("index")

    def at_z(k):
        return (group, lax.rem(z + k + owners, owners), t)

    def at_x(k):
        return (y * side + lax.rem(x + k + side, side), z, t)

    def at_y(k):
        return (lax.rem(y + k + side, side) * side + x, z, t)

    other = (group, z, 1 - t)

    received = []

    def send(src, dst, target, kind, together=False):
        if not together:
            received.append(kind)
        slot = kinds.index(kind) if together else len(shared) + len(received) - 1
        copy = pltpu.make_async_remote_copy(
            src_ref=src,
            dst_ref=dst,
            send_sem=send_sems.at[kinds.index(kind)],
            recv_sem=recv_sems.at[slot],
            device_id=target,
            device_id_type=pl.DeviceIdType.MESH,
        )
        copy.start()
        return copy

    def wait_sent(kind, ref):
        pltpu.make_async_copy(ref, ref, send_sems.at[kinds.index(kind)]).wait()

    def wait_came(kind, ref):
        pltpu.make_async_copy(ref, ref, recv_sems.at[kinds.index(kind)]).wait()

    def rows_of(slot, part=None):
        if part is None:
            return pl.ds(slot * rows, rows)
        return pl.ds(slot * rows + part * half, half)

    far = 6

    def place(k, before, start):
        if k == 4:
            return far * rows + start
        return (2 * (k - 1) + int((start < half) != before)) * rows + start

    first_lanes = lax.broadcasted_iota(jnp.int32, (1, lanes), 1) < half

    def of_tile(tile, pair):
        if tile == far:
            return pair(far)
        block = tile - tile % 2
        low, high = (block, block + 1) if tile == block else (block + 1, block)
        return jnp.where(first_lanes, pair(low), pair(high))

    z_targets = [at_z(1), at_z(-1), at_z(2), at_z(-2), at_z(3), at_z(-3), at_z(4)]
    z_homes = [at_z(-1), at_z(1), at_z(-2), at_z(2), at_z(-3), at_z(3), at_z(4)]
    x_targets = [at_x(1), at_x(-1), at_x(2)]
    x_homes = [at_x(-1), at_x(1), at_x(2)]
    y_targets = [at_y(1), at_y(-1), at_y(2)]
    y_homes = [at_y(-1), at_y(1), at_y(2)]

    load_q = pltpu.make_async_copy(q_hbm, xq.at[rows_of(0)], load_sems.at[0])
    load_p = pltpu.make_async_copy(p_hbm, p_ref, load_sems.at[1])
    load_q.start()
    load_p.start()

    barrier = pltpu.get_barrier_semaphore()
    peers = z_targets + x_targets + y_targets + [other]
    for peer in peers:
        pl.semaphore_signal(barrier, inc=1, device_id=peer, device_id_type=pl.DeviceIdType.MESH)
    pl.semaphore_wait(barrier, len(peers))

    def z_rows(k, before, c):
        return pl.ds(place(k, before, c * half), half)

    z_right = {}
    z_left = {}
    for c in range(2):
        right_own = q_hbm.at[pl.ds(c * half, half)]
        left_own = q_hbm.at[pl.ds((1 - c) * half, half)]
        z_right[1, c] = send(right_own, zq.at[z_rows(1, True, c)], at_z(1), "z")
        z_left[1, 1 - c] = send(left_own, zq.at[z_rows(1, False, 1 - c)], at_z(-1), "z")
    x_right = send(q_hbm, xq.at[rows_of(1)], at_x(1), "x")
    x_left = send(q_hbm, xq.at[rows_of(2)], at_x(-1), "x")
    load_q.wait()
    load_p.wait()
    q_ref = xq

    slots = slot_ref[0:1, :]
    for i in range(tiles):
        ids = lax.broadcasted_iota(jnp.int32, (rows, lanes), 0) + i * rows
        chosen = jnp.where(ids == slots, 1.0, 0.0).astype(f32)
        pick[:, i * rows : (i + 1) * rows] = jnp.transpose(chosen).astype(bf16)
        wt[i * rows : (i + 1) * rows, 7 * rows : 8 * rows] = chosen.astype(bf16)
        wt[i * rows : (i + 1) * rows, 8 * rows : 9 * rows] = chosen.astype(bf16)

    wide = 512

    def pick_columns(i, _):
        columns = pl.ds(pl.multiple_of(i * wide, wide), wide)
        yp[0:rows, columns] = dot_nn(pick[...], p_ref[:, columns]).astype(bf16)
        return 0

    lax.fori_loop(0, width // wide, pick_columns, 0)
    y_right = send(yp.at[rows_of(0)], yp.at[rows_of(1)], at_y(1), "y")
    y_left = send(yp.at[rows_of(0)], yp.at[rows_of(2)], at_y(-1), "y")

    strip = 32

    def square_strip(source, base):
        def body(i, _):
            part = pl.ds(pl.multiple_of(i * strip, strip), strip)
            values = source[part, :].astype(f32)
            norm_mine[pl.ds(pl.multiple_of(base + i * strip, strip), strip), :] = fold_lanes(
                values * values
            )
            return 0

        return body

    lax.fori_loop(0, p_rows // strip, square_strip(p_ref, 0), 0)
    lax.fori_loop(0, rows // strip, square_strip(q_ref, p_rows), 0)
    norm_copy = send(norm_mine, norm_peer, other, "norm")
    norm_copy.wait_recv()

    def scale_of(start):
        squares = norm_mine[start : start + rows, :] + norm_peer[start : start + rows, :]
        total = jnp.sum(squares, axis=1, keepdims=True)
        return jnp.broadcast_to(1.0 / jnp.sqrt(total + epsilon), (rows, lanes))

    position_row = jnp.zeros((1, lanes), f32)
    for i in range(tiles):
        scale = scale_of(i * rows)
        pcol[i * rows : (i + 1) * rows, :] = scale
        ids = lax.broadcasted_iota(jnp.int32, (rows, lanes), 0) + i * rows
        position_row = position_row + jnp.sum(
            jnp.where(ids == slots, scale, 0.0), axis=0, keepdims=True
        )
    q_scale = scale_of(p_rows)
    qcol[...] = q_scale
    q_row = jnp.transpose(q_scale)[0:1, :]
    owner_ids = lax.rem(offset_ref[...] + (z + 1), owners)
    aux_own[0:7, :] = (owner_ids * p_rows + hard_slot_ref[...]).astype(f32)
    aux_own[7:8, :] = q_row
    pos_own[...] = jnp.broadcast_to(position_row, (8, lanes))
    for m in range(7):
        send(aux_own, aux_z.at[m], z_targets[m], "aux_z", True)
    for m in range(3):
        send(aux_own, aux_x.at[m], x_targets[m], "aux_x", True)
        send(pos_own, aux_y.at[m], y_targets[m], "aux_y", True)

    def forward_z(k, c):
        z_right[k, c].wait_recv()
        here = zq.at[z_rows(k, True, c)]
        if k < 3 or c == 0:
            z_right[k + 1, c] = send(here, zq.at[z_rows(k + 1, True, c)], at_z(1), "z")
        z_left[k, 1 - c].wait_recv()
        here = zq.at[z_rows(k, False, 1 - c)]
        if k < 3 or c == 0:
            z_left[k + 1, 1 - c] = send(here, zq.at[z_rows(k + 1, False, 1 - c)], at_z(-1), "z")

    line = lax.broadcasted_iota(jnp.int32, (8, lanes), 0)
    hard_copies = {}

    def hard_part(tile, count):
        def body(i, _):
            part = pl.ds(pl.multiple_of(i * 256, 256), 256)
            scores = dot_nt(p_ref[part, :], zq[tile * rows : (tile + count) * rows, :])
            for n in range(count):
                sh_mine[tile + n, part, :] = scores[:, n * lanes : (n + 1) * lanes]
            return 0

        lax.fori_loop(0, p_rows // 256, body, 0)
        here = pl.ds(tile, count)
        copy = send(sh_mine.at[here], sh_peer.at[here], other, "hard")
        for n in range(count):
            hard_copies[tile + n] = copy if n == 0 else None

    first_slot = (z * p_rows).astype(f32)
    hard_sums = {}

    def hard_exp(tile):
        if hard_copies[tile] is not None:
            hard_copies[tile].wait_recv()
        if tile == 0:
            wait_came("aux_z", aux_z)
        packet = of_tile(tile, lambda block: aux_z[block])
        row_scale = inverse_temp * packet[7:8, :]
        columns = slice(tile * rows, (tile + 1) * rows)

        def body(i, carry):
            sums, moments = carry
            part = pl.ds(pl.multiple_of(i * rows, rows), rows)
            ids = (
                lax.broadcasted_iota(jnp.int32, (rows, lanes), 0) + i * rows
            ).astype(f32) + first_slot
            times = jnp.zeros((rows, lanes), f32)
            for j in range(7):
                times = times + jnp.where(ids == packet[j : j + 1, :], 1.0, 0.0)
            scale = pcol[part, :]
            score = (sh_mine[tile, part, :] + sh_peer[tile, part, :]) * (scale * row_scale)
            weight = jnp.where(times > 0.0, times * jnp.exp(score), 0.0)
            eh_t[part, columns] = weight
            eh[columns, part] = jnp.transpose(weight * scale).astype(bf16)
            return (
                sums + jnp.sum(weight, axis=0, keepdims=True),
                moments + jnp.sum(weight * score, axis=0, keepdims=True),
            )

        zero = jnp.zeros((1, lanes), f32)
        sums, moments = lax.fori_loop(0, tiles, body, (zero, zero))
        hard_sums[tile] = jnp.where(line == 0, sums, moments)

    def send_hard_sum(slot):
        sum_out[slot] = of_tile(slot, lambda tile: hard_sums[tile])
        send(sum_out.at[slot], sum_z.at[slot], z_homes[slot], "sum_z", True)

    forward_z(1, 0)
    forward_z(1, 1)
    x_right.wait_recv()
    x_far_right = send(xq.at[rows_of(1, 0)], xq.at[rows_of(3, 0)], at_x(1), "x")
    x_left.wait_recv()
    x_far_left = send(xq.at[rows_of(2, 1)], xq.at[rows_of(3, 1)], at_x(-1), "x")
    y_right.wait_recv()
    y_far_right = send(yp.at[rows_of(1, 0)], yp.at[rows_of(3, 0)], at_y(1), "y")
    y_left.wait_recv()
    y_far_left = send(yp.at[rows_of(2, 1)], yp.at[rows_of(3, 1)], at_y(-1), "y")
    hard_part(0, 2)
    hard_exp(0)
    hard_exp(1)
    forward_z(2, 0)

    x_far_right.wait_recv()
    x_far_left.wait_recv()
    y_far_right.wait_recv()
    y_far_left.wait_recv()

    def in_part(i, _):
        part = pl.ds(pl.multiple_of(i * rows, rows), rows)
        si_mine[part, :] = dot_nt(yp[part, :], xq[...])
        return 0

    lax.fori_loop(0, side, in_part, 0)
    in_copy = send(si_mine, si_peer, other, "in")
    hard_part(2, 1)
    wait_came("aux_x", aux_x)
    wait_came("aux_y", aux_y)
    in_copy.wait_recv()
    in_sums = [jnp.zeros((1, lanes), f32) for _ in range(side)]
    in_moments = [jnp.zeros((1, lanes), f32) for _ in range(side)]
    own_score = None
    diagonal = lax.broadcasted_iota(jnp.int32, (rows, lanes), 0) == lax.broadcasted_iota(
        jnp.int32, (rows, lanes), 1
    )
    for c in range(side):
        c_row = position_row if c == 0 else aux_y[c - 1][0:1, :]
        scale = to_column(c_row)
        ccol[c * rows : (c + 1) * rows, :] = scale
        part = slice(c * rows, (c + 1) * rows)
        for n in range(side):
            row_scale = inverse_temp * (q_row if n == 0 else aux_x[n - 1][7:8, :])
            columns = slice(n * rows, (n + 1) * rows)
            score = (si_mine[part, columns] + si_peer[part, columns]) * (scale * row_scale)
            weight = jnp.exp(score)
            if c == 0 and n == 0:
                own_score = jnp.sum(jnp.where(diagonal, score, 0.0), axis=0, keepdims=True)
                weight = jnp.where(diagonal, 0.0, weight)
            ein_t[part, columns] = weight
            ein_s[part, columns] = weight * score
            ein[columns, part] = jnp.transpose(weight * scale).astype(bf16)
            in_sums[n] = in_sums[n] + jnp.sum(weight, axis=0, keepdims=True)
            in_moments[n] = in_moments[n] + jnp.sum(weight * score, axis=0, keepdims=True)
    for n in range(1, side):
        sum_out[6 + n] = jnp.where(line == 0, in_sums[n], in_moments[n])
        send(sum_out.at[6 + n], sum_x.at[n - 1], x_homes[n - 1], "sum_x", True)

    forward_z(2, 1)

    def in_product(start, stop, other_rows):
        def body(i, _):
            columns = pl.ds(pl.multiple_of(i * wide, wide), wide)
            pin[start:stop, columns] = dot_nn(ein[start:stop, :], other_rows[:, columns])
            return 0

        lax.fori_loop(0, width // wide, body, 0)

    in_product(3 * rows, 4 * rows, yp)

    grain = 16

    def stage(dst, dst_row, src, src_row, count, add=None, add_row=0):
        def body(i, _):
            values = src[pl.ds(pl.multiple_of(src_row + i * grain, grain), grain), :]
            if add is not None:
                values = values + add[
                    pl.ds(pl.multiple_of(add_row + i * grain, grain), grain), :
                ].astype(f32)
            dst[pl.ds(pl.multiple_of(dst_row + i * grain, grain), grain), :] = values.astype(
                dst.dtype
            )
            return 0

        lax.fori_loop(0, count // grain, body, 0)

    def square_first(send_buffer, recv_buffer, at, kind):
        stage(send_buffer, 2 * rows, pin, 3 * rows, rows)
        return (
            send(send_buffer.at[rows_of(2, 0)], recv_buffer.at[rows_of(2, 0)], at(1), kind),
            send(send_buffer.at[rows_of(2, 1)], recv_buffer.at[rows_of(2, 1)], at(-1), kind),
        )

    def square_free(send_buffer, recv_buffer, at, kind):
        stage(send_buffer, 0, pin, rows, half)
        before = send(send_buffer.at[rows_of(0, 0)], recv_buffer.at[rows_of(0, 0)], at(-1), kind)
        stage(send_buffer, rows + half, pin, 2 * rows + half, half)
        after = send(send_buffer.at[rows_of(1, 1)], recv_buffer.at[rows_of(1, 1)], at(1), kind)
        return [before, after]

    def square_last(first, send_buffer, recv_buffer, at, kind):
        first[0].wait_recv()
        stage(send_buffer, rows, pin, 2 * rows, half, recv_buffer, 2 * rows)
        after = send(send_buffer.at[rows_of(1, 0)], recv_buffer.at[rows_of(1, 0)], at(1), kind)
        first[1].wait_recv()
        stage(send_buffer, half, pin, rows + half, half, recv_buffer, 2 * rows + half)
        before = send(send_buffer.at[rows_of(0, 1)], recv_buffer.at[rows_of(0, 1)], at(-1), kind)
        return [before, after]

    x_first = square_first(xs_send, xs_recv, at_x, "back_x")
    hard_part(3, 1)
    in_product(0, 3 * rows, yp)
    x_second = square_free(xs_send, xs_recv, at_x, "back_x")
    hard_exp(2)
    forward_z(3, 0)
    hard_part(4, 1)
    hard_exp(3)
    hard_exp(4)

    def hard_query(slot, count, base):
        def body(i, _):
            columns = pl.ds(pl.multiple_of(i * wide, wide), wide)
            pq[base : base + count * rows, columns] = dot_nn(
                eh[slot * rows : (slot + count) * rows, :], p_ref[:, columns]
            )
            return 0

        lax.fori_loop(0, width // wide, body, 0)

    back_right = {}
    back_left = {}

    pq_base = {3: 0, 2: 2 * rows, 1: 0, 4: 4 * rows}

    def stage_back(k, start, count, right, came=None, wait=True):
        first = place(k, not right, start)
        base = first - 2 * (k - 1) * rows + pq_base[k]
        if came is None:
            stage(zs_send, first, pq, base, count)
        else:
            if wait:
                (back_right if right else back_left)[came].wait_recv()
            stage(zs_send, first, pq, base, count, zs_recv, place(k + 1, not right, start))

    def start_back(k, start, count, right):
        here = pl.ds(place(k, not right, start), count)
        (back_right if right else back_left)[k, start] = send(
            zs_send.at[here], zs_recv.at[here], at_z(1 if right else -1), "back_z"
        )

    def send_back(k, start, count, right, came=None, wait=True):
        stage_back(k, start, count, right, came, wait)
        start_back(k, start, count, right)

    hard_query(4, 1, 0)
    stage_back(3, half, half, True)
    stage_back(3, 0, half, False)
    x_second += square_last(x_first, xs_send, xs_recv, at_x, "back_x")
    forward_z(3, 1)
    hard_part(5, 1)
    start_back(3, half, half, True)
    start_back(3, 0, half, False)
    hard_exp(5)
    for slot in range(6):
        send_hard_sum(slot)
    z_right[4, 0].wait_recv()
    z_left[4, 1].wait_recv()
    hard_part(far, 1)
    hard_query(5, 1, rows)
    hard_exp(far)
    send_hard_sum(far)
    hard_query(far, 1, 4 * rows)
    send_back(4, 0, half, True)
    send_back(4, half, half, False)

    rest = in_sums[0]
    moment = in_moments[0]
    wait_came("sum_x", sum_x)
    wait_came("sum_z", sum_z)
    for m in range(3):
        rest = rest + sum_x[m][0:1, :]
        moment = moment + sum_x[m][1:2, :]
    for m in range(7):
        rest = rest + sum_z[m][0:1, :]
        moment = moment + sum_z[m][1:2, :]
    total = rest + jnp.exp(own_score)
    ratio = inverse_temp / total
    factor = ratio * q_row
    inverse = 1.0 / total
    fac_own[...] = jnp.where(line == 0, factor, inverse)
    for m in range(3):
        send(fac_own, fac_x.at[m], x_targets[m], "fac_x", True)
    for m in range(7):
        send(fac_own, fac_z.at[m], z_targets[m], "fac_z", True)
    loss_z[z] = jnp.broadcast_to(jnp.log(total) - own_score, (8, lanes))
    for k in range(1, 8):
        send(loss_z.at[z], loss_z.at[z], at_z(k), "loss_z", True)

    hard_query(2, 2, 2 * rows)

    along = (moment - rest * own_score) / total
    own_col[...] = to_column(factor * rest)
    ratio_col[...] = to_column(factor)
    rest_col[...] = to_column(factor * rest * position_row)
    along_col[...] = to_column(along * q_row * q_row)
    repeat = width // lanes

    wait_came("fac_x", fac_x)
    for n in range(side):
        fac_row = factor if n == 0 else fac_x[n - 1][0:1, :]
        columns = slice(n * rows, (n + 1) * rows)
        for c in range(side):
            part = slice(c * rows, (c + 1) * rows)
            ein[part, columns] = (ein_t[part, columns] * fac_row).astype(bf16)

    in_product(3 * rows, 4 * rows, xq)
    y_first = square_first(ys_send, ys_recv, at_y, "back_y")
    send_back(2, half, half, True, came=(3, half))
    send_back(2, 0, half, False, came=(3, 0))
    in_product(rows, 3 * rows, xq)
    y_second = square_free(ys_send, ys_recv, at_y, "back_y")

    for copy in x_second:
        copy.wait_recv()

    def gather_x(i, _):
        part = pl.ds(pl.multiple_of(i * grain, grain), grain)
        after = pl.ds(pl.multiple_of(rows + i * grain, grain), grain)
        values = pin[part, :] + (
            xs_recv[part, :].astype(f32) + xs_recv[after, :].astype(f32)
        )
        dq_acc[part, :] = (
            values * tile_lanes(ratio_col[part, :], repeat)
            - yp[part, :].astype(f32) * tile_lanes(rest_col[part, :], repeat)
            - q_ref[part, :].astype(f32) * tile_lanes(along_col[part, :], repeat)
        )
        return 0

    lax.fori_loop(0, rows // grain, gather_x, 0)

    in_product(0, rows, xq)

    own_along = None
    for c in range(side):
        part = slice(c * rows, (c + 1) * rows)
        shares = jnp.zeros((rows, lanes), f32)
        for n in range(side):
            inverse_row = inverse if n == 0 else fac_x[n - 1][1:2, :]
            shares = shares + ein_s[part, n * rows : (n + 1) * rows] * inverse_row
        row = jnp.sum(jnp.transpose(shares), axis=0, keepdims=True)
        if c == 0:
            own_along = row - rest * own_score * inverse
        else:
            own_out[c - 1] = jnp.broadcast_to(row, (8, lanes))
            send(own_out.at[c - 1], own_y.at[c - 1], y_homes[c - 1], "own", True)
    send_back(3, 0, half, True, came=(4, 0))
    send_back(3, half, half, False, came=(4, half))
    hard_query(0, 2, 0)

    wait_came("fac_z", fac_z)
    for m in range(7):
        columns = slice(m * rows, (m + 1) * rows)
        fac_row = of_tile(m, lambda block: fac_z[block][0:1, :])
        for c in range(tiles):
            part = slice(c * rows, (c + 1) * rows)
            wt[part, columns] = (eh_t[part, columns] * fac_row).astype(bf16)

    y_second += square_last(y_first, ys_send, ys_recv, at_y, "back_y")
    send_back(1, half, half, True, came=(2, half))
    send_back(1, 0, half, False, came=(2, 0))

    def passage_hard(i, _):
        columns = pl.ds(pl.multiple_of(i * 256, 256), 256)
        dp_acc[:, columns] = dot_nn(wt[:, 0 : 7 * rows], zq[0 : 7 * rows, columns])
        return 0

    lax.fori_loop(0, width // 256, passage_hard, 0)
    wait_sent("z", zq.at[pl.ds(0, 7 * rows)])
    wait_sent("x", xq.at[pl.ds(0, 3 * rows)])
    wait_sent("y", yp.at[pl.ds(0, 3 * rows)])
    wait_sent("back_x", xs_send)
    wait_sent("norm", norm_mine)
    wait_sent("hard", sh_mine)
    wait_sent("in", si_mine)
    wait_sent("aux_z", aux_z)
    wait_sent("aux_x", aux_x)
    wait_sent("aux_y", aux_y)
    wait_sent("sum_z", sum_z)
    wait_sent("sum_x", sum_x)
    wait_sent("fac_z", fac_z)
    wait_sent("fac_x", fac_x)
    wait_sent("own", own_y)

    def passage_along(i, _):
        part = pl.ds(pl.multiple_of(i * grain, grain), grain)
        along_p_mine[part, :] = fold_lanes(dp_acc[part, :] * p_ref[part, :].astype(f32))
        return 0

    lax.fori_loop(0, p_rows // grain, passage_along, 0)
    along_p_copy = send(along_p_mine, along_p_peer, other, "along")
    quarter = half // 2
    for start in (0, quarter):
        send_back(2, start, quarter, True, came=(3, 0), wait=start == 0)
        send_back(2, half + start, quarter, False, came=(3, half), wait=start == 0)

    wait_came("loss_z", loss_z.at[pl.ds(0, 7)])
    value = loss_z[0]
    for k in range(1, 8):
        value = value + loss_z[k]
    loss_x[x] = value
    for k in range(1, side):
        send(loss_x.at[x], loss_x.at[x], at_x(k), "loss_x", True)
    wait_came("loss_x", loss_x.at[pl.ds(0, 3)])
    value = loss_x[0]
    for k in range(1, side):
        value = value + loss_x[k]
    loss_y[y] = value
    for k in range(1, side):
        send(loss_y.at[y], loss_y.at[y], at_y(k), "loss_y", True)

    wait_came("own", own_y)
    for m in range(3):
        own_along = own_along + own_y[m][0:1, :]
    along_p_copy.wait_recv()
    for copy in y_second:
        copy.wait_recv()

    def positive_rows(i, _):
        part = pl.ds(pl.multiple_of(i * grain, grain), grain)
        after = pl.ds(pl.multiple_of(rows + i * grain, grain), grain)
        values = pin[part, :] + (ys_recv[part, :].astype(f32) + ys_recv[after, :].astype(f32))
        values = values - tile_lanes(own_col[part, :], repeat) * q_ref[part, :].astype(f32)
        high = values.astype(bf16)
        zq[pl.ds(pl.multiple_of(7 * rows + i * grain, grain), grain), :] = high
        zq[pl.ds(pl.multiple_of(8 * rows + i * grain, grain), grain), :] = (
            values - high.astype(f32)
        ).astype(bf16)
        return 0

    lax.fori_loop(0, rows // grain, positive_rows, 0)

    def passage_out(i, _):
        part = pl.ds(pl.multiple_of(i * rows, rows), rows)
        scale = pcol[part, :]
        shares = (along_p_mine[part, :] + along_p_peer[part, :]) * scale
        shares = shares + wt[part, 7 * rows : 8 * rows].astype(f32) * own_along
        along = jnp.sum(shares, axis=1, keepdims=True)
        along = jnp.broadcast_to(along, (rows, lanes)) * scale
        for c in range(width // wide):
            columns = slice(c * wide, (c + 1) * wide)
            values = dp_acc[part, columns] + dot_nn(
                wt[part, 7 * rows : 9 * rows], zq[7 * rows : 9 * rows, columns]
            )
            dp_ref[part, columns] = (
                (values - p_ref[part, columns].astype(f32) * tile_lanes(along, wide // lanes))
                * tile_lanes(scale, wide // lanes)
            ).astype(bf16)
        return 0

    lax.fori_loop(0, tiles // 2, passage_out, 0)
    send_back(1, 0, quarter, True, came=(2, 0))
    send_back(1, half, quarter, False, came=(2, half))
    lax.fori_loop(tiles // 2, tiles, passage_out, 0)
    send_back(1, quarter, quarter, True, came=(2, quarter))
    send_back(1, half + quarter, quarter, False, came=(2, half + quarter))
    wait_came("loss_y", loss_y.at[pl.ds(0, 3)])
    value = loss_y[0]
    for k in range(1, side):
        value = value + loss_y[k]
    queries = rows * owners * side * side
    mean = jnp.sum(value[0:1, :], axis=1, keepdims=True) * (1.0 / queries)
    loss_ref[...] = jnp.broadcast_to(mean, (8, lanes))
    wait_sent("loss_z", loss_z.at[pl.ds(0, 7)])
    wait_sent("loss_x", loss_x.at[pl.ds(0, 3)])
    wait_sent("loss_y", loss_y.at[pl.ds(0, 3)])
    wait_sent("along", along_p_mine)
    wait_sent("back_y", ys_send)

    def query_out(first):
        def body(i, _):
            part = pl.ds(pl.multiple_of(first + i * grain, grain), grain)
            before = pl.ds(pl.multiple_of(place(1, True, first) + i * grain, grain), grain)
            after = pl.ds(pl.multiple_of(place(1, False, first) + i * grain, grain), grain)
            back = zs_recv[before, :].astype(f32) + zs_recv[after, :].astype(f32)
            dq_ref[part, :] = (
                dq_acc[part, :] + back * tile_lanes(ratio_col[part, :], repeat)
            ).astype(bf16)
            return 0

        lax.fori_loop(0, quarter // grain, body, 0)

    back_right[1, half].wait_recv()
    back_left[1, 0].wait_recv()
    for start in (0, quarter):
        back_right[1, start].wait_recv()
        query_out(start)
        back_left[1, half + start].wait_recv()
        query_out(half + start)
    wait_sent("back_z", zs_send)


def flush(loss_ref, dq_ref, dp_ref, loss_out, dq_out, dp_out, one, sems):
    copies = [
        pltpu.make_async_copy(dp_ref, dp_out, sems.at[0]),
        pltpu.make_async_copy(dq_ref, dq_out, sems.at[1]),
    ]
    for copy in copies:
        copy.start()
    one[...] = loss_ref[0:1, 0:1]
    copies.append(pltpu.make_async_copy(one, loss_out, sems.at[2]))
    copies[2].start()
    for copy in copies:
        copy.wait()


def on_device(queries, passages, positive_slot, hard_offset, hard_slot):
    rows, width = queries.shape
    p_rows = passages.shape[0]
    vmem = pl.BlockSpec(memory_space=pltpu.VMEM)
    hbm = pl.BlockSpec(memory_space=pltpu.HBM)

    def f(*shape):
        return pltpu.VMEM(shape, f32)

    def b(*shape):
        return pltpu.VMEM(shape, bf16)

    loss, query_grad, passage_grad = pl.pallas_call(
        kernel,
        out_shape=(
            pltpu.VMEM((8, lanes), f32),
            pltpu.VMEM(queries.shape, bf16),
            pltpu.VMEM(passages.shape, bf16),
        ),
        in_specs=[vmem, vmem, vmem, hbm, hbm],
        out_specs=(vmem, vmem, vmem),
        scratch_shapes=[
            b(p_rows, width),
            b(9 * rows, width),
            f(7, p_rows, rows),
            f(7, p_rows, rows),
            f(p_rows, 7 * rows),
            b(7 * rows, p_rows),
            b(7 * rows, width),
            b(7 * rows, width),
            f(5 * rows, width),
            b(4 * rows, width),
            b(4 * rows, width),
            f(4 * rows, 4 * rows),
            f(4 * rows, 4 * rows),
            f(4 * rows, 4 * rows),
            f(4 * rows, 4 * rows),
            b(4 * rows, 4 * rows),
            f(4 * rows, width),
            b(3 * rows, width),
            b(3 * rows, width),
            b(3 * rows, width),
            b(3 * rows, width),
            f(rows, width),
            f(p_rows, width),
            b(p_rows, 9 * rows),
            b(rows, p_rows),
            f(p_rows + rows, lanes),
            f(p_rows + rows, lanes),
            f(p_rows, lanes),
            f(rows, lanes),
            f(4 * rows, lanes),
            f(8, lanes),
            f(7, 8, lanes),
            f(3, 8, lanes),
            f(8, lanes),
            f(3, 8, lanes),
            f(10, 8, lanes),
            f(7, 8, lanes),
            f(3, 8, lanes),
            f(8, lanes),
            f(7, 8, lanes),
            f(3, 8, lanes),
            f(3, 8, lanes),
            f(3, 8, lanes),
            f(8, 8, lanes),
            f(4, 8, lanes),
            f(4, 8, lanes),
            f(p_rows, lanes),
            f(p_rows, lanes),
            f(rows, lanes),
            f(rows, lanes),
            f(rows, lanes),
            f(rows, lanes),
            pltpu.SemaphoreType.DMA((len(kinds),)),
            pltpu.SemaphoreType.DMA((len(shared) + alone,)),
            pltpu.SemaphoreType.DMA((2,)),
        ],
        compiler_params=pltpu.CompilerParams(
            collective_id=0, has_side_effects=True, vmem_limit_bytes=58 * 1024 * 1024
        ),
        cost_estimate=pl.CostEstimate(
            flops=15_000_000_000, bytes_accessed=6_000_000, transcendentals=800_000
        ),
    )(positive_slot.reshape(1, rows), hard_offset.T, hard_slot.T, queries, passages)
    loss, query_grad, passage_grad = pl.pallas_call(
        flush,
        out_shape=(
            jax.ShapeDtypeStruct((1, 1), f32),
            jax.ShapeDtypeStruct(queries.shape, bf16),
            jax.ShapeDtypeStruct(passages.shape, bf16),
        ),
        in_specs=[vmem, vmem, vmem],
        out_specs=(hbm, hbm, hbm),
        scratch_shapes=[f(1, 1), pltpu.SemaphoreType.DMA((3,))],
        compiler_params=pltpu.CompilerParams(vmem_limit_bytes=1024 * 1024),
    )(
        pltpu.with_memory_space_constraint(loss, pltpu.VMEM),
        pltpu.with_memory_space_constraint(query_grad, pltpu.VMEM),
        pltpu.with_memory_space_constraint(passage_grad, pltpu.VMEM),
    )
    return loss[0, 0], query_grad, passage_grad


def solution(mesh):
    in_specs = (
        P(("group", "index"), "tensor"),
        P(("group", "index"), "tensor"),
        P(("group", "index")),
        P(("group", "index"), None),
        P(("group", "index"), None),
    )
    out_specs = (P(), P(("group", "index"), "tensor"), P(("group", "index"), "tensor"))
    return jax.shard_map(
        on_device, mesh=mesh, in_specs=in_specs, out_specs=out_specs, check_vma=False
    )
```

```python
import jax
import jax.numpy as jnp
from jax import lax
from jax.experimental import pallas as pl
from jax.experimental.pallas import tpu as pltpu
from jax.sharding import PartitionSpec as P

epsilon = 1e-06
inverse_temp = 50.0
side = 4
lanes = 128
shared = ("aux_z", "aux_x", "aux_y", "sum_z", "sum_x", "fac_z", "fac_x", "own")
shared = shared + ("loss_z", "loss_x", "loss_y")
kinds = shared + ("z", "x", "y", "back_z", "back_x", "back_y", "norm", "hard", "in", "along")
alone = 61
f32 = jnp.float32
bf16 = jnp.bfloat16


def dot_nt(a, b):
    return lax.dot_general(a, b, (((1,), (1,)), ((), ())), preferred_element_type=f32)


def dot_nn(a, b):
    return jnp.dot(a, b, preferred_element_type=f32)


def tile_lanes(values, count):
    return jnp.concatenate([values] * count, axis=1)


def fold_lanes(values):
    total = values[:, :lanes]
    for k in range(1, values.shape[1] // lanes):
        total = total + values[:, k * lanes : (k + 1) * lanes]
    return total


def to_column(row):
    return jnp.transpose(jnp.broadcast_to(row, (lanes, lanes)))


def kernel(
    slot_ref,
    offset_ref,
    hard_slot_ref,
    q_hbm,
    p_hbm,
    loss_ref,
    dq_ref,
    dp_ref,
    p_ref,
    zq,
    sh_mine,
    sh_peer,
    eh_t,
    eh,
    zs_send,
    zs_recv,
    pq,
    xq,
    yp,
    si_mine,
    si_peer,
    ein_t,
    ein_s,
    ein,
    pin,
    xs_send,
    xs_recv,
    ys_send,
    ys_recv,
    dq_acc,
    dp_acc,
    wt,
    pick,
    norm_mine,
    norm_peer,
    pcol,
    qcol,
    ccol,
    aux_own,
    aux_z,
    aux_x,
    pos_own,
    aux_y,
    sum_out,
    sum_z,
    sum_x,
    fac_row,
    fac_own,
    fac_z,
    fac_x,
    own_out,
    own_y,
    loss_z,
    loss_x,
    loss_y,
    along_p_mine,
    along_p_peer,
    own_col,
    rest_col,
    ratio_col,
    along_col,
    send_sems,
    recv_sems,
    load_sems,
):
    rows, width = q_hbm.shape
    p_rows = p_ref.shape[0]
    half = rows // 2
    tiles = p_rows // rows
    group = lax.axis_index("group")
    z = lax.axis_index("index")
    t = lax.axis_index("tensor")
    y = lax.div(group, side)
    x = lax.rem(group, side)
    owners = lax.axis_size("index")

    def at_z(k):
        return (group, lax.rem(z + k + owners, owners), t)

    def at_x(k):
        return (y * side + lax.rem(x + k + side, side), z, t)

    def at_y(k):
        return (lax.rem(y + k + side, side) * side + x, z, t)

    other = (group, z, 1 - t)

    received = []

    def send(src, dst, target, kind, together=False):
        if not together:
            received.append(kind)
        slot = kinds.index(kind) if together else len(shared) + len(received) - 1
        copy = pltpu.make_async_remote_copy(
            src_ref=src,
            dst_ref=dst,
            send_sem=send_sems.at[kinds.index(kind)],
            recv_sem=recv_sems.at[slot],
            device_id=target,
            device_id_type=pl.DeviceIdType.MESH,
        )
        copy.start()
        return copy

    def wait_sent(kind, ref):
        pltpu.make_async_copy(ref, ref, send_sems.at[kinds.index(kind)]).wait()

    def wait_came(kind, ref):
        pltpu.make_async_copy(ref, ref, recv_sems.at[kinds.index(kind)]).wait()

    def rows_of(slot, part=None):
        if part is None:
            return pl.ds(slot * rows, rows)
        return pl.ds(slot * rows + part * half, half)

    far = 6

    def place(k, before, start):
        if k == 4:
            return far * rows + start
        return (2 * (k - 1) + int((start < half) != before)) * rows + start

    first_lanes = lax.broadcasted_iota(jnp.int32, (1, lanes), 1) < half

    def of_tile(tile, pair):
        if tile == far:
            return pair(far)
        block = tile - tile % 2
        low, high = (block, block + 1) if tile == block else (block + 1, block)
        return jnp.where(first_lanes, pair(low), pair(high))

    z_targets = [at_z(1), at_z(-1), at_z(2), at_z(-2), at_z(3), at_z(-3), at_z(4)]
    z_homes = [at_z(-1), at_z(1), at_z(-2), at_z(2), at_z(-3), at_z(3), at_z(4)]
    x_targets = [at_x(1), at_x(-1), at_x(2)]
    x_homes = [at_x(-1), at_x(1), at_x(2)]
    y_targets = [at_y(1), at_y(-1), at_y(2)]
    y_homes = [at_y(-1), at_y(1), at_y(2)]

    load_q = pltpu.make_async_copy(q_hbm, xq.at[rows_of(0)], load_sems.at[0])
    load_p = pltpu.make_async_copy(p_hbm, p_ref, load_sems.at[1])
    load_q.start()
    load_p.start()

    barrier = pltpu.get_barrier_semaphore()
    peers = z_targets + x_targets + y_targets + [other]
    for peer in peers:
        pl.semaphore_signal(barrier, inc=1, device_id=peer, device_id_type=pl.DeviceIdType.MESH)
    pl.semaphore_wait(barrier, len(peers))

    def z_rows(k, before, c):
        return pl.ds(place(k, before, c * half), half)

    z_right = {}
    z_left = {}
    for c in range(2):
        right_own = q_hbm.at[pl.ds(c * half, half)]
        left_own = q_hbm.at[pl.ds((1 - c) * half, half)]
        z_right[1, c] = send(right_own, zq.at[z_rows(1, True, c)], at_z(1), "z")
        z_left[1, 1 - c] = send(left_own, zq.at[z_rows(1, False, 1 - c)], at_z(-1), "z")
    x_right = send(q_hbm, xq.at[rows_of(1)], at_x(1), "x")
    x_left = send(q_hbm, xq.at[rows_of(2)], at_x(-1), "x")
    load_q.wait()
    load_p.wait()
    q_ref = xq

    slots = slot_ref[0:1, :]
    for i in range(tiles):
        ids = lax.broadcasted_iota(jnp.int32, (rows, lanes), 0) + i * rows
        chosen = jnp.where(ids == slots, 1.0, 0.0).astype(f32)
        pick[:, i * rows : (i + 1) * rows] = jnp.transpose(chosen).astype(bf16)
        wt[i * rows : (i + 1) * rows, 7 * rows : 8 * rows] = chosen.astype(bf16)
        wt[i * rows : (i + 1) * rows, 8 * rows : 9 * rows] = chosen.astype(bf16)

    wide = 512

    def pick_columns(i, _):
        columns = pl.ds(pl.multiple_of(i * wide, wide), wide)
        yp[0:rows, columns] = dot_nn(pick[...], p_ref[:, columns]).astype(bf16)
        return 0

    lax.fori_loop(0, width // wide, pick_columns, 0)
    y_right = send(yp.at[rows_of(0)], yp.at[rows_of(1)], at_y(1), "y")
    y_left = send(yp.at[rows_of(0)], yp.at[rows_of(2)], at_y(-1), "y")

    strip = 32

    def square_strip(source, base):
        def body(i, _):
            part = pl.ds(pl.multiple_of(i * strip, strip), strip)
            values = source[part, :].astype(f32)
            norm_mine[pl.ds(pl.multiple_of(base + i * strip, strip), strip), :] = fold_lanes(
                values * values
            )
            return 0

        return body

    lax.fori_loop(0, p_rows // strip, square_strip(p_ref, 0), 0)
    lax.fori_loop(0, rows // strip, square_strip(q_ref, p_rows), 0)
    norm_copy = send(norm_mine, norm_peer, other, "norm")
    norm_copy.wait_recv()

    def scale_of(start):
        squares = norm_mine[start : start + rows, :] + norm_peer[start : start + rows, :]
        total = jnp.sum(squares, axis=1, keepdims=True)
        return jnp.broadcast_to(1.0 / jnp.sqrt(total + epsilon), (rows, lanes))

    position_row = jnp.zeros((1, lanes), f32)
    for i in range(tiles):
        scale = scale_of(i * rows)
        pcol[i * rows : (i + 1) * rows, :] = scale
        ids = lax.broadcasted_iota(jnp.int32, (rows, lanes), 0) + i * rows
        position_row = position_row + jnp.sum(
            jnp.where(ids == slots, scale, 0.0), axis=0, keepdims=True
        )
    q_scale = scale_of(p_rows)
    qcol[...] = q_scale
    q_row = jnp.transpose(q_scale)[0:1, :]
    owner_ids = lax.rem(offset_ref[...] + (z + 1), owners)
    aux_own[0:7, :] = (owner_ids * p_rows + hard_slot_ref[...]).astype(f32)
    aux_own[7:8, :] = q_row
    pos_own[...] = position_row
    for m in range(7):
        send(aux_own, aux_z.at[m], z_targets[m], "aux_z", True)
    for m in range(3):
        send(aux_own, aux_x.at[m], x_targets[m], "aux_x", True)
        send(pos_own, aux_y.at[m], y_targets[m], "aux_y", True)

    def forward_z(k, c):
        z_right[k, c].wait_recv()
        here = zq.at[z_rows(k, True, c)]
        if k < 3 or c == 0:
            z_right[k + 1, c] = send(here, zq.at[z_rows(k + 1, True, c)], at_z(1), "z")
        z_left[k, 1 - c].wait_recv()
        here = zq.at[z_rows(k, False, 1 - c)]
        if k < 3 or c == 0:
            z_left[k + 1, 1 - c] = send(here, zq.at[z_rows(k + 1, False, 1 - c)], at_z(-1), "z")

    line = lax.broadcasted_iota(jnp.int32, (2, lanes), 0)
    hard_copies = {}

    def hard_part(tile, count):
        def body(i, _):
            part = pl.ds(pl.multiple_of(i * 256, 256), 256)
            scores = dot_nt(p_ref[part, :], zq[tile * rows : (tile + count) * rows, :])
            for n in range(count):
                sh_mine[tile + n, part, :] = scores[:, n * lanes : (n + 1) * lanes]
            return 0

        lax.fori_loop(0, p_rows // 256, body, 0)
        here = pl.ds(tile, count)
        copy = send(sh_mine.at[here], sh_peer.at[here], other, "hard")
        for n in range(count):
            hard_copies[tile + n] = copy if n == 0 else None

    first_slot = (z * p_rows).astype(f32)
    hard_sums = {}

    def hard_exp(tile):
        if hard_copies[tile] is not None:
            hard_copies[tile].wait_recv()
        if tile == 0:
            wait_came("aux_z", aux_z)
        packet = of_tile(tile, lambda block: aux_z[block])
        row_scale = inverse_temp * packet[7:8, :]
        columns = slice(tile * rows, (tile + 1) * rows)

        def body(i, carry):
            sums, moments = carry
            part = pl.ds(pl.multiple_of(i * rows, rows), rows)
            ids = (
                lax.broadcasted_iota(jnp.int32, (rows, lanes), 0) + i * rows
            ).astype(f32) + first_slot
            times = jnp.zeros((rows, lanes), f32)
            for j in range(7):
                times = times + jnp.where(ids == packet[j : j + 1, :], 1.0, 0.0)
            scale = pcol[part, :]
            score = (sh_mine[tile, part, :] + sh_peer[tile, part, :]) * (scale * row_scale)
            weight = jnp.where(times > 0.0, times * jnp.exp(score), 0.0)
            eh_t[part, columns] = weight
            eh[columns, part] = jnp.transpose(weight * scale).astype(bf16)
            return (
                sums + jnp.sum(weight, axis=0, keepdims=True),
                moments + jnp.sum(weight * score, axis=0, keepdims=True),
            )

        zero = jnp.zeros((1, lanes), f32)
        sums, moments = lax.fori_loop(0, tiles, body, (zero, zero))
        hard_sums[tile] = jnp.where(line == 0, sums, moments)

    def send_hard_sum(slot):
        sum_out[slot] = of_tile(slot, lambda tile: hard_sums[tile])
        send(sum_out.at[slot], sum_z.at[slot], z_homes[slot], "sum_z", True)

    forward_z(1, 0)
    forward_z(1, 1)
    x_right.wait_recv()
    x_far_right = send(xq.at[rows_of(1, 0)], xq.at[rows_of(3, 0)], at_x(1), "x")
    x_left.wait_recv()
    x_far_left = send(xq.at[rows_of(2, 1)], xq.at[rows_of(3, 1)], at_x(-1), "x")
    y_right.wait_recv()
    y_far_right = send(yp.at[rows_of(1, 0)], yp.at[rows_of(3, 0)], at_y(1), "y")
    y_left.wait_recv()
    y_far_left = send(yp.at[rows_of(2, 1)], yp.at[rows_of(3, 1)], at_y(-1), "y")
    hard_part(0, 2)
    hard_exp(0)
    hard_exp(1)
    forward_z(2, 0)

    x_far_right.wait_recv()
    x_far_left.wait_recv()
    y_far_right.wait_recv()
    y_far_left.wait_recv()

    def in_part(i, _):
        part = pl.ds(pl.multiple_of(i * rows, rows), rows)
        si_mine[part, :] = dot_nt(yp[part, :], xq[...])
        return 0

    lax.fori_loop(0, side, in_part, 0)
    in_copy = send(si_mine, si_peer, other, "in")
    hard_part(2, 1)
    wait_came("aux_x", aux_x)
    wait_came("aux_y", aux_y)
    in_copy.wait_recv()
    in_sums = [jnp.zeros((1, lanes), f32) for _ in range(side)]
    in_moments = [jnp.zeros((1, lanes), f32) for _ in range(side)]
    own_score = None
    diagonal = lax.broadcasted_iota(jnp.int32, (rows, lanes), 0) == lax.broadcasted_iota(
        jnp.int32, (rows, lanes), 1
    )
    for c in range(side):
        c_row = position_row if c == 0 else aux_y[c - 1][0:1, :]
        scale = to_column(c_row)
        ccol[c * rows : (c + 1) * rows, :] = scale
        part = slice(c * rows, (c + 1) * rows)
        for n in range(side):
            row_scale = inverse_temp * (q_row if n == 0 else aux_x[n - 1][7:8, :])
            columns = slice(n * rows, (n + 1) * rows)
            score = (si_mine[part, columns] + si_peer[part, columns]) * (scale * row_scale)
            weight = jnp.exp(score)
            if c == 0 and n == 0:
                own_score = jnp.sum(jnp.where(diagonal, score, 0.0), axis=0, keepdims=True)
                weight = jnp.where(diagonal, 0.0, weight)
            ein_t[part, columns] = weight
            ein_s[part, columns] = weight * score
            ein[columns, part] = jnp.transpose(weight * scale).astype(bf16)
            in_sums[n] = in_sums[n] + jnp.sum(weight, axis=0, keepdims=True)
            in_moments[n] = in_moments[n] + jnp.sum(weight * score, axis=0, keepdims=True)
    for n in range(1, side):
        sum_out[6 + n] = jnp.where(line == 0, in_sums[n], in_moments[n])
        send(sum_out.at[6 + n], sum_x.at[n - 1], x_homes[n - 1], "sum_x", True)

    forward_z(2, 1)

    def in_product(start, stop, other_rows):
        def body(i, _):
            columns = pl.ds(pl.multiple_of(i * wide, wide), wide)
            pin[start:stop, columns] = dot_nn(ein[start:stop, :], other_rows[:, columns])
            return 0

        lax.fori_loop(0, width // wide, body, 0)

    in_product(3 * rows, 4 * rows, yp)

    grain = 16

    def stage(dst, dst_row, src, src_row, count, add=None, add_row=0):
        def body(i, _):
            values = src[pl.ds(pl.multiple_of(src_row + i * grain, grain), grain), :]
            if add is not None:
                values = values + add[
                    pl.ds(pl.multiple_of(add_row + i * grain, grain), grain), :
                ].astype(f32)
            dst[pl.ds(pl.multiple_of(dst_row + i * grain, grain), grain), :] = values.astype(
                dst.dtype
            )
            return 0

        lax.fori_loop(0, count // grain, body, 0)

    def square_first(send_buffer, recv_buffer, at, kind):
        stage(send_buffer, 2 * rows, pin, 3 * rows, rows)
        return (
            send(send_buffer.at[rows_of(2, 0)], recv_buffer.at[rows_of(2, 0)], at(1), kind),
            send(send_buffer.at[rows_of(2, 1)], recv_buffer.at[rows_of(2, 1)], at(-1), kind),
        )

    def square_free(send_buffer, recv_buffer, at, kind):
        stage(send_buffer, 0, pin, rows, half)
        before = send(send_buffer.at[rows_of(0, 0)], recv_buffer.at[rows_of(0, 0)], at(-1), kind)
        stage(send_buffer, rows + half, pin, 2 * rows + half, half)
        after = send(send_buffer.at[rows_of(1, 1)], recv_buffer.at[rows_of(1, 1)], at(1), kind)
        return [before, after]

    def square_last(first, send_buffer, recv_buffer, at, kind):
        first[0].wait_recv()
        stage(send_buffer, rows, pin, 2 * rows, half, recv_buffer, 2 * rows)
        after = send(send_buffer.at[rows_of(1, 0)], recv_buffer.at[rows_of(1, 0)], at(1), kind)
        first[1].wait_recv()
        stage(send_buffer, half, pin, rows + half, half, recv_buffer, 2 * rows + half)
        before = send(send_buffer.at[rows_of(0, 1)], recv_buffer.at[rows_of(0, 1)], at(-1), kind)
        return [before, after]

    x_first = square_first(xs_send, xs_recv, at_x, "back_x")
    hard_part(3, 1)
    in_product(0, 3 * rows, yp)
    x_second = square_free(xs_send, xs_recv, at_x, "back_x")
    hard_exp(2)
    forward_z(3, 0)
    hard_part(4, 1)
    hard_exp(3)
    hard_exp(4)

    def hard_query(slot, count, base):
        def body(i, _):
            columns = pl.ds(pl.multiple_of(i * wide, wide), wide)
            pq[base : base + count * rows, columns] = dot_nn(
                eh[slot * rows : (slot + count) * rows, :], p_ref[:, columns]
            )
            return 0

        lax.fori_loop(0, width // wide, body, 0)

    back_right = {}
    back_left = {}

    pq_base = {3: 0, 2: 2 * rows, 1: 0, 4: 4 * rows}

    def stage_back(k, start, count, right, came=None, wait=True):
        first = place(k, not right, start)
        base = first - 2 * (k - 1) * rows + pq_base[k]
        if came is None:
            stage(zs_send, first, pq, base, count)
        else:
            if wait:
                (back_right if right else back_left)[came].wait_recv()
            stage(zs_send, first, pq, base, count, zs_recv, place(k + 1, not right, start))

    def start_back(k, start, count, right):
        here = pl.ds(place(k, not right, start), count)
        (back_right if right else back_left)[k, start] = send(
            zs_send.at[here], zs_recv.at[here], at_z(1 if right else -1), "back_z"
        )

    def send_back(k, start, count, right, came=None, wait=True):
        stage_back(k, start, count, right, came, wait)
        start_back(k, start, count, right)

    hard_query(4, 1, 0)
    stage_back(3, half, half, True)
    stage_back(3, 0, half, False)
    x_second += square_last(x_first, xs_send, xs_recv, at_x, "back_x")
    forward_z(3, 1)
    hard_part(5, 1)
    start_back(3, half, half, True)
    start_back(3, 0, half, False)
    hard_exp(5)
    for slot in range(6):
        send_hard_sum(slot)
    z_right[4, 0].wait_recv()
    z_left[4, 1].wait_recv()
    hard_part(far, 1)
    hard_query(5, 1, rows)
    hard_exp(far)
    send_hard_sum(far)
    hard_query(far, 1, 4 * rows)
    send_back(4, 0, half, True)
    send_back(4, half, half, False)

    rest = in_sums[0]
    moment = in_moments[0]
    wait_came("sum_x", sum_x)
    wait_came("sum_z", sum_z)
    for m in range(3):
        rest = rest + sum_x[m][0:1, :]
        moment = moment + sum_x[m][1:2, :]
    for m in range(7):
        rest = rest + sum_z[m][0:1, :]
        moment = moment + sum_z[m][1:2, :]
    total = rest + jnp.exp(own_score)
    ratio = inverse_temp / total
    factor = ratio * q_row
    inverse = 1.0 / total
    fac_row[...] = factor
    fac_own[...] = jnp.where(line == 0, factor, inverse)
    for m in range(3):
        send(fac_own, fac_x.at[m], x_targets[m], "fac_x", True)
    for m in range(7):
        send(fac_row, fac_z.at[m], z_targets[m], "fac_z", True)
    loss_z[z] = jnp.log(total) - own_score
    for k in range(1, 8):
        send(loss_z.at[z], loss_z.at[z], at_z(k), "loss_z", True)

    hard_query(2, 2, 2 * rows)

    along = (moment - rest * own_score) / total
    own_col[...] = to_column(factor * rest)
    ratio_col[...] = to_column(factor)
    rest_col[...] = to_column(factor * rest * position_row)
    along_col[...] = to_column(along * q_row * q_row)
    repeat = width // lanes

    wait_came("fac_x", fac_x)
    for n in range(side):
        near_row = factor if n == 0 else fac_x[n - 1][0:1, :]
        columns = slice(n * rows, (n + 1) * rows)
        for c in range(side):
            part = slice(c * rows, (c + 1) * rows)
            ein[part, columns] = (ein_t[part, columns] * near_row).astype(bf16)

    in_product(3 * rows, 4 * rows, xq)
    y_first = square_first(ys_send, ys_recv, at_y, "back_y")
    send_back(2, half, half, True, came=(3, half))
    send_back(2, 0, half, False, came=(3, 0))
    in_product(rows, 3 * rows, xq)
    y_second = square_free(ys_send, ys_recv, at_y, "back_y")

    for copy in x_second:
        copy.wait_recv()

    def gather_x(i, _):
        part = pl.ds(pl.multiple_of(i * grain, grain), grain)
        after = pl.ds(pl.multiple_of(rows + i * grain, grain), grain)
        values = pin[part, :] + (
            xs_recv[part, :].astype(f32) + xs_recv[after, :].astype(f32)
        )
        dq_acc[part, :] = (
            values * tile_lanes(ratio_col[part, :], repeat)
            - yp[part, :].astype(f32) * tile_lanes(rest_col[part, :], repeat)
            - q_ref[part, :].astype(f32) * tile_lanes(along_col[part, :], repeat)
        )
        return 0

    lax.fori_loop(0, rows // grain, gather_x, 0)

    in_product(0, rows, xq)

    own_along = None
    for c in range(side):
        part = slice(c * rows, (c + 1) * rows)
        shares = jnp.zeros((rows, lanes), f32)
        for n in range(side):
            inverse_row = inverse if n == 0 else fac_x[n - 1][1:2, :]
            shares = shares + ein_s[part, n * rows : (n + 1) * rows] * inverse_row
        row = jnp.sum(jnp.transpose(shares), axis=0, keepdims=True)
        if c == 0:
            own_along = row - rest * own_score * inverse
        else:
            own_out[c - 1] = row
            send(own_out.at[c - 1], own_y.at[c - 1], y_homes[c - 1], "own", True)
    send_back(3, 0, half, True, came=(4, 0))
    send_back(3, half, half, False, came=(4, half))
    hard_query(0, 2, 0)

    wait_came("fac_z", fac_z)
    for m in range(7):
        columns = slice(m * rows, (m + 1) * rows)
        tile_row = of_tile(m, lambda block: fac_z[block])
        for c in range(tiles):
            part = slice(c * rows, (c + 1) * rows)
            wt[part, columns] = (eh_t[part, columns] * tile_row).astype(bf16)

    y_second += square_last(y_first, ys_send, ys_recv, at_y, "back_y")
    send_back(1, half, half, True, came=(2, half))
    send_back(1, 0, half, False, came=(2, 0))

    def passage_hard(i, _):
        columns = pl.ds(pl.multiple_of(i * 256, 256), 256)
        dp_acc[:, columns] = dot_nn(wt[:, 0 : 7 * rows], zq[0 : 7 * rows, columns])
        return 0

    lax.fori_loop(0, width // 256, passage_hard, 0)
    wait_sent("z", zq.at[pl.ds(0, 7 * rows)])
    wait_sent("x", xq.at[pl.ds(0, 3 * rows)])
    wait_sent("y", yp.at[pl.ds(0, 3 * rows)])
    wait_sent("back_x", xs_send)
    wait_sent("norm", norm_mine)
    wait_sent("hard", sh_mine)
    wait_sent("in", si_mine)
    wait_sent("aux_z", aux_z)
    wait_sent("aux_x", aux_x)
    wait_sent("aux_y", aux_y)
    wait_sent("sum_z", sum_z)
    wait_sent("sum_x", sum_x)
    wait_sent("fac_z", fac_z)
    wait_sent("fac_x", fac_x)
    wait_sent("own", own_y)

    def passage_along(i, _):
        part = pl.ds(pl.multiple_of(i * grain, grain), grain)
        along_p_mine[part, :] = fold_lanes(dp_acc[part, :] * p_ref[part, :].astype(f32))
        return 0

    lax.fori_loop(0, p_rows // grain, passage_along, 0)
    along_p_copy = send(along_p_mine, along_p_peer, other, "along")
    quarter = half // 2
    for start in (0, quarter):
        send_back(2, start, quarter, True, came=(3, 0), wait=start == 0)
        send_back(2, half + start, quarter, False, came=(3, half), wait=start == 0)

    wait_came("loss_z", loss_z.at[pl.ds(0, 7)])
    value = loss_z[0]
    for k in range(1, 8):
        value = value + loss_z[k]
    loss_x[x] = value
    for k in range(1, side):
        send(loss_x.at[x], loss_x.at[x], at_x(k), "loss_x", True)
    wait_came("loss_x", loss_x.at[pl.ds(0, 3)])
    value = loss_x[0]
    for k in range(1, side):
        value = value + loss_x[k]
    loss_y[y] = value
    for k in range(1, side):
        send(loss_y.at[y], loss_y.at[y], at_y(k), "loss_y", True)

    wait_came("own", own_y)
    for m in range(3):
        own_along = own_along + own_y[m][0:1, :]
    along_p_copy.wait_recv()
    for copy in y_second:
        copy.wait_recv()

    def positive_rows(i, _):
        part = pl.ds(pl.multiple_of(i * grain, grain), grain)
        after = pl.ds(pl.multiple_of(rows + i * grain, grain), grain)
        values = pin[part, :] + (ys_recv[part, :].astype(f32) + ys_recv[after, :].astype(f32))
        values = values - tile_lanes(own_col[part, :], repeat) * q_ref[part, :].astype(f32)
        high = values.astype(bf16)
        zq[pl.ds(pl.multiple_of(7 * rows + i * grain, grain), grain), :] = high
        zq[pl.ds(pl.multiple_of(8 * rows + i * grain, grain), grain), :] = (
            values - high.astype(f32)
        ).astype(bf16)
        return 0

    lax.fori_loop(0, rows // grain, positive_rows, 0)

    def passage_out(i, _):
        part = pl.ds(pl.multiple_of(i * rows, rows), rows)
        scale = pcol[part, :]
        shares = (along_p_mine[part, :] + along_p_peer[part, :]) * scale
        shares = shares + wt[part, 7 * rows : 8 * rows].astype(f32) * own_along
        along = jnp.sum(shares, axis=1, keepdims=True)
        along = jnp.broadcast_to(along, (rows, lanes)) * scale
        for c in range(width // wide):
            columns = slice(c * wide, (c + 1) * wide)
            values = dp_acc[part, columns] + dot_nn(
                wt[part, 7 * rows : 9 * rows], zq[7 * rows : 9 * rows, columns]
            )
            dp_ref[part, columns] = (
                (values - p_ref[part, columns].astype(f32) * tile_lanes(along, wide // lanes))
                * tile_lanes(scale, wide // lanes)
            ).astype(bf16)
        return 0

    lax.fori_loop(0, tiles // 2, passage_out, 0)
    send_back(1, 0, quarter, True, came=(2, 0))
    send_back(1, half, quarter, False, came=(2, half))
    lax.fori_loop(tiles // 2, tiles, passage_out, 0)
    send_back(1, quarter, quarter, True, came=(2, quarter))
    send_back(1, half + quarter, quarter, False, came=(2, half + quarter))
    wait_came("loss_y", loss_y.at[pl.ds(0, 3)])
    value = loss_y[0]
    for k in range(1, side):
        value = value + loss_y[k]
    queries = rows * owners * side * side
    mean = jnp.sum(value[0:1, :], axis=1, keepdims=True) * (1.0 / queries)
    loss_ref[...] = jnp.broadcast_to(mean, (8, lanes))
    wait_sent("loss_z", loss_z.at[pl.ds(0, 7)])
    wait_sent("loss_x", loss_x.at[pl.ds(0, 3)])
    wait_sent("loss_y", loss_y.at[pl.ds(0, 3)])
    wait_sent("along", along_p_mine)
    wait_sent("back_y", ys_send)

    def query_out(first):
        def body(i, _):
            part = pl.ds(pl.multiple_of(first + i * grain, grain), grain)
            before = pl.ds(pl.multiple_of(place(1, True, first) + i * grain, grain), grain)
            after = pl.ds(pl.multiple_of(place(1, False, first) + i * grain, grain), grain)
            back = zs_recv[before, :].astype(f32) + zs_recv[after, :].astype(f32)
            dq_ref[part, :] = (
                dq_acc[part, :] + back * tile_lanes(ratio_col[part, :], repeat)
            ).astype(bf16)
            return 0

        lax.fori_loop(0, quarter // grain, body, 0)

    back_right[1, half].wait_recv()
    back_left[1, 0].wait_recv()
    for start in (0, quarter):
        back_right[1, start].wait_recv()
        query_out(start)
        back_left[1, half + start].wait_recv()
        query_out(half + start)
    wait_sent("back_z", zs_send)


def flush(loss_ref, dq_ref, dp_ref, loss_out, dq_out, dp_out, one, sems):
    copies = [
        pltpu.make_async_copy(dp_ref, dp_out, sems.at[0]),
        pltpu.make_async_copy(dq_ref, dq_out, sems.at[1]),
    ]
    for copy in copies:
        copy.start()
    one[...] = loss_ref[0:1, 0:1]
    copies.append(pltpu.make_async_copy(one, loss_out, sems.at[2]))
    copies[2].start()
    for copy in copies:
        copy.wait()


def on_device(queries, passages, positive_slot, hard_offset, hard_slot):
    rows, width = queries.shape
    p_rows = passages.shape[0]
    vmem = pl.BlockSpec(memory_space=pltpu.VMEM)
    hbm = pl.BlockSpec(memory_space=pltpu.HBM)

    def f(*shape):
        return pltpu.VMEM(shape, f32)

    def b(*shape):
        return pltpu.VMEM(shape, bf16)

    loss, query_grad, passage_grad = pl.pallas_call(
        kernel,
        out_shape=(
            pltpu.VMEM((8, lanes), f32),
            pltpu.VMEM(queries.shape, bf16),
            pltpu.VMEM(passages.shape, bf16),
        ),
        in_specs=[vmem, vmem, vmem, hbm, hbm],
        out_specs=(vmem, vmem, vmem),
        scratch_shapes=[
            b(p_rows, width),
            b(9 * rows, width),
            f(7, p_rows, rows),
            f(7, p_rows, rows),
            f(p_rows, 7 * rows),
            b(7 * rows, p_rows),
            b(7 * rows, width),
            b(7 * rows, width),
            f(5 * rows, width),
            b(4 * rows, width),
            b(4 * rows, width),
            f(4 * rows, 4 * rows),
            f(4 * rows, 4 * rows),
            f(4 * rows, 4 * rows),
            f(4 * rows, 4 * rows),
            b(4 * rows, 4 * rows),
            f(4 * rows, width),
            b(3 * rows, width),
            b(3 * rows, width),
            b(3 * rows, width),
            b(3 * rows, width),
            f(rows, width),
            f(p_rows, width),
            b(p_rows, 9 * rows),
            b(rows, p_rows),
            f(p_rows + rows, lanes),
            f(p_rows + rows, lanes),
            f(p_rows, lanes),
            f(rows, lanes),
            f(4 * rows, lanes),
            f(8, lanes),
            f(7, 8, lanes),
            f(3, 8, lanes),
            f(1, lanes),
            f(3, 1, lanes),
            f(10, 2, lanes),
            f(7, 2, lanes),
            f(3, 2, lanes),
            f(1, lanes),
            f(2, lanes),
            f(7, 1, lanes),
            f(3, 2, lanes),
            f(3, 1, lanes),
            f(3, 1, lanes),
            f(8, 1, lanes),
            f(4, 1, lanes),
            f(4, 1, lanes),
            f(p_rows, lanes),
            f(p_rows, lanes),
            f(rows, lanes),
            f(rows, lanes),
            f(rows, lanes),
            f(rows, lanes),
            pltpu.SemaphoreType.DMA((len(kinds),)),
            pltpu.SemaphoreType.DMA((len(shared) + alone,)),
            pltpu.SemaphoreType.DMA((2,)),
        ],
        compiler_params=pltpu.CompilerParams(
            collective_id=0, has_side_effects=True, vmem_limit_bytes=58 * 1024 * 1024
        ),
        cost_estimate=pl.CostEstimate(
            flops=15_000_000_000, bytes_accessed=6_000_000, transcendentals=800_000
        ),
    )(positive_slot.reshape(1, rows), hard_offset.T, hard_slot.T, queries, passages)
    loss, query_grad, passage_grad = pl.pallas_call(
        flush,
        out_shape=(
            jax.ShapeDtypeStruct((1, 1), f32),
            jax.ShapeDtypeStruct(queries.shape, bf16),
            jax.ShapeDtypeStruct(passages.shape, bf16),
        ),
        in_specs=[vmem, vmem, vmem],
        out_specs=(hbm, hbm, hbm),
        scratch_shapes=[f(1, 1), pltpu.SemaphoreType.DMA((3,))],
        compiler_params=pltpu.CompilerParams(vmem_limit_bytes=1024 * 1024),
    )(
        pltpu.with_memory_space_constraint(loss, pltpu.VMEM),
        pltpu.with_memory_space_constraint(query_grad, pltpu.VMEM),
        pltpu.with_memory_space_constraint(passage_grad, pltpu.VMEM),
    )
    return loss[0, 0], query_grad, passage_grad


def solution(mesh):
    in_specs = (
        P(("group", "index"), "tensor"),
        P(("group", "index"), "tensor"),
        P(("group", "index")),
        P(("group", "index"), None),
        P(("group", "index"), None),
    )
    out_specs = (P(), P(("group", "index"), "tensor"), P(("group", "index"), "tensor"))
    return jax.shard_map(
        on_device, mesh=mesh, in_specs=in_specs, out_specs=out_specs, check_vma=False
    )
```

```python
import jax
import jax.numpy as jnp
from jax import lax
from jax.experimental import pallas as pl
from jax.experimental.pallas import tpu as pltpu
from jax.sharding import PartitionSpec as P

epsilon = 1e-06
inverse_temp = 50.0
side = 4
lanes = 128
shared = ("aux_z", "aux_x", "aux_y", "sum_z", "sum_x", "fac_z", "fac_x", "own")
shared = shared + ("loss_z", "loss_x", "loss_y")
kinds = shared + ("z", "x", "y", "back_z", "back_x", "back_y", "norm", "hard", "in", "along")
alone = 61
f32 = jnp.float32
bf16 = jnp.bfloat16


def dot_nt(a, b):
    return lax.dot_general(a, b, (((1,), (1,)), ((), ())), preferred_element_type=f32)


def dot_nn(a, b):
    return jnp.dot(a, b, preferred_element_type=f32)


def tile_lanes(values, count):
    return jnp.concatenate([values] * count, axis=1)


def fold_lanes(values):
    total = values[:, :lanes]
    for k in range(1, values.shape[1] // lanes):
        total = total + values[:, k * lanes : (k + 1) * lanes]
    return total


def to_column(row):
    return jnp.transpose(jnp.broadcast_to(row, (lanes, lanes)))


def kernel(
    slot_ref,
    offset_ref,
    hard_slot_ref,
    q_hbm,
    p_hbm,
    loss_ref,
    dq_ref,
    dp_ref,
    p_ref,
    zq,
    sh_mine,
    sh_peer,
    eh_t,
    eh,
    zs_send,
    zs_recv,
    pq,
    xq,
    yp,
    si_mine,
    si_peer,
    ein_t,
    ein_s,
    ein,
    pin,
    xs_send,
    xs_recv,
    ys_send,
    ys_recv,
    dq_acc,
    dp_acc,
    wt,
    pick,
    norm_mine,
    norm_peer,
    pcol,
    qcol,
    aux_own,
    aux_z,
    aux_x,
    pos_own,
    aux_y,
    sum_out,
    sum_z,
    sum_x,
    fac_row,
    fac_own,
    fac_z,
    fac_x,
    own_out,
    crow,
    own_y,
    loss_z,
    loss_x,
    loss_y,
    along_p_mine,
    along_p_peer,
    own_col,
    rest_col,
    ratio_col,
    along_col,
    send_sems,
    recv_sems,
    load_sems,
):
    rows, width = q_hbm.shape
    p_rows = p_ref.shape[0]
    half = rows // 2
    tiles = p_rows // rows
    group = lax.axis_index("group")
    z = lax.axis_index("index")
    t = lax.axis_index("tensor")
    y = lax.div(group, side)
    x = lax.rem(group, side)
    owners = lax.axis_size("index")

    def at_z(k):
        return (group, lax.rem(z + k + owners, owners), t)

    def at_x(k):
        return (y * side + lax.rem(x + k + side, side), z, t)

    def at_y(k):
        return (lax.rem(y + k + side, side) * side + x, z, t)

    other = (group, z, 1 - t)

    received = []

    def send(src, dst, target, kind, together=False):
        if not together:
            received.append(kind)
        slot = kinds.index(kind) if together else len(shared) + len(received) - 1
        copy = pltpu.make_async_remote_copy(
            src_ref=src,
            dst_ref=dst,
            send_sem=send_sems.at[kinds.index(kind)],
            recv_sem=recv_sems.at[slot],
            device_id=target,
            device_id_type=pl.DeviceIdType.MESH,
        )
        copy.start()
        return copy

    def wait_sent(kind, ref):
        pltpu.make_async_copy(ref, ref, send_sems.at[kinds.index(kind)]).wait()

    def wait_came(kind, ref):
        pltpu.make_async_copy(ref, ref, recv_sems.at[kinds.index(kind)]).wait()

    def rows_of(slot, part=None):
        if part is None:
            return pl.ds(slot * rows, rows)
        return pl.ds(slot * rows + part * half, half)

    far = 6

    def place(k, before, start):
        if k == 4:
            return far * rows + start
        return (2 * (k - 1) + int((start < half) != before)) * rows + start

    first_lanes = lax.broadcasted_iota(jnp.int32, (1, lanes), 1) < half

    def of_tile(tile, pair):
        if tile == far:
            return pair(far)
        block = tile - tile % 2
        low, high = (block, block + 1) if tile == block else (block + 1, block)
        return jnp.where(first_lanes, pair(low), pair(high))

    z_targets = [at_z(1), at_z(-1), at_z(2), at_z(-2), at_z(3), at_z(-3), at_z(4)]
    z_homes = [at_z(-1), at_z(1), at_z(-2), at_z(2), at_z(-3), at_z(3), at_z(4)]
    x_targets = [at_x(1), at_x(-1), at_x(2)]
    x_homes = [at_x(-1), at_x(1), at_x(2)]
    y_targets = [at_y(1), at_y(-1), at_y(2)]
    y_homes = [at_y(-1), at_y(1), at_y(2)]

    load_q = pltpu.make_async_copy(q_hbm, xq.at[rows_of(0)], load_sems.at[0])
    load_p = pltpu.make_async_copy(p_hbm, p_ref, load_sems.at[1])
    load_q.start()
    load_p.start()

    barrier = pltpu.get_barrier_semaphore()
    peers = z_targets + x_targets + y_targets + [other]
    for peer in peers:
        pl.semaphore_signal(barrier, inc=1, device_id=peer, device_id_type=pl.DeviceIdType.MESH)
    pl.semaphore_wait(barrier, len(peers))

    def z_rows(k, before, c):
        return pl.ds(place(k, before, c * half), half)

    z_right = {}
    z_left = {}
    for c in range(2):
        right_own = q_hbm.at[pl.ds(c * half, half)]
        left_own = q_hbm.at[pl.ds((1 - c) * half, half)]
        z_right[1, c] = send(right_own, zq.at[z_rows(1, True, c)], at_z(1), "z")
        z_left[1, 1 - c] = send(left_own, zq.at[z_rows(1, False, 1 - c)], at_z(-1), "z")
    x_right = send(q_hbm, xq.at[rows_of(1)], at_x(1), "x")
    x_left = send(q_hbm, xq.at[rows_of(2)], at_x(-1), "x")
    load_q.wait()
    load_p.wait()
    q_ref = xq

    slots = slot_ref[0:1, :]
    for i in range(tiles):
        ids = lax.broadcasted_iota(jnp.int32, (rows, lanes), 0) + i * rows
        chosen = jnp.where(ids == slots, 1.0, 0.0).astype(f32)
        pick[:, i * rows : (i + 1) * rows] = jnp.transpose(chosen).astype(bf16)
        wt[i * rows : (i + 1) * rows, 7 * rows : 8 * rows] = chosen.astype(bf16)
        wt[i * rows : (i + 1) * rows, 8 * rows : 9 * rows] = chosen.astype(bf16)

    wide = 512

    def pick_columns(i, _):
        columns = pl.ds(pl.multiple_of(i * wide, wide), wide)
        yp[0:rows, columns] = dot_nn(pick[...], p_ref[:, columns]).astype(bf16)
        return 0

    lax.fori_loop(0, width // wide, pick_columns, 0)
    y_right = send(yp.at[rows_of(0)], yp.at[rows_of(1)], at_y(1), "y")
    y_left = send(yp.at[rows_of(0)], yp.at[rows_of(2)], at_y(-1), "y")

    strip = 32

    def square_strip(source, base):
        def body(i, _):
            part = pl.ds(pl.multiple_of(i * strip, strip), strip)
            values = source[part, :].astype(f32)
            norm_mine[pl.ds(pl.multiple_of(base + i * strip, strip), strip), :] = fold_lanes(
                values * values
            )
            return 0

        return body

    lax.fori_loop(0, p_rows // strip, square_strip(p_ref, 0), 0)
    lax.fori_loop(0, rows // strip, square_strip(q_ref, p_rows), 0)
    norm_copy = send(norm_mine, norm_peer, other, "norm")
    norm_copy.wait_recv()

    def scale_of(start):
        squares = norm_mine[start : start + rows, :] + norm_peer[start : start + rows, :]
        total = jnp.sum(squares, axis=1, keepdims=True)
        return jnp.broadcast_to(1.0 / jnp.sqrt(total + epsilon), (rows, lanes))

    position_row = jnp.zeros((1, lanes), f32)
    for i in range(tiles):
        scale = scale_of(i * rows)
        pcol[i * rows : (i + 1) * rows, :] = scale
        ids = lax.broadcasted_iota(jnp.int32, (rows, lanes), 0) + i * rows
        position_row = position_row + jnp.sum(
            jnp.where(ids == slots, scale, 0.0), axis=0, keepdims=True
        )
    q_scale = scale_of(p_rows)
    qcol[...] = q_scale
    q_row = jnp.transpose(q_scale)[0:1, :]
    owner_ids = lax.rem(offset_ref[...] + (z + 1), owners)
    aux_own[0:7, :] = (owner_ids * p_rows + hard_slot_ref[...]).astype(f32)
    aux_own[7:8, :] = q_row
    pos_own[...] = position_row
    for m in range(7):
        send(aux_own, aux_z.at[m], z_targets[m], "aux_z", True)
    for m in range(3):
        send(aux_own, aux_x.at[m], x_targets[m], "aux_x", True)
        send(pos_own, aux_y.at[m], y_targets[m], "aux_y", True)

    def forward_z(k, c):
        z_right[k, c].wait_recv()
        here = zq.at[z_rows(k, True, c)]
        if k < 3 or c == 0:
            z_right[k + 1, c] = send(here, zq.at[z_rows(k + 1, True, c)], at_z(1), "z")
        z_left[k, 1 - c].wait_recv()
        here = zq.at[z_rows(k, False, 1 - c)]
        if k < 3 or c == 0:
            z_left[k + 1, 1 - c] = send(here, zq.at[z_rows(k + 1, False, 1 - c)], at_z(-1), "z")

    line = lax.broadcasted_iota(jnp.int32, (2, lanes), 0)
    hard_copies = {}

    def hard_part(tile, count):
        def body(i, _):
            part = pl.ds(pl.multiple_of(i * 256, 256), 256)
            scores = dot_nt(p_ref[part, :], zq[tile * rows : (tile + count) * rows, :])
            for n in range(count):
                sh_mine[tile + n, part, :] = scores[:, n * lanes : (n + 1) * lanes]
            return 0

        lax.fori_loop(0, p_rows // 256, body, 0)
        here = pl.ds(tile, count)
        copy = send(sh_mine.at[here], sh_peer.at[here], other, "hard")
        for n in range(count):
            hard_copies[tile + n] = copy if n == 0 else None

    first_slot = (z * p_rows).astype(f32)
    hard_sums = {}

    def hard_exp(tile):
        if hard_copies[tile] is not None:
            hard_copies[tile].wait_recv()
        if tile == 0:
            wait_came("aux_z", aux_z)
        packet = of_tile(tile, lambda block: aux_z[block])
        row_scale = inverse_temp * packet[7:8, :]
        columns = slice(tile * rows, (tile + 1) * rows)

        def body(i, carry):
            sums, moments = carry
            part = pl.ds(pl.multiple_of(i * rows, rows), rows)
            ids = (
                lax.broadcasted_iota(jnp.int32, (rows, lanes), 0) + i * rows
            ).astype(f32) + first_slot
            times = jnp.zeros((rows, lanes), f32)
            for j in range(7):
                times = times + jnp.where(ids == packet[j : j + 1, :], 1.0, 0.0)
            scale = pcol[part, :]
            score = (sh_mine[tile, part, :] + sh_peer[tile, part, :]) * (scale * row_scale)
            weight = jnp.where(times > 0.0, times * jnp.exp(score), 0.0)
            eh_t[part, columns] = weight
            eh[columns, part] = jnp.transpose(weight * scale).astype(bf16)
            return (
                sums + jnp.sum(weight, axis=0, keepdims=True),
                moments + jnp.sum(weight * score, axis=0, keepdims=True),
            )

        zero = jnp.zeros((1, lanes), f32)
        sums, moments = lax.fori_loop(0, tiles, body, (zero, zero))
        hard_sums[tile] = jnp.where(line == 0, sums, moments)

    def send_hard_sum(slot):
        sum_out[slot] = of_tile(slot, lambda tile: hard_sums[tile])
        send(sum_out.at[slot], sum_z.at[slot], z_homes[slot], "sum_z", True)

    forward_z(1, 0)
    forward_z(1, 1)
    x_right.wait_recv()
    x_far_right = send(xq.at[rows_of(1, 0)], xq.at[rows_of(3, 0)], at_x(1), "x")
    x_left.wait_recv()
    x_far_left = send(xq.at[rows_of(2, 1)], xq.at[rows_of(3, 1)], at_x(-1), "x")
    y_right.wait_recv()
    y_far_right = send(yp.at[rows_of(1, 0)], yp.at[rows_of(3, 0)], at_y(1), "y")
    y_left.wait_recv()
    y_far_left = send(yp.at[rows_of(2, 1)], yp.at[rows_of(3, 1)], at_y(-1), "y")
    hard_part(0, 2)
    hard_exp(0)
    hard_exp(1)
    forward_z(2, 0)

    x_far_right.wait_recv()
    x_far_left.wait_recv()
    y_far_right.wait_recv()
    y_far_left.wait_recv()

    def in_part(i, _):
        part = pl.ds(pl.multiple_of(i * rows, rows), rows)
        si_mine[part, :] = dot_nt(yp[part, :], xq[...])
        return 0

    lax.fori_loop(0, side, in_part, 0)
    in_copy = send(si_mine, si_peer, other, "in")
    hard_part(2, 1)
    wait_came("aux_x", aux_x)
    wait_came("aux_y", aux_y)
    in_copy.wait_recv()
    crow[0] = position_row
    for c in range(1, side):
        crow[c] = aux_y[c - 1]
    near_scale = [inverse_temp * (q_row if n == 0 else aux_x[n - 1][7:8, :]) for n in range(side)]
    ahead = lax.broadcasted_iota(jnp.int32, (rows, lanes), 0) - lax.broadcasted_iota(
        jnp.int32, (rows, lanes), 1
    )

    def in_exp(i, carry):
        sums, moments, own = carry
        scale = to_column(crow[i])
        part = pl.ds(pl.multiple_of(i * rows, rows), rows)
        own_place = ahead == i * (2 * rows)
        new_sums, new_moments = [], []
        for n in range(side):
            columns = slice(n * rows, (n + 1) * rows)
            score = (si_mine[part, columns] + si_peer[part, columns]) * (scale * near_scale[n])
            weight = jnp.exp(score)
            if n == 0:
                own = own + jnp.sum(jnp.where(own_place, score, 0.0), axis=0, keepdims=True)
                weight = jnp.where(own_place, 0.0, weight)
            moment = weight * score
            ein_t[part, columns] = weight
            ein_s[part, columns] = moment
            ein[columns, part] = jnp.transpose(weight * scale).astype(bf16)
            new_sums.append(sums[n] + jnp.sum(weight, axis=0, keepdims=True))
            new_moments.append(moments[n] + jnp.sum(moment, axis=0, keepdims=True))
        return tuple(new_sums), tuple(new_moments), own

    zeros = tuple(jnp.zeros((1, lanes), f32) for _ in range(side))
    in_sums, in_moments, own_score = lax.fori_loop(0, side, in_exp, (zeros, zeros, zeros[0]))
    for n in range(1, side):
        sum_out[6 + n] = jnp.where(line == 0, in_sums[n], in_moments[n])
        send(sum_out.at[6 + n], sum_x.at[n - 1], x_homes[n - 1], "sum_x", True)

    forward_z(2, 1)

    def in_product(start, stop, other_rows):
        def body(i, _):
            columns = pl.ds(pl.multiple_of(i * wide, wide), wide)
            pin[start:stop, columns] = dot_nn(ein[start:stop, :], other_rows[:, columns])
            return 0

        lax.fori_loop(0, width // wide, body, 0)

    in_product(3 * rows, 4 * rows, yp)

    grain = 16

    def stage(dst, dst_row, src, src_row, count, add=None, add_row=0):
        def body(i, _):
            values = src[pl.ds(pl.multiple_of(src_row + i * grain, grain), grain), :]
            if add is not None:
                values = values + add[
                    pl.ds(pl.multiple_of(add_row + i * grain, grain), grain), :
                ].astype(f32)
            dst[pl.ds(pl.multiple_of(dst_row + i * grain, grain), grain), :] = values.astype(
                dst.dtype
            )
            return 0

        lax.fori_loop(0, count // grain, body, 0)

    def square_first(send_buffer, recv_buffer, at, kind):
        stage(send_buffer, 2 * rows, pin, 3 * rows, rows)
        return (
            send(send_buffer.at[rows_of(2, 0)], recv_buffer.at[rows_of(2, 0)], at(1), kind),
            send(send_buffer.at[rows_of(2, 1)], recv_buffer.at[rows_of(2, 1)], at(-1), kind),
        )

    def square_free(send_buffer, recv_buffer, at, kind):
        stage(send_buffer, 0, pin, rows, half)
        before = send(send_buffer.at[rows_of(0, 0)], recv_buffer.at[rows_of(0, 0)], at(-1), kind)
        stage(send_buffer, rows + half, pin, 2 * rows + half, half)
        after = send(send_buffer.at[rows_of(1, 1)], recv_buffer.at[rows_of(1, 1)], at(1), kind)
        return [before, after]

    def square_last(first, send_buffer, recv_buffer, at, kind):
        first[0].wait_recv()
        stage(send_buffer, rows, pin, 2 * rows, half, recv_buffer, 2 * rows)
        after = send(send_buffer.at[rows_of(1, 0)], recv_buffer.at[rows_of(1, 0)], at(1), kind)
        first[1].wait_recv()
        stage(send_buffer, half, pin, rows + half, half, recv_buffer, 2 * rows + half)
        before = send(send_buffer.at[rows_of(0, 1)], recv_buffer.at[rows_of(0, 1)], at(-1), kind)
        return [before, after]

    x_first = square_first(xs_send, xs_recv, at_x, "back_x")
    hard_part(3, 1)
    in_product(0, 3 * rows, yp)
    x_second = square_free(xs_send, xs_recv, at_x, "back_x")
    hard_exp(2)
    forward_z(3, 0)
    hard_part(4, 1)
    hard_exp(3)
    hard_exp(4)

    def hard_query(slot, count, base):
        def body(i, _):
            columns = pl.ds(pl.multiple_of(i * wide, wide), wide)
            pq[base : base + count * rows, columns] = dot_nn(
                eh[slot * rows : (slot + count) * rows, :], p_ref[:, columns]
            )
            return 0

        lax.fori_loop(0, width // wide, body, 0)

    back_right = {}
    back_left = {}

    pq_base = {3: 0, 2: 2 * rows, 1: 0, 4: 4 * rows}

    def stage_back(k, start, count, right, came=None, wait=True):
        first = place(k, not right, start)
        base = first - 2 * (k - 1) * rows + pq_base[k]
        if came is None:
            stage(zs_send, first, pq, base, count)
        else:
            if wait:
                (back_right if right else back_left)[came].wait_recv()
            stage(zs_send, first, pq, base, count, zs_recv, place(k + 1, not right, start))

    def start_back(k, start, count, right):
        here = pl.ds(place(k, not right, start), count)
        (back_right if right else back_left)[k, start] = send(
            zs_send.at[here], zs_recv.at[here], at_z(1 if right else -1), "back_z"
        )

    def send_back(k, start, count, right, came=None, wait=True):
        stage_back(k, start, count, right, came, wait)
        start_back(k, start, count, right)

    hard_query(4, 1, 0)
    stage_back(3, half, half, True)
    stage_back(3, 0, half, False)
    x_second += square_last(x_first, xs_send, xs_recv, at_x, "back_x")
    forward_z(3, 1)
    hard_part(5, 1)
    start_back(3, half, half, True)
    start_back(3, 0, half, False)
    hard_exp(5)
    for slot in range(6):
        send_hard_sum(slot)
    z_right[4, 0].wait_recv()
    z_left[4, 1].wait_recv()
    hard_part(far, 1)
    hard_query(5, 1, rows)
    hard_exp(far)
    send_hard_sum(far)
    hard_query(far, 1, 4 * rows)
    send_back(4, 0, half, True)
    send_back(4, half, half, False)

    rest = in_sums[0]
    moment = in_moments[0]
    wait_came("sum_x", sum_x)
    wait_came("sum_z", sum_z)
    for m in range(3):
        rest = rest + sum_x[m][0:1, :]
        moment = moment + sum_x[m][1:2, :]
    for m in range(7):
        rest = rest + sum_z[m][0:1, :]
        moment = moment + sum_z[m][1:2, :]
    total = rest + jnp.exp(own_score)
    ratio = inverse_temp / total
    factor = ratio * q_row
    inverse = 1.0 / total
    fac_row[...] = factor
    fac_own[...] = jnp.where(line == 0, factor, inverse)
    for m in range(3):
        send(fac_own, fac_x.at[m], x_targets[m], "fac_x", True)
    for m in range(7):
        send(fac_row, fac_z.at[m], z_targets[m], "fac_z", True)
    loss_z[z] = jnp.log(total) - own_score
    for k in range(1, 8):
        send(loss_z.at[z], loss_z.at[z], at_z(k), "loss_z", True)

    hard_query(2, 2, 2 * rows)

    along = (moment - rest * own_score) / total
    own_col[...] = to_column(factor * rest)
    ratio_col[...] = to_column(factor)
    rest_col[...] = to_column(factor * rest * position_row)
    along_col[...] = to_column(along * q_row * q_row)
    repeat = width // lanes

    wait_came("fac_x", fac_x)
    near_rows = [factor if n == 0 else fac_x[n - 1][0:1, :] for n in range(side)]

    def in_weights(i, _):
        part = pl.ds(pl.multiple_of(i * rows, rows), rows)
        for n in range(side):
            columns = slice(n * rows, (n + 1) * rows)
            ein[part, columns] = (ein_t[part, columns] * near_rows[n]).astype(bf16)
        return 0

    lax.fori_loop(0, side, in_weights, 0)

    in_product(3 * rows, 4 * rows, xq)
    y_first = square_first(ys_send, ys_recv, at_y, "back_y")
    send_back(2, half, half, True, came=(3, half))
    send_back(2, 0, half, False, came=(3, 0))
    in_product(rows, 3 * rows, xq)
    y_second = square_free(ys_send, ys_recv, at_y, "back_y")

    for copy in x_second:
        copy.wait_recv()

    def gather_x(i, _):
        part = pl.ds(pl.multiple_of(i * grain, grain), grain)
        after = pl.ds(pl.multiple_of(rows + i * grain, grain), grain)
        values = pin[part, :] + (
            xs_recv[part, :].astype(f32) + xs_recv[after, :].astype(f32)
        )
        dq_acc[part, :] = (
            values * tile_lanes(ratio_col[part, :], repeat)
            - yp[part, :].astype(f32) * tile_lanes(rest_col[part, :], repeat)
            - q_ref[part, :].astype(f32) * tile_lanes(along_col[part, :], repeat)
        )
        return 0

    lax.fori_loop(0, rows // grain, gather_x, 0)

    in_product(0, rows, xq)

    inverse_rows = [inverse if n == 0 else fac_x[n - 1][1:2, :] for n in range(side)]

    def own_shares(i, _):
        part = pl.ds(pl.multiple_of(i * rows, rows), rows)
        shares = jnp.zeros((rows, lanes), f32)
        for n in range(side):
            shares = shares + ein_s[part, n * rows : (n + 1) * rows] * inverse_rows[n]
        own_out[i] = jnp.sum(jnp.transpose(shares), axis=0, keepdims=True)
        return 0

    lax.fori_loop(0, side, own_shares, 0)
    own_along = own_out[0] - rest * own_score * inverse
    for c in range(1, side):
        send(own_out.at[c], own_y.at[c - 1], y_homes[c - 1], "own", True)
    send_back(3, 0, half, True, came=(4, 0))
    send_back(3, half, half, False, came=(4, half))
    hard_query(0, 2, 0)

    wait_came("fac_z", fac_z)
    tile_rows = [of_tile(m, lambda block: fac_z[block]) for m in range(7)]

    def hard_weights(i, _):
        part = pl.ds(pl.multiple_of(i * rows, rows), rows)
        for m in range(7):
            columns = slice(m * rows, (m + 1) * rows)
            wt[part, columns] = (eh_t[part, columns] * tile_rows[m]).astype(bf16)
        return 0

    lax.fori_loop(0, tiles, hard_weights, 0)

    y_second += square_last(y_first, ys_send, ys_recv, at_y, "back_y")
    send_back(1, half, half, True, came=(2, half))
    send_back(1, 0, half, False, came=(2, 0))

    def passage_hard(i, _):
        columns = pl.ds(pl.multiple_of(i * 256, 256), 256)
        dp_acc[:, columns] = dot_nn(wt[:, 0 : 7 * rows], zq[0 : 7 * rows, columns])
        return 0

    lax.fori_loop(0, width // 256, passage_hard, 0)
    wait_sent("z", zq.at[pl.ds(0, 7 * rows)])
    wait_sent("x", xq.at[pl.ds(0, 3 * rows)])
    wait_sent("y", yp.at[pl.ds(0, 3 * rows)])
    wait_sent("back_x", xs_send)
    wait_sent("norm", norm_mine)
    wait_sent("hard", sh_mine)
    wait_sent("in", si_mine)
    wait_sent("aux_z", aux_z)
    wait_sent("aux_x", aux_x)
    wait_sent("aux_y", aux_y)
    wait_sent("sum_z", sum_z)
    wait_sent("sum_x", sum_x)
    wait_sent("fac_z", fac_z)
    wait_sent("fac_x", fac_x)
    wait_sent("own", own_y)

    def passage_along(i, _):
        part = pl.ds(pl.multiple_of(i * grain, grain), grain)
        along_p_mine[part, :] = fold_lanes(dp_acc[part, :] * p_ref[part, :].astype(f32))
        return 0

    lax.fori_loop(0, p_rows // grain, passage_along, 0)
    along_p_copy = send(along_p_mine, along_p_peer, other, "along")
    quarter = half // 2
    for start in (0, quarter):
        send_back(2, start, quarter, True, came=(3, 0), wait=start == 0)
        send_back(2, half + start, quarter, False, came=(3, half), wait=start == 0)

    wait_came("loss_z", loss_z.at[pl.ds(0, 7)])
    value = loss_z[0]
    for k in range(1, 8):
        value = value + loss_z[k]
    loss_x[x] = value
    for k in range(1, side):
        send(loss_x.at[x], loss_x.at[x], at_x(k), "loss_x", True)
    wait_came("loss_x", loss_x.at[pl.ds(0, 3)])
    value = loss_x[0]
    for k in range(1, side):
        value = value + loss_x[k]
    loss_y[y] = value
    for k in range(1, side):
        send(loss_y.at[y], loss_y.at[y], at_y(k), "loss_y", True)

    wait_came("own", own_y)
    for m in range(3):
        own_along = own_along + own_y[m][0:1, :]
    along_p_copy.wait_recv()
    for copy in y_second:
        copy.wait_recv()

    def positive_rows(i, _):
        part = pl.ds(pl.multiple_of(i * grain, grain), grain)
        after = pl.ds(pl.multiple_of(rows + i * grain, grain), grain)
        values = pin[part, :] + (ys_recv[part, :].astype(f32) + ys_recv[after, :].astype(f32))
        values = values - tile_lanes(own_col[part, :], repeat) * q_ref[part, :].astype(f32)
        high = values.astype(bf16)
        zq[pl.ds(pl.multiple_of(7 * rows + i * grain, grain), grain), :] = high
        zq[pl.ds(pl.multiple_of(8 * rows + i * grain, grain), grain), :] = (
            values - high.astype(f32)
        ).astype(bf16)
        return 0

    lax.fori_loop(0, rows // grain, positive_rows, 0)

    def passage_out(i, _):
        part = pl.ds(pl.multiple_of(i * rows, rows), rows)
        scale = pcol[part, :]
        shares = (along_p_mine[part, :] + along_p_peer[part, :]) * scale
        shares = shares + wt[part, 7 * rows : 8 * rows].astype(f32) * own_along
        along = jnp.sum(shares, axis=1, keepdims=True)
        along = jnp.broadcast_to(along, (rows, lanes)) * scale
        for c in range(width // wide):
            columns = slice(c * wide, (c + 1) * wide)
            values = dp_acc[part, columns] + dot_nn(
                wt[part, 7 * rows : 9 * rows], zq[7 * rows : 9 * rows, columns]
            )
            dp_ref[part, columns] = (
                (values - p_ref[part, columns].astype(f32) * tile_lanes(along, wide // lanes))
                * tile_lanes(scale, wide // lanes)
            ).astype(bf16)
        return 0

    lax.fori_loop(0, tiles // 2, passage_out, 0)
    send_back(1, 0, quarter, True, came=(2, 0))
    send_back(1, half, quarter, False, came=(2, half))
    lax.fori_loop(tiles // 2, tiles, passage_out, 0)
    send_back(1, quarter, quarter, True, came=(2, quarter))
    send_back(1, half + quarter, quarter, False, came=(2, half + quarter))
    wait_came("loss_y", loss_y.at[pl.ds(0, 3)])
    value = loss_y[0]
    for k in range(1, side):
        value = value + loss_y[k]
    queries = rows * owners * side * side
    mean = jnp.sum(value[0:1, :], axis=1, keepdims=True) * (1.0 / queries)
    loss_ref[...] = jnp.broadcast_to(mean, (8, lanes))
    wait_sent("loss_z", loss_z.at[pl.ds(0, 7)])
    wait_sent("loss_x", loss_x.at[pl.ds(0, 3)])
    wait_sent("loss_y", loss_y.at[pl.ds(0, 3)])
    wait_sent("along", along_p_mine)
    wait_sent("back_y", ys_send)

    def query_out(first):
        def body(i, _):
            part = pl.ds(pl.multiple_of(first + i * grain, grain), grain)
            before = pl.ds(pl.multiple_of(place(1, True, first) + i * grain, grain), grain)
            after = pl.ds(pl.multiple_of(place(1, False, first) + i * grain, grain), grain)
            back = zs_recv[before, :].astype(f32) + zs_recv[after, :].astype(f32)
            dq_ref[part, :] = (
                dq_acc[part, :] + back * tile_lanes(ratio_col[part, :], repeat)
            ).astype(bf16)
            return 0

        lax.fori_loop(0, quarter // grain, body, 0)

    back_right[1, half].wait_recv()
    back_left[1, 0].wait_recv()
    for start in (0, quarter):
        back_right[1, start].wait_recv()
        query_out(start)
        back_left[1, half + start].wait_recv()
        query_out(half + start)
    wait_sent("back_z", zs_send)


def flush(loss_ref, dq_ref, dp_ref, loss_out, dq_out, dp_out, one, sems):
    copies = [
        pltpu.make_async_copy(dp_ref, dp_out, sems.at[0]),
        pltpu.make_async_copy(dq_ref, dq_out, sems.at[1]),
    ]
    for copy in copies:
        copy.start()
    one[...] = loss_ref[0:1, 0:1]
    copies.append(pltpu.make_async_copy(one, loss_out, sems.at[2]))
    copies[2].start()
    for copy in copies:
        copy.wait()


def on_device(queries, passages, positive_slot, hard_offset, hard_slot):
    rows, width = queries.shape
    p_rows = passages.shape[0]
    vmem = pl.BlockSpec(memory_space=pltpu.VMEM)
    hbm = pl.BlockSpec(memory_space=pltpu.HBM)

    def f(*shape):
        return pltpu.VMEM(shape, f32)

    def b(*shape):
        return pltpu.VMEM(shape, bf16)

    loss, query_grad, passage_grad = pl.pallas_call(
        kernel,
        out_shape=(
            pltpu.VMEM((8, lanes), f32),
            pltpu.VMEM(queries.shape, bf16),
            pltpu.VMEM(passages.shape, bf16),
        ),
        in_specs=[vmem, vmem, vmem, hbm, hbm],
        out_specs=(vmem, vmem, vmem),
        scratch_shapes=[
            b(p_rows, width),
            b(9 * rows, width),
            f(7, p_rows, rows),
            f(7, p_rows, rows),
            f(p_rows, 7 * rows),
            b(7 * rows, p_rows),
            b(7 * rows, width),
            b(7 * rows, width),
            f(5 * rows, width),
            b(4 * rows, width),
            b(4 * rows, width),
            f(4 * rows, 4 * rows),
            f(4 * rows, 4 * rows),
            f(4 * rows, 4 * rows),
            f(4 * rows, 4 * rows),
            b(4 * rows, 4 * rows),
            f(4 * rows, width),
            b(3 * rows, width),
            b(3 * rows, width),
            b(3 * rows, width),
            b(3 * rows, width),
            f(rows, width),
            f(p_rows, width),
            b(p_rows, 9 * rows),
            b(rows, p_rows),
            f(p_rows + rows, lanes),
            f(p_rows + rows, lanes),
            f(p_rows, lanes),
            f(rows, lanes),
            f(8, lanes),
            f(7, 8, lanes),
            f(3, 8, lanes),
            f(1, lanes),
            f(3, 1, lanes),
            f(10, 2, lanes),
            f(7, 2, lanes),
            f(3, 2, lanes),
            f(1, lanes),
            f(2, lanes),
            f(7, 1, lanes),
            f(3, 2, lanes),
            f(4, 1, lanes),
            f(4, 1, lanes),
            f(3, 1, lanes),
            f(8, 1, lanes),
            f(4, 1, lanes),
            f(4, 1, lanes),
            f(p_rows, lanes),
            f(p_rows, lanes),
            f(rows, lanes),
            f(rows, lanes),
            f(rows, lanes),
            f(rows, lanes),
            pltpu.SemaphoreType.DMA((len(kinds),)),
            pltpu.SemaphoreType.DMA((len(shared) + alone,)),
            pltpu.SemaphoreType.DMA((2,)),
        ],
        compiler_params=pltpu.CompilerParams(
            collective_id=0, has_side_effects=True, vmem_limit_bytes=58 * 1024 * 1024
        ),
        cost_estimate=pl.CostEstimate(
            flops=15_000_000_000, bytes_accessed=6_000_000, transcendentals=800_000
        ),
    )(positive_slot.reshape(1, rows), hard_offset.T, hard_slot.T, queries, passages)
    loss, query_grad, passage_grad = pl.pallas_call(
        flush,
        out_shape=(
            jax.ShapeDtypeStruct((1, 1), f32),
            jax.ShapeDtypeStruct(queries.shape, bf16),
            jax.ShapeDtypeStruct(passages.shape, bf16),
        ),
        in_specs=[vmem, vmem, vmem],
        out_specs=(hbm, hbm, hbm),
        scratch_shapes=[f(1, 1), pltpu.SemaphoreType.DMA((3,))],
        compiler_params=pltpu.CompilerParams(vmem_limit_bytes=1024 * 1024),
    )(
        pltpu.with_memory_space_constraint(loss, pltpu.VMEM),
        pltpu.with_memory_space_constraint(query_grad, pltpu.VMEM),
        pltpu.with_memory_space_constraint(passage_grad, pltpu.VMEM),
    )
    return loss[0, 0], query_grad, passage_grad


def solution(mesh):
    in_specs = (
        P(("group", "index"), "tensor"),
        P(("group", "index"), "tensor"),
        P(("group", "index")),
        P(("group", "index"), None),
        P(("group", "index"), None),
    )
    out_specs = (P(), P(("group", "index"), "tensor"), P(("group", "index"), "tensor"))
    return jax.shard_map(
        on_device, mesh=mesh, in_specs=in_specs, out_specs=out_specs, check_vma=False
    )
```

```python
import jax
import jax.numpy as jnp
from jax import lax
from jax.experimental import pallas as pl
from jax.experimental.pallas import tpu as pltpu
from jax.sharding import PartitionSpec as P

epsilon = 1e-06
inverse_temp = 50.0
side = 4
lanes = 128
shared = ("aux_z", "aux_x", "aux_y", "sum_z", "sum_x", "fac_z", "fac_x", "own")
shared = shared + ("loss_z", "loss_x", "loss_y")
kinds = shared + ("z", "x", "y", "back_z", "back_x", "back_y", "norm", "hard", "in", "along")
alone = 61
f32 = jnp.float32
bf16 = jnp.bfloat16


def dot_nt(a, b):
    return lax.dot_general(a, b, (((1,), (1,)), ((), ())), preferred_element_type=f32)


def dot_nn(a, b):
    return jnp.dot(a, b, preferred_element_type=f32)


def tile_lanes(values, count):
    return jnp.concatenate([values] * count, axis=1)


def fold_lanes(values):
    total = values[:, :lanes]
    for k in range(1, values.shape[1] // lanes):
        total = total + values[:, k * lanes : (k + 1) * lanes]
    return total


def to_column(row):
    return jnp.transpose(jnp.broadcast_to(row, (lanes, lanes)))


def kernel(
    slot_hbm,
    offset_hbm,
    hard_slot_hbm,
    q_hbm,
    p_hbm,
    loss_ref,
    dq_ref,
    dp_ref,
    slot_ref,
    offset_ref,
    hard_slot_ref,
    p_ref,
    zq,
    sh_mine,
    sh_peer,
    eh_t,
    eh,
    zs_send,
    zs_recv,
    pq,
    xq,
    yp,
    si_mine,
    si_peer,
    ein_t,
    ein_s,
    ein,
    pin,
    xs_send,
    xs_recv,
    ys_send,
    ys_recv,
    dq_acc,
    dp_acc,
    wt,
    pick,
    norm_mine,
    norm_peer,
    pcol,
    qcol,
    aux_own,
    aux_z,
    aux_x,
    pos_own,
    aux_y,
    sum_out,
    sum_z,
    sum_x,
    fac_row,
    fac_own,
    fac_z,
    fac_x,
    own_out,
    crow,
    own_y,
    loss_z,
    loss_x,
    loss_y,
    along_p_mine,
    along_p_peer,
    own_col,
    rest_col,
    ratio_col,
    along_col,
    send_sems,
    recv_sems,
    load_sems,
):
    rows, width = q_hbm.shape
    p_rows = p_ref.shape[0]
    half = rows // 2
    tiles = p_rows // rows
    group = lax.axis_index("group")
    z = lax.axis_index("index")
    t = lax.axis_index("tensor")
    y = lax.div(group, side)
    x = lax.rem(group, side)
    owners = lax.axis_size("index")

    def at_z(k):
        return (group, lax.rem(z + k + owners, owners), t)

    def at_x(k):
        return (y * side + lax.rem(x + k + side, side), z, t)

    def at_y(k):
        return (lax.rem(y + k + side, side) * side + x, z, t)

    other = (group, z, 1 - t)

    received = []

    def send(src, dst, target, kind, together=False):
        if not together:
            received.append(kind)
        slot = kinds.index(kind) if together else len(shared) + len(received) - 1
        copy = pltpu.make_async_remote_copy(
            src_ref=src,
            dst_ref=dst,
            send_sem=send_sems.at[kinds.index(kind)],
            recv_sem=recv_sems.at[slot],
            device_id=target,
            device_id_type=pl.DeviceIdType.MESH,
        )
        copy.start()
        return copy

    def wait_sent(kind, ref):
        pltpu.make_async_copy(ref, ref, send_sems.at[kinds.index(kind)]).wait()

    def wait_came(kind, ref):
        pltpu.make_async_copy(ref, ref, recv_sems.at[kinds.index(kind)]).wait()

    def rows_of(slot, part=None):
        if part is None:
            return pl.ds(slot * rows, rows)
        return pl.ds(slot * rows + part * half, half)

    far = 6

    def place(k, before, start):
        if k == 4:
            return far * rows + start
        return (2 * (k - 1) + int((start < half) != before)) * rows + start

    first_lanes = lax.broadcasted_iota(jnp.int32, (1, lanes), 1) < half

    def of_tile(tile, pair):
        if tile == far:
            return pair(far)
        block = tile - tile % 2
        low, high = (block, block + 1) if tile == block else (block + 1, block)
        return jnp.where(first_lanes, pair(low), pair(high))

    z_targets = [at_z(1), at_z(-1), at_z(2), at_z(-2), at_z(3), at_z(-3), at_z(4)]
    z_homes = [at_z(-1), at_z(1), at_z(-2), at_z(2), at_z(-3), at_z(3), at_z(4)]
    x_targets = [at_x(1), at_x(-1), at_x(2)]
    x_homes = [at_x(-1), at_x(1), at_x(2)]
    y_targets = [at_y(1), at_y(-1), at_y(2)]
    y_homes = [at_y(-1), at_y(1), at_y(2)]

    barrier = pltpu.get_barrier_semaphore()
    peers = z_targets + x_targets + y_targets + [other]
    for peer in peers:
        pl.semaphore_signal(barrier, inc=1, device_id=peer, device_id_type=pl.DeviceIdType.MESH)
    loads = [
        pltpu.make_async_copy(src, dst, load_sems.at[i])
        for i, (src, dst) in enumerate(
            [
                (slot_hbm, slot_ref),
                (offset_hbm, offset_ref),
                (hard_slot_hbm, hard_slot_ref),
                (p_hbm, p_ref),
                (q_hbm, xq.at[rows_of(0)]),
            ]
        )
    ]
    for load in loads:
        load.start()
    pl.semaphore_wait(barrier, len(peers))

    def z_rows(k, before, c):
        return pl.ds(place(k, before, c * half), half)

    z_right = {}
    z_left = {}
    for c in range(2):
        right_own = q_hbm.at[pl.ds(c * half, half)]
        left_own = q_hbm.at[pl.ds((1 - c) * half, half)]
        z_right[1, c] = send(right_own, zq.at[z_rows(1, True, c)], at_z(1), "z")
        z_left[1, 1 - c] = send(left_own, zq.at[z_rows(1, False, 1 - c)], at_z(-1), "z")
    x_right = send(q_hbm, xq.at[rows_of(1)], at_x(1), "x")
    x_left = send(q_hbm, xq.at[rows_of(2)], at_x(-1), "x")
    for load in loads:
        load.wait()
    q_ref = xq

    slots = slot_ref[0:1, :]
    for i in range(tiles):
        ids = lax.broadcasted_iota(jnp.int32, (rows, lanes), 0) + i * rows
        chosen = jnp.where(ids == slots, 1.0, 0.0).astype(f32)
        pick[:, i * rows : (i + 1) * rows] = jnp.transpose(chosen).astype(bf16)
        wt[i * rows : (i + 1) * rows, 7 * rows : 8 * rows] = chosen.astype(bf16)
        wt[i * rows : (i + 1) * rows, 8 * rows : 9 * rows] = chosen.astype(bf16)

    wide = 512

    def pick_columns(i, _):
        columns = pl.ds(pl.multiple_of(i * wide, wide), wide)
        yp[0:rows, columns] = dot_nn(pick[...], p_ref[:, columns]).astype(bf16)
        return 0

    lax.fori_loop(0, width // wide, pick_columns, 0)
    y_right = send(yp.at[rows_of(0)], yp.at[rows_of(1)], at_y(1), "y")
    y_left = send(yp.at[rows_of(0)], yp.at[rows_of(2)], at_y(-1), "y")

    strip = 32

    def square_strip(source, base):
        def body(i, _):
            part = pl.ds(pl.multiple_of(i * strip, strip), strip)
            values = source[part, :].astype(f32)
            norm_mine[pl.ds(pl.multiple_of(base + i * strip, strip), strip), :] = fold_lanes(
                values * values
            )
            return 0

        return body

    lax.fori_loop(0, p_rows // strip, square_strip(p_ref, 0), 0)
    lax.fori_loop(0, rows // strip, square_strip(q_ref, p_rows), 0)
    norm_copy = send(norm_mine, norm_peer, other, "norm")
    norm_copy.wait_recv()

    def scale_of(start):
        squares = norm_mine[start : start + rows, :] + norm_peer[start : start + rows, :]
        total = jnp.sum(squares, axis=1, keepdims=True)
        return jnp.broadcast_to(1.0 / jnp.sqrt(total + epsilon), (rows, lanes))

    position_row = jnp.zeros((1, lanes), f32)
    for i in range(tiles):
        scale = scale_of(i * rows)
        pcol[i * rows : (i + 1) * rows, :] = scale
        ids = lax.broadcasted_iota(jnp.int32, (rows, lanes), 0) + i * rows
        position_row = position_row + jnp.sum(
            jnp.where(ids == slots, scale, 0.0), axis=0, keepdims=True
        )
    q_scale = scale_of(p_rows)
    qcol[...] = q_scale
    q_row = jnp.transpose(q_scale)[0:1, :]
    owner_ids = lax.rem(offset_ref[...] + (z + 1), owners)
    aux_own[0:7, :] = (owner_ids * p_rows + hard_slot_ref[...]).astype(f32)
    aux_own[7:8, :] = q_row
    pos_own[...] = position_row
    for m in range(7):
        send(aux_own, aux_z.at[m], z_targets[m], "aux_z", True)
    for m in range(3):
        send(aux_own, aux_x.at[m], x_targets[m], "aux_x", True)
        send(pos_own, aux_y.at[m], y_targets[m], "aux_y", True)

    def forward_z(k, c):
        z_right[k, c].wait_recv()
        here = zq.at[z_rows(k, True, c)]
        if k < 3 or c == 0:
            z_right[k + 1, c] = send(here, zq.at[z_rows(k + 1, True, c)], at_z(1), "z")
        z_left[k, 1 - c].wait_recv()
        here = zq.at[z_rows(k, False, 1 - c)]
        if k < 3 or c == 0:
            z_left[k + 1, 1 - c] = send(here, zq.at[z_rows(k + 1, False, 1 - c)], at_z(-1), "z")

    line = lax.broadcasted_iota(jnp.int32, (2, lanes), 0)
    hard_copies = {}

    def hard_part(tile, count):
        def body(i, _):
            part = pl.ds(pl.multiple_of(i * 256, 256), 256)
            scores = dot_nt(p_ref[part, :], zq[tile * rows : (tile + count) * rows, :])
            for n in range(count):
                sh_mine[tile + n, part, :] = scores[:, n * lanes : (n + 1) * lanes]
            return 0

        lax.fori_loop(0, p_rows // 256, body, 0)
        here = pl.ds(tile, count)
        copy = send(sh_mine.at[here], sh_peer.at[here], other, "hard")
        for n in range(count):
            hard_copies[tile + n] = copy if n == 0 else None

    first_slot = (z * p_rows).astype(f32)
    hard_sums = {}

    def hard_exp(tile):
        if hard_copies[tile] is not None:
            hard_copies[tile].wait_recv()
        if tile == 0:
            wait_came("aux_z", aux_z)
        packet = of_tile(tile, lambda block: aux_z[block])
        row_scale = inverse_temp * packet[7:8, :]
        columns = slice(tile * rows, (tile + 1) * rows)

        def body(i, carry):
            sums, moments = carry
            part = pl.ds(pl.multiple_of(i * rows, rows), rows)
            ids = (
                lax.broadcasted_iota(jnp.int32, (rows, lanes), 0) + i * rows
            ).astype(f32) + first_slot
            times = jnp.zeros((rows, lanes), f32)
            for j in range(7):
                times = times + jnp.where(ids == packet[j : j + 1, :], 1.0, 0.0)
            scale = pcol[part, :]
            score = (sh_mine[tile, part, :] + sh_peer[tile, part, :]) * (scale * row_scale)
            weight = jnp.where(times > 0.0, times * jnp.exp(score), 0.0)
            eh_t[part, columns] = weight
            eh[columns, part] = jnp.transpose(weight * scale).astype(bf16)
            return (
                sums + jnp.sum(weight, axis=0, keepdims=True),
                moments + jnp.sum(weight * score, axis=0, keepdims=True),
            )

        zero = jnp.zeros((1, lanes), f32)
        sums, moments = lax.fori_loop(0, tiles, body, (zero, zero))
        hard_sums[tile] = jnp.where(line == 0, sums, moments)

    def send_hard_sum(slot):
        sum_out[slot] = of_tile(slot, lambda tile: hard_sums[tile])
        send(sum_out.at[slot], sum_z.at[slot], z_homes[slot], "sum_z", True)

    forward_z(1, 0)
    forward_z(1, 1)
    x_right.wait_recv()
    x_far_right = send(xq.at[rows_of(1, 0)], xq.at[rows_of(3, 0)], at_x(1), "x")
    x_left.wait_recv()
    x_far_left = send(xq.at[rows_of(2, 1)], xq.at[rows_of(3, 1)], at_x(-1), "x")
    y_right.wait_recv()
    y_far_right = send(yp.at[rows_of(1, 0)], yp.at[rows_of(3, 0)], at_y(1), "y")
    y_left.wait_recv()
    y_far_left = send(yp.at[rows_of(2, 1)], yp.at[rows_of(3, 1)], at_y(-1), "y")
    hard_part(0, 2)
    hard_exp(0)
    hard_exp(1)
    forward_z(2, 0)

    x_far_right.wait_recv()
    x_far_left.wait_recv()
    y_far_right.wait_recv()
    y_far_left.wait_recv()

    def in_part(i, _):
        part = pl.ds(pl.multiple_of(i * rows, rows), rows)
        si_mine[part, :] = dot_nt(yp[part, :], xq[...])
        return 0

    lax.fori_loop(0, side, in_part, 0)
    in_copy = send(si_mine, si_peer, other, "in")
    hard_part(2, 1)
    wait_came("aux_x", aux_x)
    wait_came("aux_y", aux_y)
    in_copy.wait_recv()
    crow[0] = position_row
    for c in range(1, side):
        crow[c] = aux_y[c - 1]
    near_scale = [inverse_temp * (q_row if n == 0 else aux_x[n - 1][7:8, :]) for n in range(side)]
    ahead = lax.broadcasted_iota(jnp.int32, (rows, lanes), 0) - lax.broadcasted_iota(
        jnp.int32, (rows, lanes), 1
    )

    def in_exp(i, carry):
        sums, moments, own = carry
        scale = to_column(crow[i])
        part = pl.ds(pl.multiple_of(i * rows, rows), rows)
        own_place = ahead == i * (2 * rows)
        new_sums, new_moments = [], []
        for n in range(side):
            columns = slice(n * rows, (n + 1) * rows)
            score = (si_mine[part, columns] + si_peer[part, columns]) * (scale * near_scale[n])
            weight = jnp.exp(score)
            if n == 0:
                own = own + jnp.sum(jnp.where(own_place, score, 0.0), axis=0, keepdims=True)
                weight = jnp.where(own_place, 0.0, weight)
            moment = weight * score
            ein_t[part, columns] = weight
            ein_s[part, columns] = moment
            ein[columns, part] = jnp.transpose(weight * scale).astype(bf16)
            new_sums.append(sums[n] + jnp.sum(weight, axis=0, keepdims=True))
            new_moments.append(moments[n] + jnp.sum(moment, axis=0, keepdims=True))
        return tuple(new_sums), tuple(new_moments), own

    zeros = tuple(jnp.zeros((1, lanes), f32) for _ in range(side))
    in_sums, in_moments, own_score = lax.fori_loop(0, side, in_exp, (zeros, zeros, zeros[0]))
    for n in range(1, side):
        sum_out[6 + n] = jnp.where(line == 0, in_sums[n], in_moments[n])
        send(sum_out.at[6 + n], sum_x.at[n - 1], x_homes[n - 1], "sum_x", True)

    forward_z(2, 1)

    def in_product(start, stop, other_rows):
        def body(i, _):
            columns = pl.ds(pl.multiple_of(i * wide, wide), wide)
            pin[start:stop, columns] = dot_nn(ein[start:stop, :], other_rows[:, columns])
            return 0

        lax.fori_loop(0, width // wide, body, 0)

    in_product(3 * rows, 4 * rows, yp)

    grain = 16

    def stage(dst, dst_row, src, src_row, count, add=None, add_row=0):
        def body(i, _):
            values = src[pl.ds(pl.multiple_of(src_row + i * grain, grain), grain), :]
            if add is not None:
                values = values + add[
                    pl.ds(pl.multiple_of(add_row + i * grain, grain), grain), :
                ].astype(f32)
            dst[pl.ds(pl.multiple_of(dst_row + i * grain, grain), grain), :] = values.astype(
                dst.dtype
            )
            return 0

        lax.fori_loop(0, count // grain, body, 0)

    def square_first(send_buffer, recv_buffer, at, kind):
        stage(send_buffer, 2 * rows, pin, 3 * rows, rows)
        return (
            send(send_buffer.at[rows_of(2, 0)], recv_buffer.at[rows_of(2, 0)], at(1), kind),
            send(send_buffer.at[rows_of(2, 1)], recv_buffer.at[rows_of(2, 1)], at(-1), kind),
        )

    def square_free(send_buffer, recv_buffer, at, kind):
        stage(send_buffer, 0, pin, rows, half)
        before = send(send_buffer.at[rows_of(0, 0)], recv_buffer.at[rows_of(0, 0)], at(-1), kind)
        stage(send_buffer, rows + half, pin, 2 * rows + half, half)
        after = send(send_buffer.at[rows_of(1, 1)], recv_buffer.at[rows_of(1, 1)], at(1), kind)
        return [before, after]

    def square_last(first, send_buffer, recv_buffer, at, kind):
        first[0].wait_recv()
        stage(send_buffer, rows, pin, 2 * rows, half, recv_buffer, 2 * rows)
        after = send(send_buffer.at[rows_of(1, 0)], recv_buffer.at[rows_of(1, 0)], at(1), kind)
        first[1].wait_recv()
        stage(send_buffer, half, pin, rows + half, half, recv_buffer, 2 * rows + half)
        before = send(send_buffer.at[rows_of(0, 1)], recv_buffer.at[rows_of(0, 1)], at(-1), kind)
        return [before, after]

    x_first = square_first(xs_send, xs_recv, at_x, "back_x")
    hard_part(3, 1)
    in_product(0, 3 * rows, yp)
    x_second = square_free(xs_send, xs_recv, at_x, "back_x")
    hard_exp(2)
    forward_z(3, 0)
    hard_part(4, 1)
    hard_exp(3)
    hard_exp(4)

    def hard_query(slot, count, base):
        def body(i, _):
            columns = pl.ds(pl.multiple_of(i * wide, wide), wide)
            pq[base : base + count * rows, columns] = dot_nn(
                eh[slot * rows : (slot + count) * rows, :], p_ref[:, columns]
            )
            return 0

        lax.fori_loop(0, width // wide, body, 0)

    back_right = {}
    back_left = {}

    pq_base = {3: 0, 2: 2 * rows, 1: 0, 4: 4 * rows}

    def stage_back(k, start, count, right, came=None, wait=True):
        first = place(k, not right, start)
        base = first - 2 * (k - 1) * rows + pq_base[k]
        if came is None:
            stage(zs_send, first, pq, base, count)
        else:
            if wait:
                (back_right if right else back_left)[came].wait_recv()
            stage(zs_send, first, pq, base, count, zs_recv, place(k + 1, not right, start))

    def start_back(k, start, count, right):
        here = pl.ds(place(k, not right, start), count)
        (back_right if right else back_left)[k, start] = send(
            zs_send.at[here], zs_recv.at[here], at_z(1 if right else -1), "back_z"
        )

    def send_back(k, start, count, right, came=None, wait=True):
        stage_back(k, start, count, right, came, wait)
        start_back(k, start, count, right)

    hard_query(4, 1, 0)
    stage_back(3, half, half, True)
    stage_back(3, 0, half, False)
    x_second += square_last(x_first, xs_send, xs_recv, at_x, "back_x")
    forward_z(3, 1)
    hard_part(5, 1)
    start_back(3, half, half, True)
    start_back(3, 0, half, False)
    hard_exp(5)
    for slot in range(6):
        send_hard_sum(slot)
    z_right[4, 0].wait_recv()
    z_left[4, 1].wait_recv()
    hard_part(far, 1)
    hard_query(5, 1, rows)
    hard_exp(far)
    send_hard_sum(far)
    hard_query(far, 1, 4 * rows)
    send_back(4, 0, half, True)
    send_back(4, half, half, False)

    rest = in_sums[0]
    moment = in_moments[0]
    wait_came("sum_x", sum_x)
    wait_came("sum_z", sum_z)
    for m in range(3):
        rest = rest + sum_x[m][0:1, :]
        moment = moment + sum_x[m][1:2, :]
    for m in range(7):
        rest = rest + sum_z[m][0:1, :]
        moment = moment + sum_z[m][1:2, :]
    total = rest + jnp.exp(own_score)
    ratio = inverse_temp / total
    factor = ratio * q_row
    inverse = 1.0 / total
    fac_row[...] = factor
    fac_own[...] = jnp.where(line == 0, factor, inverse)
    for m in range(3):
        send(fac_own, fac_x.at[m], x_targets[m], "fac_x", True)
    for m in range(7):
        send(fac_row, fac_z.at[m], z_targets[m], "fac_z", True)
    loss_z[z] = jnp.log(total) - own_score
    for k in range(1, 8):
        send(loss_z.at[z], loss_z.at[z], at_z(k), "loss_z", True)

    hard_query(2, 2, 2 * rows)

    along = (moment - rest * own_score) / total
    own_col[...] = to_column(factor * rest)
    ratio_col[...] = to_column(factor)
    rest_col[...] = to_column(factor * rest * position_row)
    along_col[...] = to_column(along * q_row * q_row)
    repeat = width // lanes

    wait_came("fac_x", fac_x)
    near_rows = [factor if n == 0 else fac_x[n - 1][0:1, :] for n in range(side)]

    def in_weights(i, _):
        part = pl.ds(pl.multiple_of(i * rows, rows), rows)
        for n in range(side):
            columns = slice(n * rows, (n + 1) * rows)
            ein[part, columns] = (ein_t[part, columns] * near_rows[n]).astype(bf16)
        return 0

    lax.fori_loop(0, side, in_weights, 0)

    in_product(3 * rows, 4 * rows, xq)
    y_first = square_first(ys_send, ys_recv, at_y, "back_y")
    send_back(2, half, half, True, came=(3, half))
    send_back(2, 0, half, False, came=(3, 0))
    in_product(rows, 3 * rows, xq)
    y_second = square_free(ys_send, ys_recv, at_y, "back_y")

    for copy in x_second:
        copy.wait_recv()

    def gather_x(i, _):
        part = pl.ds(pl.multiple_of(i * grain, grain), grain)
        after = pl.ds(pl.multiple_of(rows + i * grain, grain), grain)
        values = pin[part, :] + (
            xs_recv[part, :].astype(f32) + xs_recv[after, :].astype(f32)
        )
        dq_acc[part, :] = (
            values * tile_lanes(ratio_col[part, :], repeat)
            - yp[part, :].astype(f32) * tile_lanes(rest_col[part, :], repeat)
            - q_ref[part, :].astype(f32) * tile_lanes(along_col[part, :], repeat)
        )
        return 0

    lax.fori_loop(0, rows // grain, gather_x, 0)

    in_product(0, rows, xq)

    inverse_rows = [inverse if n == 0 else fac_x[n - 1][1:2, :] for n in range(side)]

    def own_shares(i, _):
        part = pl.ds(pl.multiple_of(i * rows, rows), rows)
        shares = jnp.zeros((rows, lanes), f32)
        for n in range(side):
            shares = shares + ein_s[part, n * rows : (n + 1) * rows] * inverse_rows[n]
        own_out[i] = jnp.sum(jnp.transpose(shares), axis=0, keepdims=True)
        return 0

    lax.fori_loop(0, side, own_shares, 0)
    own_along = own_out[0] - rest * own_score * inverse
    for c in range(1, side):
        send(own_out.at[c], own_y.at[c - 1], y_homes[c - 1], "own", True)
    send_back(3, 0, half, True, came=(4, 0))
    send_back(3, half, half, False, came=(4, half))
    hard_query(0, 2, 0)

    wait_came("fac_z", fac_z)
    tile_rows = [of_tile(m, lambda block: fac_z[block]) for m in range(7)]

    def hard_weights(i, _):
        part = pl.ds(pl.multiple_of(i * rows, rows), rows)
        for m in range(7):
            columns = slice(m * rows, (m + 1) * rows)
            wt[part, columns] = (eh_t[part, columns] * tile_rows[m]).astype(bf16)
        return 0

    lax.fori_loop(0, tiles, hard_weights, 0)

    y_second += square_last(y_first, ys_send, ys_recv, at_y, "back_y")
    send_back(1, half, half, True, came=(2, half))
    send_back(1, 0, half, False, came=(2, 0))

    def passage_hard(i, _):
        columns = pl.ds(pl.multiple_of(i * 256, 256), 256)
        dp_acc[:, columns] = dot_nn(wt[:, 0 : 7 * rows], zq[0 : 7 * rows, columns])
        return 0

    lax.fori_loop(0, width // 256, passage_hard, 0)
    wait_sent("z", zq.at[pl.ds(0, 7 * rows)])
    wait_sent("x", xq.at[pl.ds(0, 3 * rows)])
    wait_sent("y", yp.at[pl.ds(0, 3 * rows)])
    wait_sent("back_x", xs_send)
    wait_sent("norm", norm_mine)
    wait_sent("hard", sh_mine)
    wait_sent("in", si_mine)
    wait_sent("aux_z", aux_z)
    wait_sent("aux_x", aux_x)
    wait_sent("aux_y", aux_y)
    wait_sent("sum_z", sum_z)
    wait_sent("sum_x", sum_x)
    wait_sent("fac_z", fac_z)
    wait_sent("fac_x", fac_x)
    wait_sent("own", own_y)

    def passage_along(i, _):
        part = pl.ds(pl.multiple_of(i * grain, grain), grain)
        along_p_mine[part, :] = fold_lanes(dp_acc[part, :] * p_ref[part, :].astype(f32))
        return 0

    lax.fori_loop(0, p_rows // grain, passage_along, 0)
    along_p_copy = send(along_p_mine, along_p_peer, other, "along")
    quarter = half // 2
    for start in (0, quarter):
        send_back(2, start, quarter, True, came=(3, 0), wait=start == 0)
        send_back(2, half + start, quarter, False, came=(3, half), wait=start == 0)

    wait_came("loss_z", loss_z.at[pl.ds(0, 7)])
    value = loss_z[0]
    for k in range(1, 8):
        value = value + loss_z[k]
    loss_x[x] = value
    for k in range(1, side):
        send(loss_x.at[x], loss_x.at[x], at_x(k), "loss_x", True)
    wait_came("loss_x", loss_x.at[pl.ds(0, 3)])
    value = loss_x[0]
    for k in range(1, side):
        value = value + loss_x[k]
    loss_y[y] = value
    for k in range(1, side):
        send(loss_y.at[y], loss_y.at[y], at_y(k), "loss_y", True)

    wait_came("own", own_y)
    for m in range(3):
        own_along = own_along + own_y[m][0:1, :]
    along_p_copy.wait_recv()
    for copy in y_second:
        copy.wait_recv()

    def positive_rows(i, _):
        part = pl.ds(pl.multiple_of(i * grain, grain), grain)
        after = pl.ds(pl.multiple_of(rows + i * grain, grain), grain)
        values = pin[part, :] + (ys_recv[part, :].astype(f32) + ys_recv[after, :].astype(f32))
        values = values - tile_lanes(own_col[part, :], repeat) * q_ref[part, :].astype(f32)
        high = values.astype(bf16)
        zq[pl.ds(pl.multiple_of(7 * rows + i * grain, grain), grain), :] = high
        zq[pl.ds(pl.multiple_of(8 * rows + i * grain, grain), grain), :] = (
            values - high.astype(f32)
        ).astype(bf16)
        return 0

    lax.fori_loop(0, rows // grain, positive_rows, 0)

    def passage_out(i, _):
        part = pl.ds(pl.multiple_of(i * rows, rows), rows)
        scale = pcol[part, :]
        shares = (along_p_mine[part, :] + along_p_peer[part, :]) * scale
        shares = shares + wt[part, 7 * rows : 8 * rows].astype(f32) * own_along
        along = jnp.sum(shares, axis=1, keepdims=True)
        along = jnp.broadcast_to(along, (rows, lanes)) * scale
        for c in range(width // wide):
            columns = slice(c * wide, (c + 1) * wide)
            values = dp_acc[part, columns] + dot_nn(
                wt[part, 7 * rows : 9 * rows], zq[7 * rows : 9 * rows, columns]
            )
            dp_ref[part, columns] = (
                (values - p_ref[part, columns].astype(f32) * tile_lanes(along, wide // lanes))
                * tile_lanes(scale, wide // lanes)
            ).astype(bf16)
        return 0

    lax.fori_loop(0, tiles // 2, passage_out, 0)
    send_back(1, 0, quarter, True, came=(2, 0))
    send_back(1, half, quarter, False, came=(2, half))
    lax.fori_loop(tiles // 2, tiles, passage_out, 0)
    send_back(1, quarter, quarter, True, came=(2, quarter))
    send_back(1, half + quarter, quarter, False, came=(2, half + quarter))
    wait_came("loss_y", loss_y.at[pl.ds(0, 3)])
    value = loss_y[0]
    for k in range(1, side):
        value = value + loss_y[k]
    queries = rows * owners * side * side
    mean = jnp.sum(value[0:1, :], axis=1, keepdims=True) * (1.0 / queries)
    loss_ref[...] = jnp.broadcast_to(mean, (8, lanes))
    wait_sent("loss_z", loss_z.at[pl.ds(0, 7)])
    wait_sent("loss_x", loss_x.at[pl.ds(0, 3)])
    wait_sent("loss_y", loss_y.at[pl.ds(0, 3)])
    wait_sent("along", along_p_mine)
    wait_sent("back_y", ys_send)

    def query_out(first):
        def body(i, _):
            part = pl.ds(pl.multiple_of(first + i * grain, grain), grain)
            before = pl.ds(pl.multiple_of(place(1, True, first) + i * grain, grain), grain)
            after = pl.ds(pl.multiple_of(place(1, False, first) + i * grain, grain), grain)
            back = zs_recv[before, :].astype(f32) + zs_recv[after, :].astype(f32)
            dq_ref[part, :] = (
                dq_acc[part, :] + back * tile_lanes(ratio_col[part, :], repeat)
            ).astype(bf16)
            return 0

        lax.fori_loop(0, quarter // grain, body, 0)

    back_right[1, half].wait_recv()
    back_left[1, 0].wait_recv()
    for start in (0, quarter):
        back_right[1, start].wait_recv()
        query_out(start)
        back_left[1, half + start].wait_recv()
        query_out(half + start)
    wait_sent("back_z", zs_send)


def flush(loss_ref, dq_ref, dp_ref, loss_out, dq_out, dp_out, one, sems):
    copies = [
        pltpu.make_async_copy(dp_ref, dp_out, sems.at[0]),
        pltpu.make_async_copy(dq_ref, dq_out, sems.at[1]),
    ]
    for copy in copies:
        copy.start()
    one[...] = loss_ref[0:1, 0:1]
    copies.append(pltpu.make_async_copy(one, loss_out, sems.at[2]))
    copies[2].start()
    for copy in copies:
        copy.wait()


def on_device(queries, passages, positive_slot, hard_offset, hard_slot):
    rows, width = queries.shape
    p_rows = passages.shape[0]
    vmem = pl.BlockSpec(memory_space=pltpu.VMEM)
    hbm = pl.BlockSpec(memory_space=pltpu.HBM)

    def f(*shape):
        return pltpu.VMEM(shape, f32)

    def b(*shape):
        return pltpu.VMEM(shape, bf16)

    loss, query_grad, passage_grad = pl.pallas_call(
        kernel,
        out_shape=(
            pltpu.VMEM((8, lanes), f32),
            pltpu.VMEM(queries.shape, bf16),
            pltpu.VMEM(passages.shape, bf16),
        ),
        in_specs=[hbm] * 5,
        out_specs=(vmem, vmem, vmem),
        scratch_shapes=[
            pltpu.VMEM((1, rows), jnp.int32),
            pltpu.VMEM((7, rows), jnp.int32),
            pltpu.VMEM((7, rows), jnp.int32),
            b(p_rows, width),
            b(9 * rows, width),
            f(7, p_rows, rows),
            f(7, p_rows, rows),
            f(p_rows, 7 * rows),
            b(7 * rows, p_rows),
            b(7 * rows, width),
            b(7 * rows, width),
            f(5 * rows, width),
            b(4 * rows, width),
            b(4 * rows, width),
            f(4 * rows, 4 * rows),
            f(4 * rows, 4 * rows),
            f(4 * rows, 4 * rows),
            f(4 * rows, 4 * rows),
            b(4 * rows, 4 * rows),
            f(4 * rows, width),
            b(3 * rows, width),
            b(3 * rows, width),
            b(3 * rows, width),
            b(3 * rows, width),
            f(rows, width),
            f(p_rows, width),
            b(p_rows, 9 * rows),
            b(rows, p_rows),
            f(p_rows + rows, lanes),
            f(p_rows + rows, lanes),
            f(p_rows, lanes),
            f(rows, lanes),
            f(8, lanes),
            f(7, 8, lanes),
            f(3, 8, lanes),
            f(1, lanes),
            f(3, 1, lanes),
            f(10, 2, lanes),
            f(7, 2, lanes),
            f(3, 2, lanes),
            f(1, lanes),
            f(2, lanes),
            f(7, 1, lanes),
            f(3, 2, lanes),
            f(4, 1, lanes),
            f(4, 1, lanes),
            f(3, 1, lanes),
            f(8, 1, lanes),
            f(4, 1, lanes),
            f(4, 1, lanes),
            f(p_rows, lanes),
            f(p_rows, lanes),
            f(rows, lanes),
            f(rows, lanes),
            f(rows, lanes),
            f(rows, lanes),
            pltpu.SemaphoreType.DMA((len(kinds),)),
            pltpu.SemaphoreType.DMA((len(shared) + alone,)),
            pltpu.SemaphoreType.DMA((5,)),
        ],
        compiler_params=pltpu.CompilerParams(
            collective_id=0, has_side_effects=True, vmem_limit_bytes=58 * 1024 * 1024
        ),
        cost_estimate=pl.CostEstimate(
            flops=15_000_000_000, bytes_accessed=6_000_000, transcendentals=800_000
        ),
    )(positive_slot.reshape(1, rows), hard_offset.T, hard_slot.T, queries, passages)
    loss, query_grad, passage_grad = pl.pallas_call(
        flush,
        out_shape=(
            jax.ShapeDtypeStruct((1, 1), f32),
            jax.ShapeDtypeStruct(queries.shape, bf16),
            jax.ShapeDtypeStruct(passages.shape, bf16),
        ),
        in_specs=[vmem, vmem, vmem],
        out_specs=(hbm, hbm, hbm),
        scratch_shapes=[f(1, 1), pltpu.SemaphoreType.DMA((3,))],
        compiler_params=pltpu.CompilerParams(vmem_limit_bytes=1024 * 1024),
    )(
        pltpu.with_memory_space_constraint(loss, pltpu.VMEM),
        pltpu.with_memory_space_constraint(query_grad, pltpu.VMEM),
        pltpu.with_memory_space_constraint(passage_grad, pltpu.VMEM),
    )
    return loss[0, 0], query_grad, passage_grad


def solution(mesh):
    in_specs = (
        P(("group", "index"), "tensor"),
        P(("group", "index"), "tensor"),
        P(("group", "index")),
        P(("group", "index"), None),
        P(("group", "index"), None),
    )
    out_specs = (P(), P(("group", "index"), "tensor"), P(("group", "index"), "tensor"))
    return jax.shard_map(
        on_device, mesh=mesh, in_specs=in_specs, out_specs=out_specs, check_vma=False
    )
```

```python
import jax
import jax.numpy as jnp
from jax import lax
from jax.experimental import pallas as pl
from jax.experimental.pallas import tpu as pltpu
from jax.sharding import PartitionSpec as P

epsilon = 1e-06
inverse_temp = 50.0
side = 4
lanes = 128
shared = ("aux_z", "aux_x", "aux_y", "sum_z", "sum_x", "fac_z", "fac_x", "own")
shared = shared + ("loss_z", "loss_x", "loss_y")
kinds = shared + ("z", "x", "y", "back_z", "back_x", "back_y", "norm", "hard", "in", "along")
alone = 68
f32 = jnp.float32
bf16 = jnp.bfloat16


def dot_nt(a, b):
    return lax.dot_general(a, b, (((1,), (1,)), ((), ())), preferred_element_type=f32)


def dot_nn(a, b):
    return jnp.dot(a, b, preferred_element_type=f32)


def tile_lanes(values, count):
    return jnp.concatenate([values] * count, axis=1)


def fold_lanes(values):
    total = values[:, :lanes]
    for k in range(1, values.shape[1] // lanes):
        total = total + values[:, k * lanes : (k + 1) * lanes]
    return total


def to_column(row):
    return jnp.transpose(jnp.broadcast_to(row, (lanes, lanes)))


def kernel(
    slot_hbm,
    offset_hbm,
    hard_slot_hbm,
    q_hbm,
    p_hbm,
    loss_ref,
    dq_ref,
    dp_ref,
    slot_ref,
    offset_ref,
    hard_slot_ref,
    p_ref,
    zq,
    sh_mine,
    sh_peer,
    eh_t,
    eh,
    zs_send,
    zs_recv,
    pq,
    xq,
    yp,
    si_mine,
    si_peer,
    ein_t,
    ein_s,
    ein,
    pin,
    xs_send,
    xs_recv,
    ys_send,
    ys_recv,
    dq_acc,
    dp_acc,
    wt,
    pick,
    norm_mine,
    norm_peer,
    pcol,
    qcol,
    aux_own,
    aux_z,
    aux_x,
    pos_own,
    aux_y,
    sum_out,
    sum_z,
    sum_x,
    fac_row,
    fac_own,
    fac_z,
    fac_x,
    own_out,
    crow,
    own_y,
    loss_z,
    loss_x,
    loss_y,
    along_p_mine,
    along_p_peer,
    own_col,
    rest_col,
    ratio_col,
    along_col,
    send_sems,
    recv_sems,
    load_sems,
):
    rows, width = q_hbm.shape
    p_rows = p_ref.shape[0]
    half = rows // 2
    tiles = p_rows // rows
    group = lax.axis_index("group")
    z = lax.axis_index("index")
    t = lax.axis_index("tensor")
    y = lax.div(group, side)
    x = lax.rem(group, side)
    owners = lax.axis_size("index")

    def at_z(k):
        return (group, lax.rem(z + k + owners, owners), t)

    def at_x(k):
        return (y * side + lax.rem(x + k + side, side), z, t)

    def at_y(k):
        return (lax.rem(y + k + side, side) * side + x, z, t)

    other = (group, z, 1 - t)

    received = []

    def send(src, dst, target, kind, together=False):
        if not together:
            received.append(kind)
        slot = kinds.index(kind) if together else len(shared) + len(received) - 1
        copy = pltpu.make_async_remote_copy(
            src_ref=src,
            dst_ref=dst,
            send_sem=send_sems.at[kinds.index(kind)],
            recv_sem=recv_sems.at[slot],
            device_id=target,
            device_id_type=pl.DeviceIdType.MESH,
        )
        copy.start()
        return copy

    def wait_sent(kind, ref):
        pltpu.make_async_copy(ref, ref, send_sems.at[kinds.index(kind)]).wait()

    def wait_came(kind, ref):
        pltpu.make_async_copy(ref, ref, recv_sems.at[kinds.index(kind)]).wait()

    def rows_of(slot, part=None):
        if part is None:
            return pl.ds(slot * rows, rows)
        return pl.ds(slot * rows + part * half, half)

    far = 6

    def place(k, before, start):
        if k == 4:
            return far * rows + start
        return (2 * (k - 1) + int((start < half) != before)) * rows + start

    first_lanes = lax.broadcasted_iota(jnp.int32, (1, lanes), 1) < half

    def of_tile(tile, pair):
        if tile == far:
            return pair(far)
        block = tile - tile % 2
        low, high = (block, block + 1) if tile == block else (block + 1, block)
        return jnp.where(first_lanes, pair(low), pair(high))

    z_targets = [at_z(1), at_z(-1), at_z(2), at_z(-2), at_z(3), at_z(-3), at_z(4)]
    z_homes = [at_z(-1), at_z(1), at_z(-2), at_z(2), at_z(-3), at_z(3), at_z(4)]
    x_targets = [at_x(1), at_x(-1), at_x(2)]
    x_homes = [at_x(-1), at_x(1), at_x(2)]
    y_targets = [at_y(1), at_y(-1), at_y(2)]
    y_homes = [at_y(-1), at_y(1), at_y(2)]

    barrier = pltpu.get_barrier_semaphore()
    peers = z_targets + x_targets + y_targets + [other]
    for peer in peers:
        pl.semaphore_signal(barrier, inc=1, device_id=peer, device_id_type=pl.DeviceIdType.MESH)
    loads = [
        pltpu.make_async_copy(src, dst, load_sems.at[i])
        for i, (src, dst) in enumerate(
            [
                (slot_hbm, slot_ref),
                (offset_hbm, offset_ref),
                (hard_slot_hbm, hard_slot_ref),
                (p_hbm, p_ref),
                (q_hbm, xq.at[rows_of(0)]),
            ]
        )
    ]
    for load in loads:
        load.start()
    pl.semaphore_wait(barrier, len(peers))

    def z_rows(k, before, c):
        return pl.ds(place(k, before, c * half), half)

    z_right = {}
    z_left = {}
    for c in range(2):
        right_own = q_hbm.at[pl.ds(c * half, half)]
        left_own = q_hbm.at[pl.ds((1 - c) * half, half)]
        z_right[1, c] = send(right_own, zq.at[z_rows(1, True, c)], at_z(1), "z")
        z_left[1, 1 - c] = send(left_own, zq.at[z_rows(1, False, 1 - c)], at_z(-1), "z")
    x_right = send(q_hbm, xq.at[rows_of(1)], at_x(1), "x")
    x_left = send(q_hbm, xq.at[rows_of(2)], at_x(-1), "x")
    for load in loads:
        load.wait()
    q_ref = xq

    slots = slot_ref[0:1, :]
    for i in range(tiles):
        ids = lax.broadcasted_iota(jnp.int32, (rows, lanes), 0) + i * rows
        chosen = jnp.where(ids == slots, 1.0, 0.0).astype(f32)
        pick[:, i * rows : (i + 1) * rows] = jnp.transpose(chosen).astype(bf16)
        wt[i * rows : (i + 1) * rows, 7 * rows : 8 * rows] = chosen.astype(bf16)
        wt[i * rows : (i + 1) * rows, 8 * rows : 9 * rows] = chosen.astype(bf16)

    wide = 512

    def pick_columns(i, _):
        columns = pl.ds(pl.multiple_of(i * wide, wide), wide)
        yp[0:rows, columns] = dot_nn(pick[...], p_ref[:, columns]).astype(bf16)
        return 0

    lax.fori_loop(0, width // wide, pick_columns, 0)
    y_right = send(yp.at[rows_of(0)], yp.at[rows_of(1)], at_y(1), "y")
    y_left = send(yp.at[rows_of(0)], yp.at[rows_of(2)], at_y(-1), "y")

    strip = 32

    def square_strip(source, base):
        def body(i, _):
            part = pl.ds(pl.multiple_of(i * strip, strip), strip)
            values = source[part, :].astype(f32)
            norm_mine[pl.ds(pl.multiple_of(base + i * strip, strip), strip), :] = fold_lanes(
                values * values
            )
            return 0

        return body

    lax.fori_loop(0, p_rows // strip, square_strip(p_ref, 0), 0)
    lax.fori_loop(0, rows // strip, square_strip(q_ref, p_rows), 0)
    norm_copy = send(norm_mine, norm_peer, other, "norm")
    norm_copy.wait_recv()

    def scale_of(start):
        squares = norm_mine[start : start + rows, :] + norm_peer[start : start + rows, :]
        total = jnp.sum(squares, axis=1, keepdims=True)
        return jnp.broadcast_to(1.0 / jnp.sqrt(total + epsilon), (rows, lanes))

    position_row = jnp.zeros((1, lanes), f32)
    for i in range(tiles):
        scale = scale_of(i * rows)
        pcol[i * rows : (i + 1) * rows, :] = scale
        ids = lax.broadcasted_iota(jnp.int32, (rows, lanes), 0) + i * rows
        position_row = position_row + jnp.sum(
            jnp.where(ids == slots, scale, 0.0), axis=0, keepdims=True
        )
    q_scale = scale_of(p_rows)
    qcol[...] = q_scale
    q_row = jnp.transpose(q_scale)[0:1, :]
    owner_ids = lax.rem(offset_ref[...] + (z + 1), owners)
    aux_own[0:7, :] = (owner_ids * p_rows + hard_slot_ref[...]).astype(f32)
    aux_own[7:8, :] = q_row
    pos_own[...] = position_row
    aux_copies = [
        send(aux_own, aux_z.at[0], at_z(1), "aux_z"),
        send(aux_own, aux_z.at[1], at_z(-1), "aux_z"),
    ]

    def forward_aux(blocks):
        for m in blocks:
            aux_copies[m].wait_recv()
            if m < 5:
                aux_copies.append(
                    send(aux_z.at[m], aux_z.at[m + 2], at_z(-1 if m % 2 else 1), "aux_z")
                )

    for m in range(3):
        send(aux_own, aux_x.at[m], x_targets[m], "aux_x", True)
        send(pos_own, aux_y.at[m], y_targets[m], "aux_y", True)

    def forward_z(k, c):
        z_right[k, c].wait_recv()
        here = zq.at[z_rows(k, True, c)]
        if k < 3 or c == 0:
            z_right[k + 1, c] = send(here, zq.at[z_rows(k + 1, True, c)], at_z(1), "z")
        z_left[k, 1 - c].wait_recv()
        here = zq.at[z_rows(k, False, 1 - c)]
        if k < 3 or c == 0:
            z_left[k + 1, 1 - c] = send(here, zq.at[z_rows(k + 1, False, 1 - c)], at_z(-1), "z")

    line = lax.broadcasted_iota(jnp.int32, (2, lanes), 0)
    hard_copies = {}

    def hard_part(tile, count):
        def body(i, _):
            part = pl.ds(pl.multiple_of(i * 256, 256), 256)
            scores = dot_nt(p_ref[part, :], zq[tile * rows : (tile + count) * rows, :])
            for n in range(count):
                sh_mine[tile + n, part, :] = scores[:, n * lanes : (n + 1) * lanes]
            return 0

        lax.fori_loop(0, p_rows // 256, body, 0)
        here = pl.ds(tile, count)
        copy = send(sh_mine.at[here], sh_peer.at[here], other, "hard")
        for n in range(count):
            hard_copies[tile + n] = copy if n == 0 else None

    first_slot = (z * p_rows).astype(f32)
    hard_sums = {}

    def hard_exp(tile):
        if hard_copies[tile] is not None:
            hard_copies[tile].wait_recv()
        packet = of_tile(tile, lambda block: aux_z[block])
        row_scale = inverse_temp * packet[7:8, :]
        columns = slice(tile * rows, (tile + 1) * rows)

        def body(i, carry):
            sums, moments = carry
            part = pl.ds(pl.multiple_of(i * rows, rows), rows)
            ids = (
                lax.broadcasted_iota(jnp.int32, (rows, lanes), 0) + i * rows
            ).astype(f32) + first_slot
            times = jnp.zeros((rows, lanes), f32)
            for j in range(7):
                times = times + jnp.where(ids == packet[j : j + 1, :], 1.0, 0.0)
            scale = pcol[part, :]
            score = (sh_mine[tile, part, :] + sh_peer[tile, part, :]) * (scale * row_scale)
            weight = jnp.where(times > 0.0, times * jnp.exp(score), 0.0)
            eh_t[part, columns] = weight
            eh[columns, part] = jnp.transpose(weight * scale).astype(bf16)
            return (
                sums + jnp.sum(weight, axis=0, keepdims=True),
                moments + jnp.sum(weight * score, axis=0, keepdims=True),
            )

        zero = jnp.zeros((1, lanes), f32)
        sums, moments = lax.fori_loop(0, tiles, body, (zero, zero))
        hard_sums[tile] = jnp.where(line == 0, sums, moments)

    def send_hard_sum(slot):
        sum_out[slot] = of_tile(slot, lambda tile: hard_sums[tile])
        send(sum_out.at[slot], sum_z.at[slot], z_homes[slot], "sum_z", True)

    forward_z(1, 0)
    forward_aux((0, 1))
    forward_z(1, 1)
    forward_aux((2, 3))
    x_right.wait_recv()
    x_far_right = send(xq.at[rows_of(1, 0)], xq.at[rows_of(3, 0)], at_x(1), "x")
    x_left.wait_recv()
    x_far_left = send(xq.at[rows_of(2, 1)], xq.at[rows_of(3, 1)], at_x(-1), "x")
    y_right.wait_recv()
    y_far_right = send(yp.at[rows_of(1, 0)], yp.at[rows_of(3, 0)], at_y(1), "y")
    y_left.wait_recv()
    y_far_left = send(yp.at[rows_of(2, 1)], yp.at[rows_of(3, 1)], at_y(-1), "y")
    hard_part(0, 2)
    hard_exp(0)
    hard_exp(1)
    forward_z(2, 0)
    forward_aux((4, 5))

    x_far_right.wait_recv()
    x_far_left.wait_recv()
    y_far_right.wait_recv()
    y_far_left.wait_recv()

    def in_part(i, _):
        part = pl.ds(pl.multiple_of(i * rows, rows), rows)
        si_mine[part, :] = dot_nt(yp[part, :], xq[...])
        return 0

    lax.fori_loop(0, side, in_part, 0)
    in_copy = send(si_mine, si_peer, other, "in")
    hard_part(2, 1)
    wait_came("aux_x", aux_x)
    wait_came("aux_y", aux_y)
    in_copy.wait_recv()
    crow[0] = position_row
    for c in range(1, side):
        crow[c] = aux_y[c - 1]
    near_scale = [inverse_temp * (q_row if n == 0 else aux_x[n - 1][7:8, :]) for n in range(side)]
    ahead = lax.broadcasted_iota(jnp.int32, (rows, lanes), 0) - lax.broadcasted_iota(
        jnp.int32, (rows, lanes), 1
    )

    def in_exp(i, carry):
        sums, moments, own = carry
        scale = to_column(crow[i])
        part = pl.ds(pl.multiple_of(i * rows, rows), rows)
        own_place = ahead == i * (2 * rows)
        new_sums, new_moments = [], []
        for n in range(side):
            columns = slice(n * rows, (n + 1) * rows)
            score = (si_mine[part, columns] + si_peer[part, columns]) * (scale * near_scale[n])
            weight = jnp.exp(score)
            if n == 0:
                own = own + jnp.sum(jnp.where(own_place, score, 0.0), axis=0, keepdims=True)
                weight = jnp.where(own_place, 0.0, weight)
            moment = weight * score
            ein_t[part, columns] = weight
            ein_s[part, columns] = moment
            ein[columns, part] = jnp.transpose(weight * scale).astype(bf16)
            new_sums.append(sums[n] + jnp.sum(weight, axis=0, keepdims=True))
            new_moments.append(moments[n] + jnp.sum(moment, axis=0, keepdims=True))
        return tuple(new_sums), tuple(new_moments), own

    zeros = tuple(jnp.zeros((1, lanes), f32) for _ in range(side))
    in_sums, in_moments, own_score = lax.fori_loop(0, side, in_exp, (zeros, zeros, zeros[0]))
    for n in range(1, side):
        sum_out[6 + n] = jnp.where(line == 0, in_sums[n], in_moments[n])
        send(sum_out.at[6 + n], sum_x.at[n - 1], x_homes[n - 1], "sum_x", True)

    forward_z(2, 1)
    forward_aux((6,))

    def in_product(start, stop, other_rows):
        def body(i, _):
            columns = pl.ds(pl.multiple_of(i * wide, wide), wide)
            pin[start:stop, columns] = dot_nn(ein[start:stop, :], other_rows[:, columns])
            return 0

        lax.fori_loop(0, width // wide, body, 0)

    in_product(3 * rows, 4 * rows, yp)

    grain = 16

    def stage(dst, dst_row, src, src_row, count, add=None, add_row=0):
        def body(i, _):
            values = src[pl.ds(pl.multiple_of(src_row + i * grain, grain), grain), :]
            if add is not None:
                values = values + add[
                    pl.ds(pl.multiple_of(add_row + i * grain, grain), grain), :
                ].astype(f32)
            dst[pl.ds(pl.multiple_of(dst_row + i * grain, grain), grain), :] = values.astype(
                dst.dtype
            )
            return 0

        lax.fori_loop(0, count // grain, body, 0)

    def square_first(send_buffer, recv_buffer, at, kind):
        stage(send_buffer, 2 * rows, pin, 3 * rows, rows)
        return (
            send(send_buffer.at[rows_of(2, 0)], recv_buffer.at[rows_of(2, 0)], at(1), kind),
            send(send_buffer.at[rows_of(2, 1)], recv_buffer.at[rows_of(2, 1)], at(-1), kind),
        )

    def square_free(send_buffer, recv_buffer, at, kind):
        stage(send_buffer, 0, pin, rows, half)
        before = send(send_buffer.at[rows_of(0, 0)], recv_buffer.at[rows_of(0, 0)], at(-1), kind)
        stage(send_buffer, rows + half, pin, 2 * rows + half, half)
        after = send(send_buffer.at[rows_of(1, 1)], recv_buffer.at[rows_of(1, 1)], at(1), kind)
        return [before, after]

    def square_last(first, send_buffer, recv_buffer, at, kind):
        first[0].wait_recv()
        stage(send_buffer, rows, pin, 2 * rows, half, recv_buffer, 2 * rows)
        after = send(send_buffer.at[rows_of(1, 0)], recv_buffer.at[rows_of(1, 0)], at(1), kind)
        first[1].wait_recv()
        stage(send_buffer, half, pin, rows + half, half, recv_buffer, 2 * rows + half)
        before = send(send_buffer.at[rows_of(0, 1)], recv_buffer.at[rows_of(0, 1)], at(-1), kind)
        return [before, after]

    x_first = square_first(xs_send, xs_recv, at_x, "back_x")
    hard_part(3, 1)
    in_product(0, 3 * rows, yp)
    x_second = square_free(xs_send, xs_recv, at_x, "back_x")
    hard_exp(2)
    forward_z(3, 0)
    hard_part(4, 1)
    hard_exp(3)
    hard_exp(4)

    def hard_query(slot, count, base):
        def body(i, _):
            columns = pl.ds(pl.multiple_of(i * wide, wide), wide)
            pq[base : base + count * rows, columns] = dot_nn(
                eh[slot * rows : (slot + count) * rows, :], p_ref[:, columns]
            )
            return 0

        lax.fori_loop(0, width // wide, body, 0)

    back_right = {}
    back_left = {}

    pq_base = {3: 0, 2: 2 * rows, 1: 0, 4: 4 * rows}

    def stage_back(k, start, count, right, came=None, wait=True):
        first = place(k, not right, start)
        base = first - 2 * (k - 1) * rows + pq_base[k]
        if came is None:
            stage(zs_send, first, pq, base, count)
        else:
            if wait:
                (back_right if right else back_left)[came].wait_recv()
            stage(zs_send, first, pq, base, count, zs_recv, place(k + 1, not right, start))

    def start_back(k, start, count, right):
        here = pl.ds(place(k, not right, start), count)
        (back_right if right else back_left)[k, start] = send(
            zs_send.at[here], zs_recv.at[here], at_z(1 if right else -1), "back_z"
        )

    def send_back(k, start, count, right, came=None, wait=True):
        stage_back(k, start, count, right, came, wait)
        start_back(k, start, count, right)

    hard_query(4, 1, 0)
    stage_back(3, half, half, True)
    stage_back(3, 0, half, False)
    x_second += square_last(x_first, xs_send, xs_recv, at_x, "back_x")
    forward_z(3, 1)
    hard_part(5, 1)
    start_back(3, half, half, True)
    start_back(3, 0, half, False)
    hard_exp(5)
    for slot in range(6):
        send_hard_sum(slot)
    z_right[4, 0].wait_recv()
    z_left[4, 1].wait_recv()
    hard_part(far, 1)
    hard_query(5, 1, rows)
    hard_exp(far)
    send_hard_sum(far)
    hard_query(far, 1, 4 * rows)
    send_back(4, 0, half, True)
    send_back(4, half, half, False)

    rest = in_sums[0]
    moment = in_moments[0]
    wait_came("sum_x", sum_x)
    wait_came("sum_z", sum_z)
    for m in range(3):
        rest = rest + sum_x[m][0:1, :]
        moment = moment + sum_x[m][1:2, :]
    for m in range(7):
        rest = rest + sum_z[m][0:1, :]
        moment = moment + sum_z[m][1:2, :]
    total = rest + jnp.exp(own_score)
    ratio = inverse_temp / total
    factor = ratio * q_row
    inverse = 1.0 / total
    fac_row[...] = factor
    fac_own[...] = jnp.where(line == 0, factor, inverse)
    for m in range(3):
        send(fac_own, fac_x.at[m], x_targets[m], "fac_x", True)
    for m in range(7):
        send(fac_row, fac_z.at[m], z_targets[m], "fac_z", True)
    loss_z[z] = jnp.log(total) - own_score
    for k in range(1, 8):
        send(loss_z.at[z], loss_z.at[z], at_z(k), "loss_z", True)

    hard_query(2, 2, 2 * rows)

    along = (moment - rest * own_score) / total
    own_col[...] = to_column(factor * rest)
    ratio_col[...] = to_column(factor)
    rest_col[...] = to_column(factor * rest * position_row)
    along_col[...] = to_column(along * q_row * q_row)
    repeat = width // lanes

    wait_came("fac_x", fac_x)
    near_rows = [factor if n == 0 else fac_x[n - 1][0:1, :] for n in range(side)]

    def in_weights(i, _):
        part = pl.ds(pl.multiple_of(i * rows, rows), rows)
        for n in range(side):
            columns = slice(n * rows, (n + 1) * rows)
            ein[part, columns] = (ein_t[part, columns] * near_rows[n]).astype(bf16)
        return 0

    lax.fori_loop(0, side, in_weights, 0)

    in_product(3 * rows, 4 * rows, xq)
    y_first = square_first(ys_send, ys_recv, at_y, "back_y")
    send_back(2, half, half, True, came=(3, half))
    send_back(2, 0, half, False, came=(3, 0))
    in_product(rows, 3 * rows, xq)
    y_second = square_free(ys_send, ys_recv, at_y, "back_y")

    for copy in x_second:
        copy.wait_recv()

    def gather_x(i, _):
        part = pl.ds(pl.multiple_of(i * grain, grain), grain)
        after = pl.ds(pl.multiple_of(rows + i * grain, grain), grain)
        values = pin[part, :] + (
            xs_recv[part, :].astype(f32) + xs_recv[after, :].astype(f32)
        )
        dq_acc[part, :] = (
            values * tile_lanes(ratio_col[part, :], repeat)
            - yp[part, :].astype(f32) * tile_lanes(rest_col[part, :], repeat)
            - q_ref[part, :].astype(f32) * tile_lanes(along_col[part, :], repeat)
        )
        return 0

    lax.fori_loop(0, rows // grain, gather_x, 0)

    in_product(0, rows, xq)

    inverse_rows = [inverse if n == 0 else fac_x[n - 1][1:2, :] for n in range(side)]

    def own_shares(i, _):
        part = pl.ds(pl.multiple_of(i * rows, rows), rows)
        shares = jnp.zeros((rows, lanes), f32)
        for n in range(side):
            shares = shares + ein_s[part, n * rows : (n + 1) * rows] * inverse_rows[n]
        own_out[i] = jnp.sum(jnp.transpose(shares), axis=0, keepdims=True)
        return 0

    lax.fori_loop(0, side, own_shares, 0)
    own_along = own_out[0] - rest * own_score * inverse
    for c in range(1, side):
        send(own_out.at[c], own_y.at[c - 1], y_homes[c - 1], "own", True)
    send_back(3, 0, half, True, came=(4, 0))
    send_back(3, half, half, False, came=(4, half))
    hard_query(0, 2, 0)

    wait_came("fac_z", fac_z)
    tile_rows = [of_tile(m, lambda block: fac_z[block]) for m in range(7)]

    def hard_weights(i, _):
        part = pl.ds(pl.multiple_of(i * rows, rows), rows)
        for m in range(7):
            columns = slice(m * rows, (m + 1) * rows)
            wt[part, columns] = (eh_t[part, columns] * tile_rows[m]).astype(bf16)
        return 0

    lax.fori_loop(0, tiles, hard_weights, 0)

    y_second += square_last(y_first, ys_send, ys_recv, at_y, "back_y")
    send_back(1, half, half, True, came=(2, half))
    send_back(1, 0, half, False, came=(2, 0))

    def passage_hard(i, _):
        columns = pl.ds(pl.multiple_of(i * 256, 256), 256)
        dp_acc[:, columns] = dot_nn(wt[:, 0 : 7 * rows], zq[0 : 7 * rows, columns])
        return 0

    lax.fori_loop(0, width // 256, passage_hard, 0)
    wait_sent("z", zq.at[pl.ds(0, 7 * rows)])
    wait_sent("x", xq.at[pl.ds(0, 3 * rows)])
    wait_sent("y", yp.at[pl.ds(0, 3 * rows)])
    wait_sent("back_x", xs_send)
    wait_sent("norm", norm_mine)
    wait_sent("hard", sh_mine)
    wait_sent("in", si_mine)
    wait_sent("aux_z", aux_z)
    wait_sent("aux_x", aux_x)
    wait_sent("aux_y", aux_y)
    wait_sent("sum_z", sum_z)
    wait_sent("sum_x", sum_x)
    wait_sent("fac_z", fac_z)
    wait_sent("fac_x", fac_x)
    wait_sent("own", own_y)

    def passage_along(i, _):
        part = pl.ds(pl.multiple_of(i * grain, grain), grain)
        along_p_mine[part, :] = fold_lanes(dp_acc[part, :] * p_ref[part, :].astype(f32))
        return 0

    lax.fori_loop(0, p_rows // grain, passage_along, 0)
    along_p_copy = send(along_p_mine, along_p_peer, other, "along")
    quarter = half // 2
    for start in (0, quarter):
        send_back(2, start, quarter, True, came=(3, 0), wait=start == 0)
        send_back(2, half + start, quarter, False, came=(3, half), wait=start == 0)

    wait_came("loss_z", loss_z.at[pl.ds(0, 7)])
    value = loss_z[0]
    for k in range(1, 8):
        value = value + loss_z[k]
    loss_x[x] = value
    for k in range(1, side):
        send(loss_x.at[x], loss_x.at[x], at_x(k), "loss_x", True)
    wait_came("loss_x", loss_x.at[pl.ds(0, 3)])
    value = loss_x[0]
    for k in range(1, side):
        value = value + loss_x[k]
    loss_y[y] = value
    for k in range(1, side):
        send(loss_y.at[y], loss_y.at[y], at_y(k), "loss_y", True)

    wait_came("own", own_y)
    for m in range(3):
        own_along = own_along + own_y[m][0:1, :]
    along_p_copy.wait_recv()
    for copy in y_second:
        copy.wait_recv()

    def positive_rows(i, _):
        part = pl.ds(pl.multiple_of(i * grain, grain), grain)
        after = pl.ds(pl.multiple_of(rows + i * grain, grain), grain)
        values = pin[part, :] + (ys_recv[part, :].astype(f32) + ys_recv[after, :].astype(f32))
        values = values - tile_lanes(own_col[part, :], repeat) * q_ref[part, :].astype(f32)
        high = values.astype(bf16)
        zq[pl.ds(pl.multiple_of(7 * rows + i * grain, grain), grain), :] = high
        zq[pl.ds(pl.multiple_of(8 * rows + i * grain, grain), grain), :] = (
            values - high.astype(f32)
        ).astype(bf16)
        return 0

    lax.fori_loop(0, rows // grain, positive_rows, 0)

    def passage_out(i, _):
        part = pl.ds(pl.multiple_of(i * rows, rows), rows)
        scale = pcol[part, :]
        shares = (along_p_mine[part, :] + along_p_peer[part, :]) * scale
        shares = shares + wt[part, 7 * rows : 8 * rows].astype(f32) * own_along
        along = jnp.sum(shares, axis=1, keepdims=True)
        along = jnp.broadcast_to(along, (rows, lanes)) * scale
        for c in range(width // wide):
            columns = slice(c * wide, (c + 1) * wide)
            values = dp_acc[part, columns] + dot_nn(
                wt[part, 7 * rows : 9 * rows], zq[7 * rows : 9 * rows, columns]
            )
            dp_ref[part, columns] = (
                (values - p_ref[part, columns].astype(f32) * tile_lanes(along, wide // lanes))
                * tile_lanes(scale, wide // lanes)
            ).astype(bf16)
        return 0

    lax.fori_loop(0, tiles // 2, passage_out, 0)
    send_back(1, 0, quarter, True, came=(2, 0))
    send_back(1, half, quarter, False, came=(2, half))
    lax.fori_loop(tiles // 2, tiles, passage_out, 0)
    send_back(1, quarter, quarter, True, came=(2, quarter))
    send_back(1, half + quarter, quarter, False, came=(2, half + quarter))
    wait_came("loss_y", loss_y.at[pl.ds(0, 3)])
    value = loss_y[0]
    for k in range(1, side):
        value = value + loss_y[k]
    queries = rows * owners * side * side
    mean = jnp.sum(value[0:1, :], axis=1, keepdims=True) * (1.0 / queries)
    loss_ref[...] = jnp.broadcast_to(mean, (8, lanes))
    wait_sent("loss_z", loss_z.at[pl.ds(0, 7)])
    wait_sent("loss_x", loss_x.at[pl.ds(0, 3)])
    wait_sent("loss_y", loss_y.at[pl.ds(0, 3)])
    wait_sent("along", along_p_mine)
    wait_sent("back_y", ys_send)

    def query_out(first):
        def body(i, _):
            part = pl.ds(pl.multiple_of(first + i * grain, grain), grain)
            before = pl.ds(pl.multiple_of(place(1, True, first) + i * grain, grain), grain)
            after = pl.ds(pl.multiple_of(place(1, False, first) + i * grain, grain), grain)
            back = zs_recv[before, :].astype(f32) + zs_recv[after, :].astype(f32)
            dq_ref[part, :] = (
                dq_acc[part, :] + back * tile_lanes(ratio_col[part, :], repeat)
            ).astype(bf16)
            return 0

        lax.fori_loop(0, quarter // grain, body, 0)

    back_right[1, half].wait_recv()
    back_left[1, 0].wait_recv()
    for start in (0, quarter):
        back_right[1, start].wait_recv()
        query_out(start)
        back_left[1, half + start].wait_recv()
        query_out(half + start)
    wait_sent("back_z", zs_send)


def flush(loss_ref, dq_ref, dp_ref, loss_out, dq_out, dp_out, one, sems):
    copies = [
        pltpu.make_async_copy(dp_ref, dp_out, sems.at[0]),
        pltpu.make_async_copy(dq_ref, dq_out, sems.at[1]),
    ]
    for copy in copies:
        copy.start()
    one[...] = loss_ref[0:1, 0:1]
    copies.append(pltpu.make_async_copy(one, loss_out, sems.at[2]))
    copies[2].start()
    for copy in copies:
        copy.wait()


def on_device(queries, passages, positive_slot, hard_offset, hard_slot):
    rows, width = queries.shape
    p_rows = passages.shape[0]
    vmem = pl.BlockSpec(memory_space=pltpu.VMEM)
    hbm = pl.BlockSpec(memory_space=pltpu.HBM)

    def f(*shape):
        return pltpu.VMEM(shape, f32)

    def b(*shape):
        return pltpu.VMEM(shape, bf16)

    loss, query_grad, passage_grad = pl.pallas_call(
        kernel,
        out_shape=(
            pltpu.VMEM((8, lanes), f32),
            pltpu.VMEM(queries.shape, bf16),
            pltpu.VMEM(passages.shape, bf16),
        ),
        in_specs=[hbm] * 5,
        out_specs=(vmem, vmem, vmem),
        scratch_shapes=[
            pltpu.VMEM((1, rows), jnp.int32),
            pltpu.VMEM((7, rows), jnp.int32),
            pltpu.VMEM((7, rows), jnp.int32),
            b(p_rows, width),
            b(9 * rows, width),
            f(7, p_rows, rows),
            f(7, p_rows, rows),
            f(p_rows, 7 * rows),
            b(7 * rows, p_rows),
            b(7 * rows, width),
            b(7 * rows, width),
            f(5 * rows, width),
            b(4 * rows, width),
            b(4 * rows, width),
            f(4 * rows, 4 * rows),
            f(4 * rows, 4 * rows),
            f(4 * rows, 4 * rows),
            f(4 * rows, 4 * rows),
            b(4 * rows, 4 * rows),
            f(4 * rows, width),
            b(3 * rows, width),
            b(3 * rows, width),
            b(3 * rows, width),
            b(3 * rows, width),
            f(rows, width),
            f(p_rows, width),
            b(p_rows, 9 * rows),
            b(rows, p_rows),
            f(p_rows + rows, lanes),
            f(p_rows + rows, lanes),
            f(p_rows, lanes),
            f(rows, lanes),
            f(8, lanes),
            f(7, 8, lanes),
            f(3, 8, lanes),
            f(1, lanes),
            f(3, 1, lanes),
            f(10, 2, lanes),
            f(7, 2, lanes),
            f(3, 2, lanes),
            f(1, lanes),
            f(2, lanes),
            f(7, 1, lanes),
            f(3, 2, lanes),
            f(4, 1, lanes),
            f(4, 1, lanes),
            f(3, 1, lanes),
            f(8, 1, lanes),
            f(4, 1, lanes),
            f(4, 1, lanes),
            f(p_rows, lanes),
            f(p_rows, lanes),
            f(rows, lanes),
            f(rows, lanes),
            f(rows, lanes),
            f(rows, lanes),
            pltpu.SemaphoreType.DMA((len(kinds),)),
            pltpu.SemaphoreType.DMA((len(shared) + alone,)),
            pltpu.SemaphoreType.DMA((5,)),
        ],
        compiler_params=pltpu.CompilerParams(
            collective_id=0, has_side_effects=True, vmem_limit_bytes=58 * 1024 * 1024
        ),
        cost_estimate=pl.CostEstimate(
            flops=15_000_000_000, bytes_accessed=6_000_000, transcendentals=800_000
        ),
    )(positive_slot.reshape(1, rows), hard_offset.T, hard_slot.T, queries, passages)
    loss, query_grad, passage_grad = pl.pallas_call(
        flush,
        out_shape=(
            jax.ShapeDtypeStruct((1, 1), f32),
            jax.ShapeDtypeStruct(queries.shape, bf16),
            jax.ShapeDtypeStruct(passages.shape, bf16),
        ),
        in_specs=[vmem, vmem, vmem],
        out_specs=(hbm, hbm, hbm),
        scratch_shapes=[f(1, 1), pltpu.SemaphoreType.DMA((3,))],
        compiler_params=pltpu.CompilerParams(vmem_limit_bytes=1024 * 1024),
    )(
        pltpu.with_memory_space_constraint(loss, pltpu.VMEM),
        pltpu.with_memory_space_constraint(query_grad, pltpu.VMEM),
        pltpu.with_memory_space_constraint(passage_grad, pltpu.VMEM),
    )
    return loss[0, 0], query_grad, passage_grad


def solution(mesh):
    in_specs = (
        P(("group", "index"), "tensor"),
        P(("group", "index"), "tensor"),
        P(("group", "index")),
        P(("group", "index"), None),
        P(("group", "index"), None),
    )
    out_specs = (P(), P(("group", "index"), "tensor"), P(("group", "index"), "tensor"))
    return jax.shard_map(
        on_device, mesh=mesh, in_specs=in_specs, out_specs=out_specs, check_vma=False
    )
```
